256 devices in a mesh: lon: 16 (over y, x_lo, core), lat: 16 (over x_hi, z).
Axes of the slice: x: 4 (x_hi: 2, x_lo: 2; x = x_hi * 2 + x_lo), y: 4, z: 8, core: 2. Of those that a mesh axis runs over, the one named last changes fastest.
Arguments:
- latent: float32 [128, 1024, 128], P('lat', 'lon'), may hold values from -6 to 6
- conv1_weight: float32 [3, 3, 128, 256], replicated, may hold values from -0.1875 to 0.1875
- conv1_bias: float32 [256], replicated, may hold values from -3 to 3
- conv2_weight: float32 [3, 3, 256, 256], replicated, may hold values from -0.125 to 0.125
- conv2_bias: float32 [256], replicated, may hold values from -3 to 3
- head_weight: float32 [256, 4416], replicated, may hold values from -0.375 to 0.375
- head_bias: float32 [4416], replicated, may hold values from -3 to 3
- land_sea: int32 [1024, 8192], P('lat', 'lon'), may hold values 0 or 1
- var_ok: int32 [2, 69], replicated, may hold values 0 or 1
- obs_error: float32 [69], replicated, may hold values from 1 to 3
- obs_band: int32 [16, 1536, 1], P('lon'), may hold values from 0 to 15; in each aligned block of 96 rows (0 to 95, 96 to 191, ..., all dimensions but the last counted through in order) at most 12 rows name the same one
- obs_cell: int32 [16, 1536], P('lon'), may hold values from 0 to 511
- obs_count: int32 [16, 1536], P('lon'), may hold values from 0 to 8
- obs_value: float32 [16, 1536, 4416], P('lon', 'lat'), may hold values from -6 to 6
Outputs:
- grad_latent: float32 [128, 1024, 128], P('lat', 'lon')
The draws below stay inside these ranges and needn't reach their ends.
Inputs may be any that keep to these rules, and one draw needn't show every extreme that they name: `obs_band`: among the 96 slots of one device (aligned blocks of a sector's list) no band is named more than 12 times, and in every draw some block names some band exactly 12 times. `obs_count`: 0 marks an empty slot. `land_sea`: 1 marks land. `var_ok`: 1 marks an observed variable.
All inputs are finite; a program needn't handle non-finite values. No bound on the sum of `land_sea` on one device may be relied on, other than what follows from the above.
Results may differ from the reference program's by a relative error of at most 0.0003.
Values sent between devices are 32-bit elements; how exact they have to be, the bound alone decides.
A program may use at most 128 MiB of HBM per device.

```python
import math
import jax
import jax.numpy as jnp
import numpy as np
from jax import lax

LC = 128
H = 256
VARS = 69
CLAT = 8
CLON = 64
SLOTS = 96
LAT = 128
LON = 1024
CELLS = 512
PATCH = 4416
CAP = 12
OBS_SECT = 1536
FLAT = 1024
FLON = 8192
N_LON = 16
N_LAT = 16


def touch_ends(result, key, least, high):
    place = [jax.random.randint(jax.random.fold_in(key, axis), (), 0, length) for axis, length in enumerate(result.shape)]
    main_axis = result.shape.index(max(result.shape))
    beside = place[:main_axis] + [(place[main_axis] + 1) % result.shape[main_axis]] + place[main_axis + 1:]
    return result.at[tuple(place)].set(least).at[tuple(beside)].set(high)


def shard_levels(own_key, shape, cuts, smallest, high):
    level = 1.0
    for axis_at, blocks in cuts:
        steps = jax.random.uniform(jax.random.fold_in(jax.random.fold_in(own_key, 6), axis_at), (blocks,), jnp.float32, smallest / len(cuts), high / len(cuts))
        level = level * jnp.repeat(jnp.exp(steps), shape[axis_at] // blocks).reshape((-1,) + (1,) * (len(shape) - 1 - axis_at))
    return level


def shared_out(rng, own, number, rows, amount, top, limit, skew):
    sequence = jax.random.permutation(rng, amount)
    heavy_load, usual = load_shares(amount, rows * top, limit, skew, True), load_shares(amount, rows * top, limit, skew, False)
    places = jnp.arange(amount)

    def named(lengths, rotation):
        used = int((lengths > 0).sum())
        fixed = max(1, used // 4)
        passed = fixed + (places - fixed + rotation * (used - fixed)) % max(1, amount - fixed)
        return jnp.zeros((amount,), jnp.int32).at[sequence[jnp.where(places < fixed, places, passed)]].set(jnp.asarray(lengths, jnp.int32))

    lengths = jnp.where(number % 4 == 0, named(heavy_load, number // 4), named(usual, number - number // 4 - 1))
    mixed = jax.random.permutation(jax.random.fold_in(own, 3), amount)
    giver, receiver = mixed[0:amount // 2 * 2:2], mixed[1:amount // 2 * 2:2]
    room = jnp.minimum(lengths[giver] - 1, limit - lengths[receiver]) // 2
    room = jnp.where((giver == sequence[0]) | (receiver == sequence[0]) | (lengths[receiver] == 0), 0, jnp.maximum(room, 0))
    passed = jax.random.randint(jax.random.fold_in(own, 4), (amount // 2,), 0, 1 << 20) % (room + 1)
    lengths = lengths.at[giver].add(-passed).at[receiver].add(passed)
    members = jnp.searchsorted(jnp.cumsum(lengths), jnp.arange(rows * top), side="right").astype(jnp.int32)
    listing = members.reshape(top, rows).T
    listing = listing[jax.random.permutation(jax.random.fold_in(own, 1), rows)]
    rotation = jax.random.randint(jax.random.fold_in(own, 2), (rows, 1), 0, top)
    return jnp.take_along_axis(listing, (jnp.arange(top)[None, :] + rotation) % top, axis=1)


def load_shares(number_of, total, limit, lean, full):
    portions = [(1 << 20) // math.isqrt(grade ** lean) + 1 for grade in range(1, number_of + 1)]
    largest = limit if full else min(limit, max(-(-total // number_of), total * portions[0] // sum(portions)))
    least = 1 if total - largest >= number_of - 1 else 0
    given, rest = [largest] + [least] * (number_of - 1), total - largest - least * (number_of - 1)
    while rest > 0:
        candidates = [i for i in range(1, number_of) if given[i] < largest] or [i for i in range(1, number_of) if given[i] < limit]
        mass, budget = sum([portions[i] for i in candidates]), rest
        for i in candidates:
            addition = min(limit - given[i], max(1, budget * portions[i] // mass), rest)
            given[i] = given[i] + addition
            rest = rest - addition
    return np.array(given)


def centred(key, shape, scale, most, split=(), held_as=jnp.bfloat16):
    level = shard_levels(key, shape, split, -0.22, 0.18) if split else 1.0
    entries = jax.random.normal(key, shape, jnp.float32) * scale * level
    return jnp.minimum(jnp.maximum(entries, -most), most).astype(held_as)


def setup_inputs(seed: int = 0) -> dict:
    keys = jax.random.split(jax.random.key(seed), 15)
    latent = centred(keys[0], (LAT, LON, LC), 1.0, 6.0, ((0, 16), (1, 16)), jnp.float32)
    conv1_weight = centred(keys[1], (3, 3, LC, H), (9 * LC) ** -0.5, 0.1875, (), jnp.float32)
    conv1_bias = centred(keys[2], (H,), 0.5, 3.0, (), jnp.float32)
    conv2_weight = centred(keys[3], (3, 3, H, H), (9 * H) ** -0.5, 0.125, (), jnp.float32)
    conv2_bias = centred(keys[4], (H,), 0.5, 3.0, (), jnp.float32)
    head_weight = centred(keys[5], (H, PATCH), H ** -0.5, 0.375, (), jnp.float32)
    head_bias = centred(keys[6], (PATCH,), 0.5, 3.0, (), jnp.float32)
    land_sea = touch_ends((jax.random.randint(keys[7], (FLAT, FLON), 0, 3) < 1).astype(jnp.int32), jax.random.fold_in(keys[7], 1), 0, 1)
    var_ok = touch_ends((jax.random.randint(keys[8], (2, VARS), 0, 4) < 3).astype(jnp.int32), jax.random.fold_in(keys[8], 1), 0, 1)
    obs_error = jnp.clip(jnp.exp(jax.random.uniform(keys[9], (VARS,), jnp.float32, math.log(1.0), math.log(3.0))), 1.0, 3.0)
    obs_band_keys = jax.random.split(jax.random.fold_in(keys[10], 1), N_LON * OBS_SECT // SLOTS)
    obs_band_turns = jax.random.permutation(jax.random.fold_in(keys[10], 3), N_LON * OBS_SECT // SLOTS)
    obs_band = jax.vmap(lambda own, number: shared_out(jax.random.fold_in(keys[10], 2), own, number, SLOTS, N_LAT, 1, CAP, 2))(obs_band_keys, obs_band_turns).reshape((N_LON, OBS_SECT, 1))
    obs_cell = touch_ends(jax.random.randint(keys[11], (N_LON, OBS_SECT), 0, CELLS), jax.random.fold_in(keys[11], 1), 0, CELLS - 1).astype(jnp.int32)
    obs_count = touch_ends(jax.random.randint(keys[12], (N_LON, OBS_SECT), 0, 9), jax.random.fold_in(keys[12], 1), 0, 8).astype(jnp.int32)
    obs_value = centred(keys[13], (N_LON, OBS_SECT, PATCH), 1.0, 6.0, ((0, 16), (1, 16)), jnp.float32)
    return dict(latent=latent, conv1_weight=conv1_weight, conv1_bias=conv1_bias, conv2_weight=conv2_weight, conv2_bias=conv2_bias, head_weight=head_weight, head_bias=head_bias, land_sea=land_sea, var_ok=var_ok, obs_error=obs_error, obs_band=obs_band, obs_cell=obs_cell, obs_count=obs_count, obs_value=obs_value)


def sphere_pad(field):
    half_turn = field.shape[1] // 2
    north_row = jnp.roll(field[0:1], -half_turn, axis=1)
    south_row = jnp.roll(field[-1:], -half_turn, axis=1)
    banded = jnp.concatenate([north_row, field, south_row], axis=0)
    return jnp.concatenate([banded[:, -1:], banded, banded[:, :1]], axis=1)

def convolve(padded, weight):
    row_count = padded.shape[0] - 2
    col_count = padded.shape[1] - 2
    summed = jnp.zeros((row_count * col_count, weight.shape[3]), jnp.float32)
    for row_off in range(3):
        for col_off in range(3):
            piece = padded[row_off:row_off + row_count, col_off:col_off + col_count].reshape(row_count * col_count, -1)
            summed = summed + jnp.dot(piece, weight[row_off, col_off], precision=lax.Precision.HIGHEST, preferred_element_type=jnp.float32)
    return summed.reshape(row_count, col_count, -1)

def reference(latent, conv1_weight, conv1_bias, conv2_weight, conv2_bias, head_weight, head_bias, land_sea, var_ok, obs_error, obs_band, obs_cell, obs_count, obs_value):

    def trunk_of(field):
        pre_one = convolve(sphere_pad(field), conv1_weight) + conv1_bias
        act_one = jax.nn.gelu(pre_one, approximate=True)
        pre_two = convolve(sphere_pad(act_one), conv2_weight) + conv2_bias
        return jax.nn.gelu(pre_two, approximate=True)
    act_two, pullback = jax.vjp(trunk_of, latent)
    band_ids = obs_band[:, :, 0]
    sector = jnp.arange(N_LON, dtype=jnp.int32)[:, None]
    tile_rows = (band_ids * CLAT + obs_cell // CLON).reshape(-1)
    tile_cols = (sector * CLON + obs_cell % CLON).reshape(-1)
    pixel_land = land_sea.reshape(LAT, 8, LON, 8).transpose(0, 2, 1, 3).reshape(LAT, LON, 64)
    land_tiles = pixel_land[tile_rows, tile_cols]
    columns = act_two[tile_rows, tile_cols]
    inverse = jnp.tile(1.0 / (obs_error * obs_error), 64)
    weights = obs_count.reshape(-1).astype(jnp.float32) / 8.0
    values = obs_value.reshape(-1, PATCH)
    blocks = N_LON * N_LAT

    def block_terms(pieces):
        cols_block, land_block, values_block, weight_block = pieces
        decoded = jnp.dot(cols_block, head_weight, precision=lax.Precision.HIGHEST, preferred_element_type=jnp.float32) + head_bias
        allowed = jnp.where(land_block[:, :, None] == 1, var_ok[1][None, None, :], var_ok[0][None, None, :])
        allowed = allowed.reshape(cols_block.shape[0], -1).astype(jnp.float32)
        scaled = weight_block[:, None] * inverse[None, :] * allowed * (decoded - values_block)
        return jnp.dot(scaled, head_weight.T, precision=lax.Precision.HIGHEST, preferred_element_type=jnp.float32)
    terms = lax.map(block_terms, (columns.reshape(blocks, SLOTS, -1), land_tiles.reshape(blocks, SLOTS, 64), values.reshape(blocks, SLOTS, PATCH), weights.reshape(blocks, SLOTS)))
    hidden_grad = jnp.zeros_like(act_two).at[tile_rows, tile_cols].add(terms.reshape(-1, act_two.shape[2]))
    return pullback(hidden_grad)[0]
```

```python
import functools

import jax
import jax.numpy as jnp
from jax import lax
from jax.experimental import pallas as pl
from jax.experimental.pallas import tpu as pltpu
from jax.sharding import PartitionSpec as P

F32 = jnp.float32
BF16 = jnp.bfloat16
CAP = 12
MSG = 2 * CAP
LCAP = 16
SIDE = 8
WIDE = 80
BUF = 88
CHUNK = 512
MESH = pl.DeviceIdType.MESH


def halves(x):
    high = x.astype(BF16)
    return high, (x - high.astype(F32)).astype(BF16)


def nn(a, b):
    return lax.dot_general(a, b, (((1,), (0,)), ((), ())), preferred_element_type=F32)


def nt(a, b):
    return lax.dot_general(a, b, (((1,), (1,)), ((), ())), preferred_element_type=F32)


def gelu_parts(x):
    c = 0.7978845608028654
    t = jnp.tanh(c * (x + 0.044715 * x * x * x))
    return 0.5 * x * (1.0 + t), t


def gelu_slope(x):
    c = 0.7978845608028654
    t = jnp.tanh(c * (x + 0.044715 * x * x * x))
    return 0.5 * (1.0 + t) + 0.5 * x * (1.0 - t * t) * (c * (1.0 + 3.0 * 0.044715 * x * x))


def kernel(
    n_lon, n_lat, slots, patch, variables,
    latent, w1, b1, w2, b2, head, hbias, land, ok, err, band, cell, count, value,
    out,
    lat_ext, sa_hi, sa_lo, w1_v, w1_hi, w1_lo, w2_v, w2_hi, w2_lo, b1_v, b2_v,
    pre1, act1, sb_hi, sb_lo, pre2, head_v, head_hi, head_lo, hb_v, land_v, ok_v, err_v,
    band_v, cell_v, count_v, value_v, scale_v,
    oh, oht, pm, pmt, land_send, land_recv, col_send, col_recv, term_send, term_recv,
    g_ext, sg_hi, sg_lo, p_ext, sp_hi, sp_lo, out_v,
    load_sem, h_send, h_recv, g_send, g_recv, l_send, l_recv, c_send, c_recv, t_send, t_recv,
):
    lon, lat = lax.axis_index("lon"), lax.axis_index("lat")
    north = 1 - lax.div(lat + n_lat - 1, n_lat)
    south = lax.div(lat + 1, n_lat)
    northf, southf = north.astype(F32), south.astype(F32)

    loads = [
        (latent, lat_ext.at[2:10, SIDE:SIDE + 64, :]),
        (band, band_v.at[:, 0:n_lat * slots]),
        (cell, cell_v.at[:, 0:n_lat * slots]),
        (count, count_v.at[:, 0:n_lat * slots]),
        (land, land_v),
        (w1, w1_v),
        (b1, b1_v),
        (w2, w2_v),
        (b2, b2_v),
        (ok, ok_v),
        (err, err_v),
        (hbias, hb_v),
        (head, head_v),
        (value, value_v),
    ]
    copies = [pltpu.make_async_copy(s, d, load_sem.at[i]) for i, (s, d) in enumerate(loads)]
    for copy in copies:
        copy.start()
    (ld_lat, ld_band, ld_cell, ld_count, ld_land, ld_w1, ld_b1, ld_w2, ld_b2, ld_ok, ld_err, ld_hb, ld_head,
     ld_value) = copies

    half = n_lon // 2
    up_lat, down_lat = lat - 1 + north, lat + 1 - south
    around = []
    for dr in (-1, 0, 1):
        for dc in (-1, 0, 1):
            if dr == 0 and dc == 0:
                continue
            turn = half * north if dr < 0 else half * south if dr > 0 else 0
            to_lon = lax.rem(lon + dc + turn + n_lon, n_lon)
            to_lat = up_lat if dr < 0 else down_lat if dr > 0 else lat
            around.append((dr, dc, (to_lon, to_lat)))

    barrier = pltpu.get_barrier_semaphore()
    for _, _, device in around:
        pl.semaphore_signal(barrier, inc=1, device_id=device, device_id_type=MESH)
    for step in range(1, n_lat):
        peer = lax.rem(lat + step, n_lat)
        pl.semaphore_signal(barrier, inc=1, device_id=(lon, peer), device_id_type=MESH)

    def rim(buf, send_sem, recv_sem):
        sent = []
        for number, (dr, dc, device) in enumerate(around):
            src_r = (2, 2) if dr < 0 else (8, 2) if dr > 0 else (2, 8)
            src_c = (SIDE, SIDE) if dc < 0 else (SIDE + 56, SIDE) if dc > 0 else (SIDE, 64)
            dst_c = 72 if dc < 0 else 0 if dc > 0 else SIDE
            if dr < 0:
                dst_r, side = 10 - 10 * north, 2 - 2 * north
            elif dr > 0:
                dst_r, side = 10 * south, 2 * south
            else:
                dst_r, side = 2, 1
            slot = side * 3 + (1 - dc)
            src = buf.at[pl.ds(src_r[0], src_r[1]), pl.ds(src_c[0], src_c[1]), :]
            dst = buf.at[pl.ds(dst_r, src_r[1]), pl.ds(dst_c, src_c[1]), :]
            copy = pltpu.make_async_remote_copy(
                src_ref=src, dst_ref=dst, send_sem=send_sem.at[number], recv_sem=recv_sem.at[slot],
                device_id=device, device_id_type=MESH)
            copy.start()
            sent.append(copy)
        return sent

    def rim_arrived(buf, recv_sem, send_sem):
        for number, (dr, dc, device) in enumerate(around):
            rows = (0, 2) if dr < 0 else (10, 2) if dr > 0 else (2, 8)
            cols = (0, SIDE) if dc < 0 else (72, SIDE) if dc > 0 else (SIDE, 64)
            ref = buf.at[pl.ds(rows[0], rows[1]), pl.ds(cols[0], cols[1]), :]
            slot = (dr + 1) * 3 + dc + 1
            pltpu.make_async_remote_copy(
                src_ref=ref, dst_ref=ref, send_sem=send_sem.at[number], recv_sem=recv_sem.at[slot],
                device_id=device, device_id_type=MESH).wait_recv()

    def exchange(src, dst, send_sem, recv_sem):
        sent = []
        for step in range(1, n_lat):
            peer = lax.rem(lat + step, n_lat)
            copy = pltpu.make_async_remote_copy(
                src_ref=src.at[peer], dst_ref=dst.at[lat], send_sem=send_sem.at[step], recv_sem=recv_sem.at[lat],
                device_id=(lon, peer), device_id_type=MESH)
            copy.start()
            sent.append(copy)
        dst[pl.ds(lat, 1)] = src[pl.ds(lat, 1)]
        return sent

    def arrived(dst, send_sem, recv_sem):
        for step in range(1, n_lat):
            peer = lax.rem(lat + step, n_lat)
            pltpu.make_async_remote_copy(
                src_ref=dst.at[peer], dst_ref=dst.at[peer], send_sem=send_sem.at[step], recv_sem=recv_sem.at[peer],
                device_id=(lon, peer), device_id_type=MESH).wait_recv()

    lat_ext[:, 80:88, :] = jnp.zeros((12, 8, lat_ext.shape[2]), F32)
    g_ext[:, 80:88, :] = jnp.zeros((12, 8, g_ext.shape[2]), F32)

    pl.semaphore_wait(barrier, len(around) + n_lat - 1)
    ld_lat.wait()
    rim1 = rim(lat_ext, h_send, h_recv)

    ld_band.wait()
    ld_cell.wait()
    ld_count.wait()
    lane = lax.broadcasted_iota(jnp.int32, (n_lat, 128), 1)
    live = lane < slots

    def blocks(ref):
        row = ref[...]
        return jnp.concatenate([row[:, slots * a:slots * a + 128] for a in range(n_lat)], axis=0)

    bands, cells, counts = blocks(band_v), blocks(cell_v), blocks(count_v)
    below = (lax.broadcasted_iota(jnp.int32, (128, 128), 0) < lax.broadcasted_iota(jnp.int32, (128, 128), 1))
    below = below.astype(F32).astype(BF16)
    mine = jnp.where(live & (bands == lat), 1.0, 0.0)
    rank = nn(mine.astype(BF16), below)
    pick = jnp.where(mine > 0.0, rank, -1.0)
    cellsf = cells.astype(F32) + 1.0
    msg_k = lax.rem(lax.broadcasted_iota(jnp.int32, (MSG, 128), 0), CAP).astype(F32)
    land_k = lax.broadcasted_iota(jnp.int32, (LCAP, 128), 0).astype(F32)
    named, named_land = [], []
    for a in range(n_lat):
        p, c = pick[a:a + 1], cellsf[a:a + 1]
        named.append(jnp.sum(jnp.where(p == msg_k, c, 0.0), axis=1, keepdims=True))
        named_land.append(jnp.sum(jnp.where(p == land_k, c, 0.0), axis=1, keepdims=True))
    wanted = jnp.concatenate(named, axis=0).astype(jnp.int32) - 1
    wanted_land = jnp.concatenate(named_land, axis=0).astype(jnp.int32) - 1
    rows = n_lat * MSG
    oh[...] = jnp.where(wanted == lax.broadcasted_iota(jnp.int32, (rows, 512), 1), 1.0, 0.0).astype(BF16)
    wanted_row = jnp.transpose(jnp.broadcast_to(wanted.astype(F32), (rows, 128)))[0:1, :].astype(jnp.int32)
    oht[...] = jnp.where(wanted_row == lax.broadcasted_iota(jnp.int32, (512, rows), 0), 1.0, 0.0).astype(BF16)

    own = lax.broadcasted_iota(jnp.int32, (n_lat, 128), 0) == lat
    own_band = jnp.sum(jnp.where(own, bands, 0), axis=0, keepdims=True)
    own_count = jnp.sum(jnp.where(own, counts, 0), axis=0, keepdims=True)
    theirs = jnp.where(live & (own_band == lax.broadcasted_iota(jnp.int32, (n_lat, 128), 0)), 1.0, 0.0)
    place = jnp.where(theirs > 0.0, nn(theirs.astype(BF16), below), -1.0)
    pmt_f = jnp.concatenate([jnp.where(place[b:b + 1] == msg_k, 1.0, 0.0) for b in range(n_lat)], axis=0)
    pmt[...] = pmt_f.astype(BF16)
    pm[...] = jnp.transpose(pmt_f).astype(BF16)
    pml = jnp.concatenate([jnp.where(place[b:b + 1] == land_k, 1.0, 0.0) for b in range(n_lat)], axis=0)
    pml = jnp.transpose(pml).astype(BF16)
    weight = jnp.transpose(jnp.broadcast_to(own_count.astype(F32) * 0.125, (128, 128)))[:slots, 0:1]

    ld_land.wait()
    lrows = n_lat * LCAP
    land_b = land_v[...].astype(F32).astype(BF16)
    tile_row, tile_col = wanted_land >> 6, wanted_land & 63
    valid = wanted_land >= 0
    tile_row = jnp.where(valid, tile_row, -1000)
    in_tile = (lax.broadcasted_iota(jnp.int32, (lrows, 512), 1) >> 3) == tile_col
    flags = jnp.zeros((lrows, 128), F32)
    for p in range(8):
        pick_row = (lax.broadcasted_iota(jnp.int32, (lrows, 64), 1) == tile_row * 8 + p)
        found = nn(jnp.where(pick_row, 1.0, 0.0).astype(BF16), land_b)
        found = jnp.where(in_tile, found, 0.0).astype(BF16)
        col = lax.broadcasted_iota(jnp.int32, (512, 128), 1)
        fold = (lax.broadcasted_iota(jnp.int32, (512, 128), 0) & 7) + 8 * p == col
        flags = flags + nn(found, jnp.where(fold, 1.0, 0.0).astype(BF16))
    on_land = jnp.concatenate([flags[:, :64], jnp.where(valid, 1.0 - flags[:, :64], 0.0)], axis=1)
    land_send[...] = on_land.reshape(n_lat, LCAP, 128)
    land_sent = exchange(land_send, land_recv, l_send, l_recv)

    ld_w1.wait()
    high, low = halves(w1_v[...])
    w1_hi[...] = high
    w1_lo[...] = low
    ld_w2.wait()
    high, low = halves(w2_v[...])
    w2_hi[...] = high
    w2_lo[...] = low
    ld_b1.wait()
    ld_b2.wait()

    rim_arrived(lat_ext, h_recv, h_send)
    for j in range(3):
        span = slice(SIDE - 2 + j, SIDE - 2 + j + WIDE)
        for at, source, length in ((0, north, 1), (1, 1 - north, 1), (2, 2, 8), (10, 10 + south, 1), (11, 11 - south, 1)):
            high, low = halves(lat_ext[pl.ds(source, length), span, :])
            sa_hi[j, at:at + length] = high
            sa_lo[j, at:at + length] = low

    def taps1(ref):
        parts = []
        for i in range(3):
            for j in range(3):
                if i == 1:
                    rows_ = ref[j, 1:11]
                else:
                    first = 2 * north if i == 0 else 2 - 2 * north
                    last = 9 + 2 * south if i == 0 else 11 - 2 * south
                    rows_ = jnp.concatenate(
                        [ref[j, pl.ds(first, 1)], ref[j, 1 + i:9 + i], ref[j, pl.ds(last, 1)]], axis=0)
                parts.append(rows_.reshape(10 * WIDE, rows_.shape[2]))
        return jnp.concatenate(parts, axis=1)

    k1 = w1_v.shape[1]
    hid = w1_v.shape[2]
    wh = w1_hi[...].reshape(9 * k1, hid)
    wl = w1_lo[...].reshape(9 * k1, hid)
    lhs = taps1(sa_hi)
    summed = nn(lhs, wh) + nn(lhs, wl) + nn(taps1(sa_lo), wh) + b1_v[...]
    pre1[...] = summed.reshape(10, WIDE, hid)
    act1[...] = gelu_parts(summed)[0].reshape(10, WIDE, hid)

    for j in range(3):
        high, low = halves(act1[:, j:j + 64, :])
        sb_hi[j] = high
        sb_lo[j] = low

    def taps2(ref):
        return jnp.concatenate([ref[j, i:i + 8].reshape(512, hid) for i in range(3) for j in range(3)], axis=1)

    wh = w2_hi[...].reshape(9 * hid, hid)
    wl = w2_lo[...].reshape(9 * hid, hid)
    lhs = taps2(sb_hi)
    summed = nn(lhs, wh) + nn(lhs, wl) + nn(taps2(sb_lo), wh) + b2_v[...]
    pre2[...] = summed
    act2, _ = gelu_parts(summed)

    upper = lax.rem(lax.broadcasted_iota(jnp.int32, (rows, 128), 0), MSG) < CAP

    def fold_halves(x):
        return jnp.where(upper, x[:, :128], x[:, 128:])

    def unfold(x):
        return jnp.concatenate([jnp.where(upper, x, 0.0), jnp.where(upper, 0.0, x)], axis=1)

    high, low = halves(act2)
    sent_cols = nn(oh[...], jnp.concatenate([high, low], axis=1))
    col_send[...] = fold_halves(sent_cols[:, :hid] + sent_cols[:, hid:]).reshape(n_lat, MSG, 128)
    cols_sent = exchange(col_send, col_recv, c_send, c_recv)

    ld_head.wait()
    high, low = halves(head_v[...])
    head_hi[...] = high
    head_lo[...] = low
    ld_ok.wait()
    ld_err.wait()
    ld_hb.wait()
    ld_value.wait()
    arrived(land_recv, l_send, l_recv)
    flags_own = nn(pml, land_recv[...].reshape(lrows, 128).astype(BF16))[:slots].astype(BF16)
    inv = 1.0 / (err_v[...] * err_v[...])
    inv_hi = inv.astype(BF16).astype(F32)
    inv_mid = (inv - inv_hi).astype(BF16).astype(F32)
    inv_lo = inv - inv_hi - inv_mid
    okf = ok_v[...].astype(F32)
    kind = lax.broadcasted_iota(jnp.int32, (16, variables), 0)
    table = jnp.where(kind == 0, inv_hi, jnp.where(kind == 1, inv_mid, jnp.where(kind == 2, inv_lo, 0.0)))
    table = table + jnp.where(kind == 3, okf[1:2], 0.0) + jnp.where(kind == 4, okf[0:1], 0.0)
    table = table.astype(BF16)
    spans = [(at, min(CHUNK, patch - at)) for at in range(0, patch, CHUNK)]
    for at, size in spans:
        place_ = lax.broadcasted_iota(jnp.int32, (1, size), 1) + at
        pixel = ((place_.astype(F32) + 0.5) * (1.0 / variables)).astype(jnp.int32)
        variable = place_ - pixel * variables
        spread = nn(table, jnp.where(lax.broadcasted_iota(jnp.int32, (variables, size), 0) == variable, 1.0, 0.0).astype(BF16))
        inv_row = spread[0:1] + spread[1:2] + spread[2:3]
        which = lax.broadcasted_iota(jnp.int32, (128, size), 0)
        ok_rows = jnp.where(which == pixel, spread[3:4], jnp.where(which == pixel + 64, spread[4:5], 0.0))
        allowed = nn(flags_own, ok_rows.astype(BF16))
        scale_v[:, at:at + size] = weight * inv_row * allowed
        value_v[:, at:at + size] = value_v[:, at:at + size] - hb_v[:, at:at + size]

    arrived(col_recv, c_send, c_recv)
    high, low = halves(unfold(col_recv[...].reshape(rows, 128)))
    cols = nn(pm[...], jnp.concatenate([high, low], axis=1))[:slots].astype(BF16)
    cols_hi, cols_lo = cols[:, :hid], cols[:, hid:]
    cols_both = jnp.concatenate([cols_hi, cols_lo], axis=0)
    terms = jnp.zeros((slots, hid), F32)
    for at, size in spans:
        hh, hl = head_hi[at:at + size, :], head_lo[at:at + size, :]
        both = nt(cols_both, hh)
        decoded = both[:slots] + both[slots:] + nt(cols_hi, hl)
        scaled = scale_v[:, at:at + size] * (decoded - value_v[:, at:at + size])
        high, low = halves(scaled)
        both = nn(jnp.concatenate([high, low], axis=0), hh)
        terms = terms + both[:slots] + both[slots:] + nn(high, hl)
    high, low = halves(terms)
    both = jnp.concatenate([high, low], axis=1)
    if slots < 128:
        both = jnp.concatenate([both, jnp.zeros((128 - slots, 2 * hid), BF16)], axis=0)
    sent_terms = nn(pmt[...], both)
    term_send[...] = fold_halves(sent_terms[:, :hid] + sent_terms[:, hid:]).reshape(n_lat, MSG, 128)
    terms_sent = exchange(term_send, term_recv, t_send, t_recv)

    pre2[...] = gelu_slope(pre2[...])
    pre1[...] = gelu_slope(pre1[...])

    arrived(term_recv, t_send, t_recv)
    high, low = halves(unfold(term_recv[...].reshape(rows, 128)))
    hidden = nn(oht[...], jnp.concatenate([high, low], axis=1))
    grad2 = (hidden[:, :hid] + hidden[:, hid:]) * pre2[...]
    g_ext[2:10, SIDE:SIDE + 64, :] = grad2.reshape(8, 64, hid)
    rim2 = rim(g_ext, g_send, g_recv)
    rim_arrived(g_ext, g_recv, g_send)

    for j in range(3):
        span = slice(SIDE - j, SIDE - j + WIDE)

        def row(at, length=1):
            return g_ext[pl.ds(at, length), span, :]

        r0, r1, r10, r11 = row(north), row(1 - north), row(10 + south), row(11 - south)
        pieces = (
            (0, r0), (1, r1), (2, row(2, 8)), (10, r10), (11, r11),
            (12, row(2) + northf * r0), (13, row(3) + northf * r1),
            (14, r10 * (1.0 - southf)), (15, r11 * (1.0 - southf)),
            (16, r0 * (1.0 - northf)), (17, r1 * (1.0 - northf)),
            (18, row(8) + southf * r10), (19, row(9) + southf * r11),
        )
        for at, piece in pieces:
            high, low = halves(piece)
            sg_hi[j, at:at + piece.shape[0]] = high
            sg_lo[j, at:at + piece.shape[0]] = low

    def taps3(ref):
        parts = []
        for i in range(3):
            for j in range(3):
                if i == 0:
                    rows_ = jnp.concatenate([ref[j, 12:14], ref[j, 4:10], ref[j, 14:16]], axis=0)
                elif i == 1:
                    rows_ = ref[j, 1:11]
                else:
                    rows_ = jnp.concatenate([ref[j, 16:18], ref[j, 2:8], ref[j, 18:20]], axis=0)
                parts.append(rows_.reshape(10 * WIDE, hid))
        return jnp.concatenate(parts, axis=1)

    wh = jnp.concatenate([w2_hi[t] for t in range(9)], axis=1)
    wl = jnp.concatenate([w2_lo[t] for t in range(9)], axis=1)
    lhs = taps3(sg_hi)
    grad1 = nt(lhs, wh) + nt(lhs, wl) + nt(taps3(sg_lo), wh)
    p_ext[...] = grad1.reshape(10, WIDE, hid) * pre1[...]

    for j in range(3):
        span = slice(2 - j, 2 - j + 64)
        q0, q9 = p_ext[0:1, span, :], p_ext[9:10, span, :]
        pieces = (
            (0, p_ext[:, span, :]),
            (10, p_ext[2:3, span, :] + northf * q0), (11, q9 * (1.0 - southf)),
            (12, q0 * (1.0 - northf)), (13, p_ext[7:8, span, :] + southf * q9),
        )
        for at, piece in pieces:
            high, low = halves(piece)
            sp_hi[j, at:at + piece.shape[0]] = high
            sp_lo[j, at:at + piece.shape[0]] = low

    def taps4(ref):
        parts = []
        for i in range(3):
            for j in range(3):
                if i == 0:
                    rows_ = jnp.concatenate([ref[j, 10:11], ref[j, 3:9], ref[j, 11:12]], axis=0)
                elif i == 1:
                    rows_ = ref[j, 1:9]
                else:
                    rows_ = jnp.concatenate([ref[j, 12:13], ref[j, 1:7], ref[j, 13:14]], axis=0)
                parts.append(rows_.reshape(512, hid))
        return jnp.concatenate(parts, axis=1)

    wh = jnp.concatenate([w1_hi[t] for t in range(9)], axis=1)
    wl = jnp.concatenate([w1_lo[t] for t in range(9)], axis=1)
    both = nt(taps4(sp_hi), jnp.concatenate([wh, wl], axis=0))
    result = both[:, :k1] + both[:, k1:] + nt(taps4(sp_lo), wh)
    out_v[...] = result.reshape(8, 64, k1)
    done = pltpu.make_async_copy(out_v, out, load_sem.at[0])
    done.start()
    for copy in rim1 + land_sent + cols_sent + terms_sent + rim2:
        copy.wait_send()
    done.wait()


def shards(n_lon, n_lat, latent, conv1_weight, conv1_bias, conv2_weight, conv2_bias, head_weight, head_bias, land_sea,
           var_ok, obs_error, obs_band, obs_cell, obs_count, obs_value):
    lc, hid = conv1_weight.shape[2], conv1_weight.shape[3]
    slots, patch = obs_value.shape[1], obs_value.shape[2]
    variables = var_ok.shape[1]
    listed = n_lat * slots
    padded = -(-(listed + 128) // 128) * 128
    vmem = pltpu.VMEM
    rows = n_lat * MSG
    scratch = [
        vmem((12, BUF, lc), F32),
        vmem((3, 12, WIDE, lc), BF16), vmem((3, 12, WIDE, lc), BF16),
        vmem((9, lc, hid), F32), vmem((9, lc, hid), BF16), vmem((9, lc, hid), BF16),
        vmem((9, hid, hid), F32), vmem((9, hid, hid), BF16), vmem((9, hid, hid), BF16),
        vmem((1, hid), F32), vmem((1, hid), F32),
        vmem((10, WIDE, hid), F32), vmem((10, WIDE, hid), F32),
        vmem((3, 10, 64, hid), BF16), vmem((3, 10, 64, hid), BF16),
        vmem((512, hid), F32),
        vmem((patch, hid), F32), vmem((patch, hid), BF16), vmem((patch, hid), BF16),
        vmem((1, patch), F32), vmem(land_sea.shape, jnp.int32), vmem(var_ok.shape, jnp.int32),
        vmem((1, variables), F32),
        vmem((1, padded), jnp.int32), vmem((1, padded), jnp.int32), vmem((1, padded), jnp.int32),
        vmem((slots, patch), F32), vmem((slots, patch), F32),
        vmem((rows, 512), BF16), vmem((512, rows), BF16),
        vmem((128, rows), BF16), vmem((rows, 128), BF16),
        vmem((n_lat, LCAP, 128), F32), vmem((n_lat, LCAP, 128), F32),
        vmem((n_lat, MSG, 128), F32), vmem((n_lat, MSG, 128), F32),
        vmem((n_lat, MSG, 128), F32), vmem((n_lat, MSG, 128), F32),
        vmem((12, BUF, hid), F32),
        vmem((3, 20, WIDE, hid), BF16), vmem((3, 20, WIDE, hid), BF16),
        vmem((10, WIDE, hid), F32),
        vmem((3, 14, 64, hid), BF16), vmem((3, 14, 64, hid), BF16),
        vmem((8, 64, lc), F32),
        pltpu.SemaphoreType.DMA((14,)),
        pltpu.SemaphoreType.DMA((8,)), pltpu.SemaphoreType.DMA((9,)),
        pltpu.SemaphoreType.DMA((8,)), pltpu.SemaphoreType.DMA((9,)),
    ] + [pltpu.SemaphoreType.DMA((n_lat,))] * 6
    return pl.pallas_call(
        functools.partial(kernel, n_lon, n_lat, slots, patch, variables),
        out_shape=jax.ShapeDtypeStruct(latent.shape, F32),
        in_specs=[pl.BlockSpec(memory_space=pl.ANY)] * 14,
        out_specs=pl.BlockSpec(memory_space=pl.ANY),
        scratch_shapes=scratch,
        compiler_params=pltpu.CompilerParams(
            collective_id=0, has_side_effects=True, vmem_limit_bytes=60 * 1024 * 1024),
    )(latent, conv1_weight.reshape(9, lc, hid), conv1_bias.reshape(1, hid), conv2_weight.reshape(9, hid, hid),
      conv2_bias.reshape(1, hid), head_weight.T, head_bias.reshape(1, patch), land_sea, var_ok,
      obs_error.reshape(1, variables), obs_band.reshape(1, listed), obs_cell, obs_count, obs_value[0])


def solution(mesh):
    in_specs = (
        P("lat", "lon", None),
        P(),
        P(),
        P(),
        P(),
        P(),
        P(),
        P("lat", "lon"),
        P(),
        P(),
        P("lon", None, None),
        P("lon", None),
        P("lon", None),
        P("lon", "lat", None),
    )
    out_specs = P("lat", "lon", None)
    body = functools.partial(shards, mesh.shape["lon"], mesh.shape["lat"])
    return jax.shard_map(body, mesh=mesh, in_specs=in_specs, out_specs=out_specs, check_vma=False)
```

```python
import functools

import jax
import jax.numpy as jnp
from jax import lax
from jax.experimental import pallas as pl
from jax.experimental.pallas import tpu as pltpu
from jax.sharding import PartitionSpec as P

F32 = jnp.float32
BF16 = jnp.bfloat16
CAP = 12
MSG = 2 * CAP
LCAP = 16
SIDE = 8
WIDE = 80
BUF = 88
CHUNK = 512
MESH = pl.DeviceIdType.MESH


def halves(x):
    high = x.astype(BF16)
    return high, (x - high.astype(F32)).astype(BF16)


def nn(a, b):
    return lax.dot_general(a, b, (((1,), (0,)), ((), ())), preferred_element_type=F32)


def nt(a, b):
    return lax.dot_general(a, b, (((1,), (1,)), ((), ())), preferred_element_type=F32)


def gelu_parts(x):
    c = 0.7978845608028654
    t = jnp.tanh(c * (x + 0.044715 * x * x * x))
    return 0.5 * x * (1.0 + t), t


def gelu_slope(x):
    c = 0.7978845608028654
    t = jnp.tanh(c * (x + 0.044715 * x * x * x))
    return 0.5 * (1.0 + t) + 0.5 * x * (1.0 - t * t) * (c * (1.0 + 3.0 * 0.044715 * x * x))


def kernel(
    n_lon, n_lat, slots, patch, variables,
    latent, w1, b1, w2, b2, head, hbias, land, ok, err, band, cell, count, value,
    out,
    lat_ext, sa_hi, sa_lo, w1_v, w1_hi, w1_lo, w2_v, w2_hi, w2_lo, b1_v, b2_v,
    pre1, act1, sb_hi, sb_lo, pre2, head_v, head_hi, head_lo, hb_v, land_v, ok_v, err_v,
    band_v, cell_v, count_v, value_v, ok_rows, inv_row,
    oh, oht, oht_msg, pmt, land_send, land_recv, term_send, term_recv,
    g_ext, sg_hi, sg_lo, p_ext, sp_hi, sp_lo, out_v,
    load_sem, h_send, h_recv, g_send, g_recv, l_send, l_recv, t_send, t_recv,
):
    lon, lat = lax.axis_index("lon"), lax.axis_index("lat")
    north = 1 - lax.div(lat + n_lat - 1, n_lat)
    south = lax.div(lat + 1, n_lat)
    northf, southf = north.astype(F32), south.astype(F32)
    hid = w1_v.shape[1]
    k1 = lat_ext.shape[2]

    loads = [
        (band, band_v.at[:, 0:n_lat * slots]),
        (cell, cell_v.at[:, 0:n_lat * slots]),
        (count, count_v.at[:, 0:n_lat * slots]),
        (land, land_v),
        (latent, lat_ext.at[2:10, SIDE:SIDE + 64, :]),
        (w1, w1_v),
        (b1, b1_v),
        (ok, ok_v),
        (err, err_v),
        (hbias, hb_v),
        (w2, w2_v),
        (b2, b2_v),
        (value, value_v),
        (head, head_v),
    ]
    copies = [pltpu.make_async_copy(s, d, load_sem.at[i]) for i, (s, d) in enumerate(loads)]
    (ld_band, ld_cell, ld_count, ld_land, ld_lat, ld_w1, ld_b1, ld_ok, ld_err, ld_hb, ld_w2, ld_b2, ld_value,
     ld_head) = copies
    for copy in copies[:5]:
        copy.start()

    half = n_lon // 2
    up_lat, down_lat = lat - 1 + north, lat + 1 - south
    around = []
    for dr in (-1, 0, 1):
        for dc in (-1, 0, 1):
            if dr == 0 and dc == 0:
                continue
            turn = half * north if dr < 0 else half * south if dr > 0 else 0
            to_lon = lax.rem(lon + dc + turn + n_lon, n_lon)
            to_lat = up_lat if dr < 0 else down_lat if dr > 0 else lat
            around.append((dr, dc, (to_lon, to_lat)))

    deep = n_lat // 2
    steps = [(far, step) for far in range(2) for step in range(deep) if far or step]
    steps.sort(key=lambda s: -(2 * s[0] + min(s[1], deep - s[1])))
    peers = [lax.rem(lax.div(lat, deep) + far, 2) * deep + lax.rem(lax.rem(lat, deep) + step, deep)
             for far, step in steps]

    barrier = pltpu.get_barrier_semaphore()
    for peer in peers:
        pl.semaphore_signal(barrier, inc=1, device_id=(lon, peer), device_id_type=MESH)
    for _, _, device in around:
        pl.semaphore_signal(barrier, inc=1, device_id=device, device_id_type=MESH)
    for copy in copies[5:]:
        copy.start()

    def rim(buf, send_sem, recv_sem):
        sent = []
        for number, (dr, dc, device) in enumerate(around):
            src_r = (2, 2) if dr < 0 else (8, 2) if dr > 0 else (2, 8)
            src_c = (SIDE, SIDE) if dc < 0 else (SIDE + 56, SIDE) if dc > 0 else (SIDE, 64)
            dst_c = 72 if dc < 0 else 0 if dc > 0 else SIDE
            if dr < 0:
                dst_r, side = 10 - 10 * north, 2 - 2 * north
            elif dr > 0:
                dst_r, side = 10 * south, 2 * south
            else:
                dst_r, side = 2, 1
            slot = side * 3 + (1 - dc)
            src = buf.at[pl.ds(src_r[0], src_r[1]), pl.ds(src_c[0], src_c[1]), :]
            dst = buf.at[pl.ds(dst_r, src_r[1]), pl.ds(dst_c, src_c[1]), :]
            copy = pltpu.make_async_remote_copy(
                src_ref=src, dst_ref=dst, send_sem=send_sem.at[number], recv_sem=recv_sem.at[slot],
                device_id=device, device_id_type=MESH)
            copy.start()
            sent.append(copy)
        return sent

    def rim_arrived(buf, recv_sem, send_sem):
        for number, (dr, dc, device) in enumerate(around):
            rows_ = (0, 2) if dr < 0 else (10, 2) if dr > 0 else (2, 8)
            cols_ = (0, SIDE) if dc < 0 else (72, SIDE) if dc > 0 else (SIDE, 64)
            ref = buf.at[pl.ds(rows_[0], rows_[1]), pl.ds(cols_[0], cols_[1]), :]
            slot = (dr + 1) * 3 + dc + 1
            pltpu.make_async_remote_copy(
                src_ref=ref, dst_ref=ref, send_sem=send_sem.at[number], recv_sem=recv_sem.at[slot],
                device_id=device, device_id_type=MESH).wait_recv()

    def exchange(src, dst, send_sem, recv_sem):
        sent = []
        for number, peer in enumerate(peers):
            copy = pltpu.make_async_remote_copy(
                src_ref=src.at[peer], dst_ref=dst.at[lat], send_sem=send_sem.at[number], recv_sem=recv_sem.at[lat],
                device_id=(lon, peer), device_id_type=MESH)
            copy.start()
            sent.append(copy)
        dst[pl.ds(lat, 1)] = src[pl.ds(lat, 1)]
        return sent

    def arrived(dst, send_sem, recv_sem):
        for number, peer in enumerate(peers):
            pltpu.make_async_remote_copy(
                src_ref=dst.at[peer], dst_ref=dst.at[peer], send_sem=send_sem.at[number], recv_sem=recv_sem.at[peer],
                device_id=(lon, peer), device_id_type=MESH).wait_recv()

    def split(src, high_ref, low_ref, step):
        def body(i, carry):
            at = pl.ds(pl.multiple_of(i * step, step), step)
            high, low = halves(src[at, :])
            high_ref[at, :] = high
            low_ref[at, :] = low
            return carry
        lax.fori_loop(0, src.shape[0] // step, body, 0)

    lat_ext[:, 80:88, :] = jnp.zeros((12, 8, k1), F32)
    g_ext[:, 80:88, :] = jnp.zeros((12, 8, hid), F32)

    ld_band.wait()
    ld_cell.wait()
    ld_count.wait()
    lane = lax.broadcasted_iota(jnp.int32, (n_lat, 128), 1)
    live = lane < slots

    def blocks(ref):
        row = ref[...]
        return jnp.concatenate([row[:, slots * a:slots * a + 128] for a in range(n_lat)], axis=0)

    bands, cells, counts = blocks(band_v), blocks(cell_v), blocks(count_v)
    below = (lax.broadcasted_iota(jnp.int32, (128, 128), 0) < lax.broadcasted_iota(jnp.int32, (128, 128), 1))
    below = below.astype(F32).astype(BF16)
    mine = jnp.where(live & (bands == lat), 1.0, 0.0)
    pick = jnp.where(mine > 0.0, nn(mine.astype(BF16), below), -1.0)
    cellsf = cells.astype(F32) + 1.0
    countsf = counts.astype(F32) * 0.125
    msg_k = lax.rem(lax.broadcasted_iota(jnp.int32, (MSG, 128), 0), CAP).astype(F32)
    first = lax.broadcasted_iota(jnp.int32, (MSG, 128), 0) < CAP
    taken = n_lat * CAP
    named, merged = [], []
    for q in range(n_lat // 2):
        def two(x):
            return jnp.where(first, x[2 * q:2 * q + 1], x[2 * q + 1:2 * q + 2])
        hit = two(pick) == msg_k
        named.append(jnp.sum(jnp.where(hit, two(cellsf), 0.0), axis=1, keepdims=True))
        merged.append(jnp.sum(jnp.where(hit, two(countsf), 0.0), axis=1, keepdims=True))
    wanted = jnp.concatenate(named, axis=0).astype(jnp.int32) - 1
    weight = jnp.concatenate(merged, axis=0)
    oh[...] = jnp.where(wanted == lax.broadcasted_iota(jnp.int32, (taken, 512), 1), 1.0, 0.0).astype(BF16)

    ld_land.wait()
    fold = (lax.broadcasted_iota(jnp.int32, (64, 512), 1) >> 3) == lax.broadcasted_iota(jnp.int32, (64, 512), 0)
    fold = jnp.where(fold, 1.0, 0.0).astype(BF16)
    kept = (lax.broadcasted_iota(jnp.int32, (8, 512), 1) & 7) == lax.broadcasted_iota(jnp.int32, (8, 512), 0)
    tiles = []
    for r in range(8):
        strip = land_v[8 * r:8 * r + 8, :].astype(F32)
        spread = jnp.concatenate([jnp.where(kept, strip[p:p + 1], 0.0) for p in range(8)], axis=0)
        tiles.append(nt(fold, spread.astype(BF16)))
    tiles = jnp.concatenate(tiles, axis=0)
    tiles = jnp.concatenate([tiles, 1.0 - tiles], axis=1).astype(BF16)
    flags = nn(oh[...], tiles)
    lrows = n_lat * LCAP
    row = lax.broadcasted_iota(jnp.int32, (lrows, taken), 0)
    into = (row & (LCAP - 1)) + (row >> 4) * CAP == lax.broadcasted_iota(jnp.int32, (lrows, taken), 1)
    into = into & ((row & (LCAP - 1)) < CAP)
    land_send[...] = nn(jnp.where(into, 1.0, 0.0).astype(BF16), flags.astype(BF16)).reshape(n_lat, LCAP, 128)
    flags_w = (flags * weight).astype(BF16)

    pl.semaphore_wait(barrier, len(around) + len(peers))
    land_sent = exchange(land_send, land_recv, l_send, l_recv)
    ld_lat.wait()
    rim1 = rim(lat_ext, h_send, h_recv)

    ld_w1.wait()
    split(w1_v, w1_hi, w1_lo, 128)

    own = lax.broadcasted_iota(jnp.int32, (n_lat, 128), 0) == lat
    own_band = jnp.sum(jnp.where(own, bands, 0), axis=0, keepdims=True)
    own_count = jnp.sum(jnp.where(own, countsf, 0.0), axis=0, keepdims=True)
    theirs = jnp.where(live & (own_band == lax.broadcasted_iota(jnp.int32, (n_lat, 128), 0)), 1.0, 0.0)
    place = jnp.where(theirs > 0.0, nn(theirs.astype(BF16), below), -1.0)
    land_k = lax.broadcasted_iota(jnp.int32, (LCAP, 128), 0).astype(F32)
    pmt[...] = jnp.concatenate(
        [jnp.where(place[b:b + 1] == msg_k, 1.0, 0.0) for b in range(n_lat)], axis=0).astype(BF16)
    pml = jnp.concatenate([jnp.where(place[b:b + 1] == land_k, 1.0, 0.0) for b in range(n_lat)], axis=0)
    pml = jnp.transpose(pml).astype(BF16)
    own_weight = jnp.transpose(jnp.broadcast_to(own_count, (128, 128)))[:, 0:1]

    ld_ok.wait()
    ld_err.wait()
    ld_hb.wait()
    ld_w2.wait()
    split(w2_v, w2_hi, w2_lo, 128)
    inv = 1.0 / (err_v[...] * err_v[...])
    inv_hi = inv.astype(BF16).astype(F32)
    inv_mid = (inv - inv_hi).astype(BF16).astype(F32)
    inv_lo = inv - inv_hi - inv_mid
    okf = ok_v[...].astype(F32)
    kind = lax.broadcasted_iota(jnp.int32, (16, variables), 0)
    table = jnp.where(kind == 0, inv_hi, jnp.where(kind == 1, inv_mid, jnp.where(kind == 2, inv_lo, 0.0)))
    table = table + jnp.where(kind == 3, okf[1:2], 0.0) + jnp.where(kind == 4, okf[0:1], 0.0)
    table = table.astype(BF16)
    spans = [(at, min(CHUNK, patch - at)) for at in range(0, patch, CHUNK)]
    for at, size in spans:
        place_ = lax.broadcasted_iota(jnp.int32, (1, size), 1) + at
        pixel = ((place_.astype(F32) + 0.5) * (1.0 / variables)).astype(jnp.int32)
        variable = place_ - pixel * variables
        chosen = lax.broadcasted_iota(jnp.int32, (variables, size), 0) == variable
        spread = nn(table, jnp.where(chosen, 1.0, 0.0).astype(BF16))
        inv_row[:, at:at + size] = spread[0:1] + spread[1:2] + spread[2:3]
        which = lax.broadcasted_iota(jnp.int32, (128, size), 0)
        seen = jnp.where(which == pixel, spread[3:4], jnp.where(which == pixel + 64, spread[4:5], 0.0))
        ok_rows[:, at:at + size] = seen.astype(BF16)
    ld_b1.wait()
    ld_b2.wait()
    ld_value.wait()
    ld_head.wait()
    split(head_v, head_hi, head_lo, 96)

    rim_arrived(lat_ext, h_recv, h_send)

    for j in range(3):
        span = slice(SIDE - 2 + j, SIDE - 2 + j + WIDE)
        for at, source, length in ((0, north, 1), (1, 1 - north, 1), (2, 2, 8), (10, 10 + south, 1), (11, 11 - south, 1)):
            high, low = halves(lat_ext[pl.ds(source, length), span, :])
            sa_hi[j, at:at + length] = high
            sa_lo[j, at:at + length] = low

    def taps1(ref):
        parts = []
        for i in range(3):
            for j in range(3):
                if i == 1:
                    rows_ = ref[j, 1:11]
                else:
                    first = 2 * north if i == 0 else 2 - 2 * north
                    last = 9 + 2 * south if i == 0 else 11 - 2 * south
                    rows_ = jnp.concatenate(
                        [ref[j, pl.ds(first, 1)], ref[j, 1 + i:9 + i], ref[j, pl.ds(last, 1)]], axis=0)
                parts.append(rows_.reshape(10 * WIDE, rows_.shape[2]))
        return jnp.concatenate(parts, axis=1)

    wh, wl = w1_hi[...], w1_lo[...]
    lhs = taps1(sa_hi)
    summed = nn(lhs, wh) + nn(lhs, wl) + nn(taps1(sa_lo), wh) + b1_v[...]
    pre1[...] = summed.reshape(10, WIDE, hid)
    act1[...] = gelu_parts(summed)[0].reshape(10, WIDE, hid)

    for j in range(3):
        high, low = halves(act1[:, j:j + 64, :])
        sb_hi[j] = high
        sb_lo[j] = low

    def taps2(ref):
        return jnp.concatenate([ref[j, i:i + 8].reshape(512, hid) for i in range(3) for j in range(3)], axis=1)

    wh, wl = w2_hi[...], w2_lo[...]
    lhs = taps2(sb_hi)
    summed = nn(lhs, wh) + nn(lhs, wl) + nn(taps2(sb_lo), wh) + b2_v[...]
    pre2[...] = summed
    act2, _ = gelu_parts(summed)

    arrived(land_recv, l_send, l_recv)
    flags_own = nn(pml, land_recv[...].reshape(lrows, 128).astype(BF16))
    flags_own = (flags_own * own_weight)[:slots].astype(BF16)

    def back(scaled, at, size, total):
        count_ = scaled.shape[0]
        hh, hl = head_hi[at:at + size, :], head_lo[at:at + size, :]
        high, low = halves(scaled)
        both = nn(jnp.concatenate([high, low], axis=0), hh)
        return total + both[:count_] + both[count_:] + nn(high, hl)

    terms = jnp.zeros((slots, hid), F32)
    for at, size in spans:
        span = slice(at, at + size)
        scaled = nn(flags_own, ok_rows[:, span]) * inv_row[:, span] * (value_v[:, span] - hb_v[span].reshape(1, size))
        terms = back(scaled, at, size, terms)
    high, low = halves(terms)
    both = jnp.concatenate([high, low], axis=1)
    if slots < 128:
        both = jnp.concatenate([both, jnp.zeros((128 - slots, 2 * hid), BF16)], axis=0)
    rows = n_lat * MSG
    upper = lax.rem(lax.broadcasted_iota(jnp.int32, (rows, 128), 0), MSG) < CAP
    sent_terms = nn(pmt[...], both)
    sent_terms = sent_terms[:, :hid] + sent_terms[:, hid:]
    term_send[...] = jnp.where(upper, sent_terms[:, :128], sent_terms[:, 128:]).reshape(n_lat, MSG, 128)
    terms_sent = exchange(term_send, term_recv, t_send, t_recv)

    high, low = halves(act2)
    cols = nn(oh[...], jnp.concatenate([high, low], axis=1)).astype(BF16)
    cols_hi, cols_lo = cols[:, :hid], cols[:, hid:]
    cols_both = jnp.concatenate([cols_hi, cols_lo], axis=0)
    terms = jnp.zeros((taken, hid), F32)
    for at, size in spans:
        span = slice(at, at + size)
        both = nt(cols_both, head_hi[span, :])
        decoded = both[:taken] + both[taken:] + nt(cols_hi, head_lo[span, :])
        terms = back(nn(flags_w, ok_rows[:, span]) * inv_row[:, span] * decoded, at, size, terms)

    wanted_row = jnp.transpose(jnp.broadcast_to(wanted.astype(F32), (taken, 128)))[0:1, :].astype(jnp.int32)
    oht[...] = jnp.where(wanted_row == lax.broadcasted_iota(jnp.int32, (512, taken), 0), 1.0, 0.0).astype(BF16)
    named = [jnp.sum(jnp.where(pick[a:a + 1] == msg_k, cellsf[a:a + 1], 0.0), axis=1, keepdims=True)
             for a in range(n_lat)]
    named = jnp.broadcast_to(jnp.concatenate(named, axis=0), (rows, 128))
    wanted_row = jnp.transpose(named)[0:1, :].astype(jnp.int32) - 1
    oht_msg[...] = jnp.where(wanted_row == lax.broadcasted_iota(jnp.int32, (512, rows), 0), 1.0, 0.0).astype(BF16)
    high, low = halves(terms)
    hidden = nn(oht[...], jnp.concatenate([high, low], axis=1))
    hidden = hidden[:, :hid] + hidden[:, hid:]
    pre2[...] = gelu_slope(pre2[...])
    pre1[...] = gelu_slope(pre1[...])
    for copy in rim1 + land_sent:
        copy.wait_send()

    arrived(term_recv, t_send, t_recv)

    came = term_recv[...].reshape(rows, 128)
    came = jnp.concatenate([jnp.where(upper, came, 0.0), jnp.where(upper, 0.0, came)], axis=1)
    high, low = halves(came)
    came = nn(oht_msg[...], jnp.concatenate([high, low], axis=1))
    grad2 = (hidden - came[:, :hid] - came[:, hid:]) * pre2[...]
    g_ext[2:10, SIDE:SIDE + 64, :] = grad2.reshape(8, 64, hid)
    rim2 = rim(g_ext, g_send, g_recv)
    for copy in terms_sent:
        copy.wait_send()

    rim_arrived(g_ext, g_recv, g_send)

    for j in range(3):
        span = slice(SIDE - j, SIDE - j + WIDE)

        def row(at, length=1):
            return g_ext[pl.ds(at, length), span, :]

        r0, r1, r10, r11 = row(north), row(1 - north), row(10 + south), row(11 - south)
        pieces = (
            (0, r0), (1, r1), (2, row(2, 8)), (10, r10), (11, r11),
            (12, row(2) + northf * r0), (13, row(3) + northf * r1),
            (14, r10 * (1.0 - southf)), (15, r11 * (1.0 - southf)),
            (16, r0 * (1.0 - northf)), (17, r1 * (1.0 - northf)),
            (18, row(8) + southf * r10), (19, row(9) + southf * r11),
        )
        for at, piece in pieces:
            high, low = halves(piece)
            sg_hi[j, at:at + piece.shape[0]] = high
            sg_lo[j, at:at + piece.shape[0]] = low

    def taps3(ref):
        parts = []
        for i in range(3):
            for j in range(3):
                if i == 0:
                    rows_ = jnp.concatenate([ref[j, 12:14], ref[j, 4:10], ref[j, 14:16]], axis=0)
                elif i == 1:
                    rows_ = ref[j, 1:11]
                else:
                    rows_ = jnp.concatenate([ref[j, 16:18], ref[j, 2:8], ref[j, 18:20]], axis=0)
                parts.append(rows_.reshape(10 * WIDE, hid))
        return jnp.concatenate(parts, axis=1)

    wh = jnp.concatenate([w2_hi[t * hid:(t + 1) * hid] for t in range(9)], axis=1)
    wl = jnp.concatenate([w2_lo[t * hid:(t + 1) * hid] for t in range(9)], axis=1)
    lhs = taps3(sg_hi)
    grad1 = nt(lhs, wh) + nt(lhs, wl) + nt(taps3(sg_lo), wh)
    p_ext[...] = grad1.reshape(10, WIDE, hid) * pre1[...]

    for j in range(3):
        span = slice(2 - j, 2 - j + 64)
        q0, q9 = p_ext[0:1, span, :], p_ext[9:10, span, :]
        pieces = (
            (0, p_ext[:, span, :]),
            (10, p_ext[2:3, span, :] + northf * q0), (11, q9 * (1.0 - southf)),
            (12, q0 * (1.0 - northf)), (13, p_ext[7:8, span, :] + southf * q9),
        )
        for at, piece in pieces:
            high, low = halves(piece)
            sp_hi[j, at:at + piece.shape[0]] = high
            sp_lo[j, at:at + piece.shape[0]] = low

    def taps4(ref):
        parts = []
        for i in range(3):
            for j in range(3):
                if i == 0:
                    rows_ = jnp.concatenate([ref[j, 10:11], ref[j, 3:9], ref[j, 11:12]], axis=0)
                elif i == 1:
                    rows_ = ref[j, 1:9]
                else:
                    rows_ = jnp.concatenate([ref[j, 12:13], ref[j, 1:7], ref[j, 13:14]], axis=0)
                parts.append(rows_.reshape(512, hid))
        return jnp.concatenate(parts, axis=1)

    wh = jnp.concatenate([w1_hi[t * k1:(t + 1) * k1] for t in range(9)], axis=1)
    wl = jnp.concatenate([w1_lo[t * k1:(t + 1) * k1] for t in range(9)], axis=1)
    both = nt(taps4(sp_hi), jnp.concatenate([wh, wl], axis=0))
    result = both[:, :k1] + both[:, k1:] + nt(taps4(sp_lo), wh)
    out_v[...] = result.reshape(8, 64, k1)
    done = pltpu.make_async_copy(out_v, out, load_sem.at[0])
    done.start()
    for copy in rim2:
        copy.wait_send()
    done.wait()


def shards(n_lon, n_lat, latent, conv1_weight, conv1_bias, conv2_weight, conv2_bias, head_weight, head_bias, land_sea,
           var_ok, obs_error, obs_band, obs_cell, obs_count, obs_value):
    lc, hid = conv1_weight.shape[2], conv1_weight.shape[3]
    slots, patch = obs_value.shape[1], obs_value.shape[2]
    variables = var_ok.shape[1]
    listed = n_lat * slots
    padded = -(-(listed + 128) // 128) * 128
    vmem = pltpu.VMEM
    rows = n_lat * MSG
    scratch = [
        vmem((12, BUF, lc), F32),
        vmem((3, 12, WIDE, lc), BF16), vmem((3, 12, WIDE, lc), BF16),
        vmem((9 * lc, hid), F32), vmem((9 * lc, hid), BF16), vmem((9 * lc, hid), BF16),
        vmem((9 * hid, hid), F32), vmem((9 * hid, hid), BF16), vmem((9 * hid, hid), BF16),
        vmem((1, hid), F32), vmem((1, hid), F32),
        vmem((10, WIDE, hid), F32), vmem((10, WIDE, hid), F32),
        vmem((3, 10, 64, hid), BF16), vmem((3, 10, 64, hid), BF16),
        vmem((512, hid), F32),
        vmem((patch, hid), F32), vmem((patch, hid), BF16), vmem((patch, hid), BF16),
        vmem((patch,), F32), vmem(land_sea.shape, jnp.int32), vmem(var_ok.shape, jnp.int32),
        vmem((1, variables), F32),
        vmem((1, padded), jnp.int32), vmem((1, padded), jnp.int32), vmem((1, padded), jnp.int32),
        vmem((slots, patch), F32), vmem((128, patch), BF16), vmem((1, patch), F32),
        vmem((n_lat * CAP, 512), BF16), vmem((512, n_lat * CAP), BF16), vmem((512, rows), BF16),
        vmem((rows, 128), BF16),
        vmem((n_lat, LCAP, 128), F32), vmem((n_lat, LCAP, 128), F32),
        vmem((n_lat, MSG, 128), F32), vmem((n_lat, MSG, 128), F32),
        vmem((12, BUF, hid), F32),
        vmem((3, 20, WIDE, hid), BF16), vmem((3, 20, WIDE, hid), BF16),
        vmem((10, WIDE, hid), F32),
        vmem((3, 14, 64, hid), BF16), vmem((3, 14, 64, hid), BF16),
        vmem((8, 64, lc), F32),
        pltpu.SemaphoreType.DMA((14,)),
        pltpu.SemaphoreType.DMA((8,)), pltpu.SemaphoreType.DMA((9,)),
        pltpu.SemaphoreType.DMA((8,)), pltpu.SemaphoreType.DMA((9,)),
    ] + [pltpu.SemaphoreType.DMA((n_lat,))] * 4
    return pl.pallas_call(
        functools.partial(kernel, n_lon, n_lat, slots, patch, variables),
        out_shape=jax.ShapeDtypeStruct(latent.shape, F32),
        in_specs=[pl.BlockSpec(memory_space=pl.ANY)] * 14,
        out_specs=pl.BlockSpec(memory_space=pl.ANY),
        scratch_shapes=scratch,
        compiler_params=pltpu.CompilerParams(
            collective_id=0, has_side_effects=True, vmem_limit_bytes=60 * 1024 * 1024),
    )(latent, conv1_weight.reshape(9 * lc, hid), conv1_bias.reshape(1, hid), conv2_weight.reshape(9 * hid, hid),
      conv2_bias.reshape(1, hid), head_weight.T, head_bias, land_sea, var_ok,
      obs_error.reshape(1, variables), obs_band.reshape(1, listed), obs_cell, obs_count, obs_value[0])


def solution(mesh):
    in_specs = (
        P("lat", "lon", None),
        P(),
        P(),
        P(),
        P(),
        P(),
        P(),
        P("lat", "lon"),
        P(),
        P(),
        P("lon", None, None),
        P("lon", None),
        P("lon", None),
        P("lon", "lat", None),
    )
    out_specs = P("lat", "lon", None)
    body = functools.partial(shards, mesh.shape["lon"], mesh.shape["lat"])
    return jax.shard_map(body, mesh=mesh, in_specs=in_specs, out_specs=out_specs, check_vma=False)
```

```python
import functools

import jax
import jax.numpy as jnp
from jax import lax
from jax.experimental import pallas as pl
from jax.experimental.pallas import tpu as pltpu
from jax.sharding import PartitionSpec as P

F32 = jnp.float32
BF16 = jnp.bfloat16
CAP = 12
MSG = 2 * CAP
LCAP = 16
SIDE = 8
PAIRS = 40
BUF = 88
CHUNK = 512
MESH = pl.DeviceIdType.MESH


def halves(x):
    high = x.astype(BF16)
    return high, (x - high.astype(F32)).astype(BF16)


def nn(a, b):
    return lax.dot_general(a, b, (((1,), (0,)), ((), ())), preferred_element_type=F32)


def nt(a, b):
    return lax.dot_general(a, b, (((1,), (1,)), ((), ())), preferred_element_type=F32)


def gelu_parts(x):
    c = 0.7978845608028654
    t = jnp.tanh(c * (x + 0.044715 * x * x * x))
    return 0.5 * x * (1.0 + t), t


def gelu_slope(x):
    c = 0.7978845608028654
    t = jnp.tanh(c * (x + 0.044715 * x * x * x))
    return 0.5 * (1.0 + t) + 0.5 * x * (1.0 - t * t) * (c * (1.0 + 3.0 * 0.044715 * x * x))


def kernel(
    n_lon, n_lat, slots, patch, variables,
    latent, w1, b1, w2, b2, head, hbias, land, ok, err, band, cell, count, value,
    out,
    lat_ext, sa_hi, sa_lo, w1_v, w1_hi, w1_lo, w2_v, w2_hi, w2_lo, b1_v, b2_v,
    pre1, act1, sb_hi, sb_lo, pre2, head_v, head_hi, head_lo, hb_v, land_v, ok_v, err_v,
    band_v, cell_v, count_v, value_v, val_hi, val_lo, ok_rows, inv_row,
    oh, oht, oht_msg, pmt, land_send, land_recv, term_send, term_recv,
    g_ext, sg_hi, sg_lo, p_ext, sp_hi, sp_lo, out_v,
    load_sem, h_send, h_recv, g_send, g_recv, l_send, l_recv, t_send, t_recv,
):
    lon, lat = lax.axis_index("lon"), lax.axis_index("lat")
    north = 1 - lax.div(lat + n_lat - 1, n_lat)
    south = lax.div(lat + 1, n_lat)
    northf, southf = north.astype(F32), south.astype(F32)
    hid = w1_v.shape[1]
    k1 = latent.shape[2]

    loads = [
        (band, band_v.at[:, 0:n_lat * slots]),
        (cell, cell_v.at[:, 0:n_lat * slots]),
        (count, count_v.at[:, 0:n_lat * slots]),
        (land, land_v),
        (latent, lat_ext.at[0, 2:10, SIDE:SIDE + 64, :]),
        (w1, w1_v),
        (b1, b1_v),
        (ok, ok_v),
        (err, err_v),
        (hbias, hb_v),
        (w2, w2_v),
        (b2, b2_v),
        (value, value_v),
        (head, head_v),
    ]
    copies = [pltpu.make_async_copy(s, d, load_sem.at[i]) for i, (s, d) in enumerate(loads)]
    (ld_band, ld_cell, ld_count, ld_land, ld_lat, ld_w1, ld_b1, ld_ok, ld_err, ld_hb, ld_w2, ld_b2, ld_value,
     ld_head) = copies
    for copy in copies[:5]:
        copy.start()

    half = n_lon // 2
    up_lat, down_lat = lat - 1 + north, lat + 1 - south
    around = []
    for dr in (-1, 0, 1):
        for dc in (-1, 0, 1):
            if dr == 0 and dc == 0:
                continue
            turn = half * north if dr < 0 else half * south if dr > 0 else 0
            to_lon = lax.rem(lon + dc + turn + n_lon, n_lon)
            to_lat = up_lat if dr < 0 else down_lat if dr > 0 else lat
            around.append((dr, dc, (to_lon, to_lat)))

    deep = n_lat // 2
    steps = [(far, step) for far in range(2) for step in range(deep) if far or step]
    steps.sort(key=lambda s: -(2 * s[0] + min(s[1], deep - s[1])))
    peers = [lax.rem(lax.div(lat, deep) + far, 2) * deep + lax.rem(lax.rem(lat, deep) + step, deep)
             for far, step in steps]

    barrier = pltpu.get_barrier_semaphore()
    for peer in peers:
        pl.semaphore_signal(barrier, inc=1, device_id=(lon, peer), device_id_type=MESH)
    for _, _, device in around:
        pl.semaphore_signal(barrier, inc=1, device_id=device, device_id_type=MESH)
    for copy in copies[5:]:
        copy.start()

    def rim(buf, send_sem, recv_sem):
        sent = []
        for number, (dr, dc, device) in enumerate(around):
            src_r = (2, 2) if dr < 0 else (8, 2) if dr > 0 else (2, 8)
            src_c = (SIDE, SIDE) if dc < 0 else (SIDE + 56, SIDE) if dc > 0 else (SIDE, 64)
            dst_c = 72 if dc < 0 else 0 if dc > 0 else SIDE
            if dr < 0:
                dst_r, side = 10 - 10 * north, 2 - 2 * north
            elif dr > 0:
                dst_r, side = 10 * south, 2 * south
            else:
                dst_r, side = 2, 1
            slot = side * 3 + (1 - dc)
            src = buf.at[:, pl.ds(src_r[0], src_r[1]), pl.ds(src_c[0], src_c[1]), :]
            dst = buf.at[:, pl.ds(dst_r, src_r[1]), pl.ds(dst_c, src_c[1]), :]
            copy = pltpu.make_async_remote_copy(
                src_ref=src, dst_ref=dst, send_sem=send_sem.at[number], recv_sem=recv_sem.at[slot],
                device_id=device, device_id_type=MESH)
            copy.start()
            sent.append(copy)
        return sent

    def rim_arrived(buf, recv_sem, send_sem, sides):
        for number, (dr, dc, device) in enumerate(around):
            if (dr == 0) != sides:
                continue
            rows_ = (0, 2) if dr < 0 else (10, 2) if dr > 0 else (2, 8)
            cols_ = (0, SIDE) if dc < 0 else (72, SIDE) if dc > 0 else (SIDE, 64)
            ref = buf.at[:, pl.ds(rows_[0], rows_[1]), pl.ds(cols_[0], cols_[1]), :]
            slot = (dr + 1) * 3 + dc + 1
            pltpu.make_async_remote_copy(
                src_ref=ref, dst_ref=ref, send_sem=send_sem.at[number], recv_sem=recv_sem.at[slot],
                device_id=device, device_id_type=MESH).wait_recv()

    def exchange(src, dst, send_sem, recv_sem):
        sent = []
        for number, peer in enumerate(peers):
            copy = pltpu.make_async_remote_copy(
                src_ref=src.at[peer], dst_ref=dst.at[lat], send_sem=send_sem.at[number], recv_sem=recv_sem.at[lat],
                device_id=(lon, peer), device_id_type=MESH)
            copy.start()
            sent.append(copy)
        dst[pl.ds(lat, 1)] = src[pl.ds(lat, 1)]
        return sent

    def arrived(dst, send_sem, recv_sem):
        for number, peer in enumerate(peers):
            pltpu.make_async_remote_copy(
                src_ref=dst.at[peer], dst_ref=dst.at[peer], send_sem=send_sem.at[number], recv_sem=recv_sem.at[peer],
                device_id=(lon, peer), device_id_type=MESH).wait_recv()

    def split(src, high_ref, low_ref, step):
        def body(i, carry):
            at = pl.ds(pl.multiple_of(i * step, step), step)
            high_ref[at, :], low_ref[at, :] = halves(src[at, :])
            return carry
        lax.fori_loop(0, src.shape[0] // step, body, 0)

    def split_taps(src, high_ref, low_ref, depth, step):
        for i in range(3):
            def body(n, carry):
                g0, g1, g2 = (src[pl.ds(pl.multiple_of((3 * i + j) * depth + n * step, step), step), :] for j in range(3))
                outer, inner = 0.5 * (g0 + g2), 0.5 * g1
                at = pl.ds(pl.multiple_of(i * depth + n * step, step), step)
                for m, factor in enumerate((g0, outer + inner, outer - inner, g2)):
                    high_ref[m, at, :], low_ref[m, at, :] = halves(factor)
                return carry
            lax.fori_loop(0, depth // step, body, 0)

    def factors(d0, d1, d2, d3):
        return d0 - d2, d1 + d2, d2 - d1, d1 - d3

    def pair_rows(buf, at, length=1):
        def column(d):
            lanes = [buf[h, pl.ds(at, length), pl.ds(SIDE - 2 + d, PAIRS, stride=2), :] for h in range(buf.shape[0])]
            return jnp.concatenate(lanes, axis=2)
        return factors(*[column(d) for d in range(4)])

    def put_rows(high_ref, low_ref, at, pieces):
        for m, piece in enumerate(pieces):
            count_ = piece.shape[0] // 2
            high_ref[m, at:at + count_], low_ref[m, at:at + count_] = halves(
                piece.reshape(count_, 2 * PAIRS, piece.shape[2]))

    def joined(*rows_):
        return [jnp.concatenate(list(x), axis=0) for x in zip(*rows_)]

    def inner_rows(buf, high_ref, low_ref):
        pieces = pair_rows(buf, 2, 8)
        put_rows(high_ref, low_ref, 0, pieces)
        put_rows(high_ref, low_ref, 4, [x[1:7] for x in pieces])

    def pair_sums(taken_hi, taken_lo, weights):
        parts = []
        for m in range(4):
            lhs, (wh, wl, dot) = taken_hi(m), weights(m)
            parts.append(dot(lhs, wh) + dot(lhs, wl) + dot(taken_lo(m), wh))
        m0, m1, m2, m3 = parts
        return m0 + m1 + m2, m1 - m2 - m3

    def taps(ref, chosen):
        def lhs(m):
            rows_ = [jnp.concatenate([ref[m, a:b] for a, b in part], axis=0) for part in chosen]
            return jnp.concatenate([x.reshape(x.shape[0] * x.shape[1], x.shape[2]) for x in rows_], axis=1)
        return lhs

    lat_ext[:, :, 80:88, :] = jnp.zeros((k1 // 128, 12, 8, 128), F32)
    g_ext[:, :, 80:88, :] = jnp.zeros((hid // 128, 12, 8, 128), F32)

    ld_band.wait()
    ld_cell.wait()
    ld_count.wait()
    lane = lax.broadcasted_iota(jnp.int32, (n_lat, 128), 1)
    live = lane < slots

    def blocks(ref):
        row = ref[...]
        return jnp.concatenate([row[:, slots * a:slots * a + 128] for a in range(n_lat)], axis=0)

    bands, cells, counts = blocks(band_v), blocks(cell_v), blocks(count_v)
    below = (lax.broadcasted_iota(jnp.int32, (128, 128), 0) < lax.broadcasted_iota(jnp.int32, (128, 128), 1))
    below = below.astype(F32).astype(BF16)
    mine = jnp.where(live & (bands == lat), 1.0, 0.0)
    pick = jnp.where(mine > 0.0, nn(mine.astype(BF16), below), -1.0)
    cells = ((cells >> 6) << 5) + ((cells & 63) >> 1) + ((cells & 1) << 8)
    cellsf = cells.astype(F32) + 1.0
    countsf = counts.astype(F32) * 0.125
    msg_k = lax.rem(lax.broadcasted_iota(jnp.int32, (MSG, 128), 0), CAP).astype(F32)
    first = lax.broadcasted_iota(jnp.int32, (MSG, 128), 0) < CAP
    taken = n_lat * CAP
    named, merged = [], []
    for q in range(n_lat // 2):
        def two(x):
            return jnp.where(first, x[2 * q:2 * q + 1], x[2 * q + 1:2 * q + 2])
        hit = two(pick) == msg_k
        named.append(jnp.sum(jnp.where(hit, two(cellsf), 0.0), axis=1, keepdims=True))
        merged.append(jnp.sum(jnp.where(hit, two(countsf), 0.0), axis=1, keepdims=True))
    wanted = jnp.concatenate(named, axis=0).astype(jnp.int32) - 1
    weight = jnp.concatenate(merged, axis=0)
    oh[...] = jnp.where(wanted == lax.broadcasted_iota(jnp.int32, (taken, 512), 1), 1.0, 0.0).astype(BF16)

    ld_land.wait()
    column = lax.broadcasted_iota(jnp.int32, (64, 512), 0)
    column = ((column & 31) << 1) + (column >> 5)
    fold = (lax.broadcasted_iota(jnp.int32, (64, 512), 1) >> 3) == column
    fold = jnp.where(fold, 1.0, 0.0).astype(BF16)
    kept = (lax.broadcasted_iota(jnp.int32, (8, 512), 1) & 7) == lax.broadcasted_iota(jnp.int32, (8, 512), 0)
    tiles = []
    for r in range(8):
        strip = land_v[8 * r:8 * r + 8, :].astype(F32)
        spread = jnp.concatenate([jnp.where(kept, strip[p:p + 1], 0.0) for p in range(8)], axis=0)
        tiles.append(nt(fold, spread.astype(BF16)))
    tiles = jnp.concatenate([x[:32] for x in tiles] + [x[32:] for x in tiles], axis=0)
    tiles = jnp.concatenate([tiles, 1.0 - tiles], axis=1).astype(BF16)
    flags = nn(oh[...], tiles)
    lrows = n_lat * LCAP
    row = lax.broadcasted_iota(jnp.int32, (lrows, taken), 0)
    into = (row & (LCAP - 1)) + (row >> 4) * CAP == lax.broadcasted_iota(jnp.int32, (lrows, taken), 1)
    into = into & ((row & (LCAP - 1)) < CAP)
    land_send[...] = nn(jnp.where(into, 1.0, 0.0).astype(BF16), flags.astype(BF16)).reshape(n_lat, LCAP, 128)
    flags_w = (flags * weight).astype(BF16)

    pl.semaphore_wait(barrier, len(around) + len(peers))
    land_sent = exchange(land_send, land_recv, l_send, l_recv)
    ld_lat.wait()
    rim1 = rim(lat_ext, h_send, h_recv)

    ld_w1.wait()
    split_taps(w1_v, w1_hi, w1_lo, k1, 64)

    own = lax.broadcasted_iota(jnp.int32, (n_lat, 128), 0) == lat
    own_band = jnp.sum(jnp.where(own, bands, 0), axis=0, keepdims=True)
    own_count = jnp.sum(jnp.where(own, countsf, 0.0), axis=0, keepdims=True)
    theirs = jnp.where(live & (own_band == lax.broadcasted_iota(jnp.int32, (n_lat, 128), 0)), 1.0, 0.0)
    place = jnp.where(theirs > 0.0, nn(theirs.astype(BF16), below), -1.0)
    land_k = lax.broadcasted_iota(jnp.int32, (LCAP, 128), 0).astype(F32)
    pmt[...] = jnp.concatenate(
        [jnp.where(place[b:b + 1] == msg_k, 1.0, 0.0) for b in range(n_lat)], axis=0).astype(BF16)
    pml = jnp.concatenate([jnp.where(place[b:b + 1] == land_k, 1.0, 0.0) for b in range(n_lat)], axis=0)
    pml = jnp.transpose(pml).astype(BF16)
    own_weight = jnp.transpose(jnp.broadcast_to(own_count, (128, 128)))[:, 0:1]

    ld_ok.wait()
    ld_err.wait()
    ld_hb.wait()
    ld_w2.wait()
    split_taps(w2_v, w2_hi, w2_lo, hid, 64)
    inv = 1.0 / (err_v[...] * err_v[...])
    inv_hi = inv.astype(BF16).astype(F32)
    inv_mid = (inv - inv_hi).astype(BF16).astype(F32)
    inv_lo = inv - inv_hi - inv_mid
    okf = ok_v[...].astype(F32)
    kind = lax.broadcasted_iota(jnp.int32, (16, variables), 0)
    table = jnp.where(kind == 0, inv_hi, jnp.where(kind == 1, inv_mid, jnp.where(kind == 2, inv_lo, 0.0)))
    table = table + jnp.where(kind == 3, okf[1:2], 0.0) + jnp.where(kind == 4, okf[0:1], 0.0)
    table = table.astype(BF16)
    spans = [(at, min(CHUNK, patch - at)) for at in range(0, patch, CHUNK)]
    for at, size in spans:
        place_ = lax.broadcasted_iota(jnp.int32, (1, size), 1) + at
        pixel = ((place_.astype(F32) + 0.5) * (1.0 / variables)).astype(jnp.int32)
        variable = place_ - pixel * variables
        chosen = lax.broadcasted_iota(jnp.int32, (variables, size), 0) == variable
        spread = nn(table, jnp.where(chosen, 1.0, 0.0).astype(BF16))
        inv_row[:, at:at + size] = spread[0:1] + spread[1:2] + spread[2:3]
        which = lax.broadcasted_iota(jnp.int32, (128, size), 0)
        seen = jnp.where(which == pixel, spread[3:4], jnp.where(which == pixel + 64, spread[4:5], 0.0))
        ok_rows[:, at:at + size] = seen.astype(BF16)
    ld_b1.wait()
    ld_b2.wait()
    ld_value.wait()
    for at, size in spans:
        span = slice(at, at + size)
        shifted = (value_v[:, span] - hb_v[span].reshape(1, size)) * inv_row[:, span]
        val_hi[:, span], val_lo[:, span] = halves(shifted)
    ld_head.wait()
    split(head_v, head_hi, head_lo, 96)

    rim_arrived(lat_ext, h_recv, h_send, True)

    def forward1(m):
        return w1_hi[m], w1_lo[m], nn

    def put1(chosen, groups):
        for parity, summed in enumerate(pair_sums(taps(sa_hi, chosen), taps(sa_lo, chosen), forward1)):
            summed = summed + b1_v[...]
            act = gelu_parts(summed)[0]
            for source, target, length in groups:
                part = slice(source * PAIRS, (source + length) * PAIRS)
                pre1[parity, target:target + length] = summed[part].reshape(length, PAIRS, hid)
                act1[parity, target:target + length] = act[part].reshape(length, PAIRS, hid)

    inner_rows(lat_ext, sa_hi, sa_lo)
    put1((((0, 3),), ((4, 7),), ((1, 4),)), ((0, 2, 6),))
    rim_arrived(lat_ext, h_recv, h_send, False)
    for at, one, other in (
        (7, 1 - north, 2), (8, 9, 10 + south),
        (9, 2 * north, 1 - north), (10, 8, 9 + south),
        (11, 2 - north, 3), (12, 10 + south, 11 - 2 * south),
    ):
        put_rows(sa_hi, sa_lo, at, joined(pair_rows(lat_ext, one), pair_rows(lat_ext, other)))
    put1((((9, 11),), ((7, 9),), ((11, 13),)), ((0, 0, 2), (2, 8, 2)))

    arrived(land_recv, l_send, l_recv)
    flags_own = nn(pml, land_recv[...].reshape(lrows, 128).astype(BF16))
    flags_own = flags_own[:slots].astype(BF16)

    def back(high, low, at, size, total):
        count_ = high.shape[0]
        hh, hl = head_hi[at:at + size, :], head_lo[at:at + size, :]
        both = nn(jnp.concatenate([high, low], axis=0), hh)
        return total + both[:count_] + both[count_:] + nn(high, hl)

    terms = jnp.zeros((slots, hid), F32)
    for at, size in spans:
        span = slice(at, at + size)
        seen = nn(flags_own, ok_rows[:, span]).astype(BF16)
        terms = back(val_hi[:, span] * seen, val_lo[:, span] * seen, at, size, terms)
    terms = terms * own_weight[:slots]
    high, low = halves(terms)
    both = jnp.concatenate([high, low], axis=1)
    if slots < 128:
        both = jnp.concatenate([both, jnp.zeros((128 - slots, 2 * hid), BF16)], axis=0)
    rows = n_lat * MSG
    upper = lax.rem(lax.broadcasted_iota(jnp.int32, (rows, 128), 0), MSG) < CAP
    sent_terms = nn(pmt[...], both)
    sent_terms = sent_terms[:, :hid] + sent_terms[:, hid:]
    term_send[...] = jnp.where(upper, sent_terms[:, :128], sent_terms[:, 128:]).reshape(n_lat, MSG, 128)
    terms_sent = exchange(term_send, term_recv, t_send, t_recv)

    def near(ref, rows_=slice(0, 10)):
        return factors(ref[0, rows_, 0:32], ref[1, rows_, 0:32], ref[0, rows_, 1:33], ref[1, rows_, 1:33])

    for m, piece in enumerate(near(act1)):
        sb_hi[m], sb_lo[m] = halves(piece)

    def forward2(m):
        return w2_hi[m], w2_lo[m], nn

    chosen = tuple(((i, i + 8),) for i in range(3))
    summed = jnp.concatenate(pair_sums(taps(sb_hi, chosen), taps(sb_lo, chosen), forward2), axis=0) + b2_v[...]
    pre2[...] = summed
    act2, _ = gelu_parts(summed)

    high, low = halves(act2)
    cols = nn(oh[...], jnp.concatenate([high, low], axis=1)).astype(BF16)
    cols_hi, cols_lo = cols[:, :hid], cols[:, hid:]
    cols_both = jnp.concatenate([cols_hi, cols_lo], axis=0)
    terms = jnp.zeros((taken, hid), F32)
    for at, size in spans:
        span = slice(at, at + size)
        both = nt(cols_both, head_hi[span, :])
        decoded = both[:taken] + both[taken:] + nt(cols_hi, head_lo[span, :])
        high, low = halves(nn(flags_w, ok_rows[:, span]) * inv_row[:, span] * decoded)
        terms = back(high, low, at, size, terms)

    wanted_row = jnp.transpose(jnp.broadcast_to(wanted.astype(F32), (taken, 128)))[0:1, :].astype(jnp.int32)
    oht[...] = jnp.where(wanted_row == lax.broadcasted_iota(jnp.int32, (512, taken), 0), 1.0, 0.0).astype(BF16)
    named = [jnp.sum(jnp.where(pick[a:a + 1] == msg_k, cellsf[a:a + 1], 0.0), axis=1, keepdims=True)
             for a in range(n_lat)]
    named = jnp.broadcast_to(jnp.concatenate(named, axis=0), (rows, 128))
    wanted_row = jnp.transpose(named)[0:1, :].astype(jnp.int32) - 1
    oht_msg[...] = jnp.where(wanted_row == lax.broadcasted_iota(jnp.int32, (512, rows), 0), 1.0, 0.0).astype(BF16)
    high, low = halves(terms)
    hidden = nn(oht[...], jnp.concatenate([high, low], axis=1))
    hidden = hidden[:, :hid] + hidden[:, hid:]
    pre2[...] = gelu_slope(pre2[...])
    pre1[...] = gelu_slope(pre1[...])
    for copy in rim1 + land_sent:
        copy.wait_send()

    arrived(term_recv, t_send, t_recv)

    came = term_recv[...].reshape(rows, 128)
    came = jnp.concatenate([jnp.where(upper, came, 0.0), jnp.where(upper, 0.0, came)], axis=1)
    high, low = halves(came)
    came = nn(oht_msg[...], jnp.concatenate([high, low], axis=1))
    grad2 = (hidden - came[:, :hid] - came[:, hid:]) * pre2[...]
    for parity in range(2):
        for h in range(hid // 128):
            part = grad2[256 * parity:256 * parity + 256, 128 * h:128 * h + 128]
            g_ext[h, 2:10, pl.ds(SIDE + parity, 32, stride=2), :] = part.reshape(8, 32, 128)
    rim2 = rim(g_ext, g_send, g_recv)
    for copy in terms_sent:
        copy.wait_send()

    rim_arrived(g_ext, g_recv, g_send, True)

    def backward(high_ref, low_ref, depth):
        def weights(m):
            at = (3, 1, 2, 0)[m]
            return tuple(jnp.concatenate([ref[at, i * depth:(i + 1) * depth] for i in range(3)], axis=1)
                         for ref in (high_ref, low_ref)) + (nt,)
        return weights

    def put2(chosen, groups):
        sums = pair_sums(taps(sg_hi, chosen), taps(sg_lo, chosen), backward(w2_hi, w2_lo, hid))
        for parity, grad1 in enumerate(sums):
            for source, target, length in groups:
                part = grad1[source * PAIRS:(source + length) * PAIRS].reshape(length, PAIRS, hid)
                p_ext[parity, target:target + length] = part * pre1[parity, target:target + length]

    inner_rows(g_ext, sg_hi, sg_lo)
    put2((((1, 4),), ((4, 7),), ((0, 3),)), ((0, 2, 6),))
    rim_arrived(g_ext, g_recv, g_send, False)
    r0, r1 = pair_rows(g_ext, north), pair_rows(g_ext, 1 - north)
    r10, r11 = pair_rows(g_ext, 10 + south), pair_rows(g_ext, 11 - south)

    def scaled_by(x, factor):
        return [y * factor for y in x]

    def plus(x, y, factor):
        return [u + v * factor for u, v in zip(x, y)]

    put_rows(sg_hi, sg_lo, 7, joined(r1, pair_rows(g_ext, 2)))
    put_rows(sg_hi, sg_lo, 8, joined(pair_rows(g_ext, 9), r10))
    put_rows(sg_hi, sg_lo, 9, joined(plus(pair_rows(g_ext, 2), r0, northf), plus(pair_rows(g_ext, 3), r1, northf)))
    put_rows(sg_hi, sg_lo, 10, joined(scaled_by(r10, 1.0 - southf), scaled_by(r11, 1.0 - southf)))
    put_rows(sg_hi, sg_lo, 11, joined(scaled_by(r0, 1.0 - northf), scaled_by(r1, 1.0 - northf)))
    put_rows(sg_hi, sg_lo, 12, joined(plus(pair_rows(g_ext, 8), r10, southf), plus(pair_rows(g_ext, 9), r11, southf)))
    put2((((9, 11),), ((7, 9),), ((11, 13),)), ((0, 0, 2), (2, 8, 2)))

    for m, piece in enumerate(near(p_ext)):
        q0, q9 = piece[0:1], piece[9:10]
        for at, part in (
            (0, piece), (10, piece[2:3] + northf * q0), (11, q9 * (1.0 - southf)),
            (12, q0 * (1.0 - northf)), (13, piece[7:8] + southf * q9),
        ):
            sp_hi[m, at:at + part.shape[0]], sp_lo[m, at:at + part.shape[0]] = halves(part)

    chosen = (((10, 11), (3, 9), (11, 12)), ((1, 9),), ((12, 13), (1, 7), (13, 14)))
    parts = []
    for m in range(4):
        wh, wl, dot = backward(w1_hi, w1_lo, k1)(m)
        both = dot(taps(sp_hi, chosen)(m), jnp.concatenate([wh, wl], axis=0))
        parts.append(both[:, :k1] + both[:, k1:] + dot(taps(sp_lo, chosen)(m), wh))
    m0, m1, m2, m3 = parts
    for parity, part in enumerate((m0 + m1 + m2, m1 - m2 - m3)):
        out_v[:, pl.ds(parity, 32, stride=2), :] = part.reshape(8, 32, k1)
    done = pltpu.make_async_copy(out_v, out, load_sem.at[0])
    done.start()
    for copy in rim2:
        copy.wait_send()
    done.wait()


def shards(n_lon, n_lat, latent, conv1_weight, conv1_bias, conv2_weight, conv2_bias, head_weight, head_bias, land_sea,
           var_ok, obs_error, obs_band, obs_cell, obs_count, obs_value):
    lc, hid = conv1_weight.shape[2], conv1_weight.shape[3]
    slots, patch = obs_value.shape[1], obs_value.shape[2]
    variables = var_ok.shape[1]
    listed = n_lat * slots
    padded = -(-(listed + 128) // 128) * 128
    vmem = pltpu.VMEM
    rows = n_lat * MSG
    scratch = [
        vmem((lc // 128, 12, BUF, 128), F32),
        vmem((4, 13, 2 * PAIRS, lc), BF16), vmem((4, 13, 2 * PAIRS, lc), BF16),
        vmem((9 * lc, hid), F32), vmem((4, 3 * lc, hid), BF16), vmem((4, 3 * lc, hid), BF16),
        vmem((9 * hid, hid), F32), vmem((4, 3 * hid, hid), BF16), vmem((4, 3 * hid, hid), BF16),
        vmem((1, hid), F32), vmem((1, hid), F32),
        vmem((2, 10, PAIRS, hid), F32), vmem((2, 10, PAIRS, hid), F32),
        vmem((4, 10, 32, hid), BF16), vmem((4, 10, 32, hid), BF16),
        vmem((512, hid), F32),
        vmem((patch, hid), F32), vmem((patch, hid), BF16), vmem((patch, hid), BF16),
        vmem((patch,), F32), vmem(land_sea.shape, jnp.int32), vmem(var_ok.shape, jnp.int32),
        vmem((1, variables), F32),
        vmem((1, padded), jnp.int32), vmem((1, padded), jnp.int32), vmem((1, padded), jnp.int32),
        vmem((slots, patch), F32), vmem((slots, patch), BF16), vmem((slots, patch), BF16),
        vmem((128, patch), BF16), vmem((1, patch), F32),
        vmem((n_lat * CAP, 512), BF16), vmem((512, n_lat * CAP), BF16), vmem((512, rows), BF16),
        vmem((rows, 128), BF16),
        vmem((n_lat, LCAP, 128), F32), vmem((n_lat, LCAP, 128), F32),
        vmem((n_lat, MSG, 128), F32), vmem((n_lat, MSG, 128), F32),
        vmem((hid // 128, 12, BUF, 128), F32),
        vmem((4, 13, 2 * PAIRS, hid), BF16), vmem((4, 13, 2 * PAIRS, hid), BF16),
        vmem((2, 10, PAIRS, hid), F32),
        vmem((4, 14, 32, hid), BF16), vmem((4, 14, 32, hid), BF16),
        vmem((8, 64, lc), F32),
        pltpu.SemaphoreType.DMA((14,)),
        pltpu.SemaphoreType.DMA((8,)), pltpu.SemaphoreType.DMA((9,)),
        pltpu.SemaphoreType.DMA((8,)), pltpu.SemaphoreType.DMA((9,)),
    ] + [pltpu.SemaphoreType.DMA((n_lat,))] * 4
    return pl.pallas_call(
        functools.partial(kernel, n_lon, n_lat, slots, patch, variables),
        out_shape=jax.ShapeDtypeStruct(latent.shape, F32),
        in_specs=[pl.BlockSpec(memory_space=pl.ANY)] * 14,
        out_specs=pl.BlockSpec(memory_space=pl.ANY),
        scratch_shapes=scratch,
        compiler_params=pltpu.CompilerParams(
            collective_id=0, has_side_effects=True, vmem_limit_bytes=60 * 1024 * 1024),
    )(latent, conv1_weight.reshape(9 * lc, hid), conv1_bias.reshape(1, hid), conv2_weight.reshape(9 * hid, hid),
      conv2_bias.reshape(1, hid), head_weight.T, head_bias, land_sea, var_ok,
      obs_error.reshape(1, variables), obs_band.reshape(1, listed), obs_cell, obs_count, obs_value[0])


def solution(mesh):
    in_specs = (
        P("lat", "lon", None),
        P(),
        P(),
        P(),
        P(),
        P(),
        P(),
        P("lat", "lon"),
        P(),
        P(),
        P("lon", None, None),
        P("lon", None),
        P("lon", None),
        P("lon", "lat", None),
    )
    out_specs = P("lat", "lon", None)
    body = functools.partial(shards, mesh.shape["lon"], mesh.shape["lat"])
    return jax.shard_map(body, mesh=mesh, in_specs=in_specs, out_specs=out_specs, check_vma=False)
```

```python
import functools

import jax
import jax.numpy as jnp
from jax import lax
from jax.experimental import pallas as pl
from jax.experimental.pallas import tpu as pltpu
from jax.sharding import PartitionSpec as P

F32 = jnp.float32
BF16 = jnp.bfloat16
CAP = 12
MSG = 2 * CAP
LCAP = 16
SIDE = 8
PAIRS = 40
BUF = 88
CHUNK = 512
MESH = pl.DeviceIdType.MESH


def halves(x):
    high = x.astype(BF16)
    return high, (x - high.astype(F32)).astype(BF16)


def nn(a, b):
    return lax.dot_general(a, b, (((1,), (0,)), ((), ())), preferred_element_type=F32)


def nt(a, b):
    return lax.dot_general(a, b, (((1,), (1,)), ((), ())), preferred_element_type=F32)


def gelu_parts(x):
    c = 0.7978845608028654
    t = jnp.tanh(c * (x + 0.044715 * x * x * x))
    return 0.5 * x * (1.0 + t), t


def gelu_slope(x):
    c = 0.7978845608028654
    t = jnp.tanh(c * (x + 0.044715 * x * x * x))
    return 0.5 * (1.0 + t) + 0.5 * x * (1.0 - t * t) * (c * (1.0 + 3.0 * 0.044715 * x * x))


def kernel(
    n_lon, n_lat, slots, patch, variables,
    latent, w1, b1, w2, b2, head, hbias, land, ok, err, band, cell, count, value,
    out,
    lat_ext, sa_hi, sa_lo, w1_v, w1_hi, w1_lo, w2_v, w2_hi, w2_lo, b1_v, b2_v,
    pre1, act1, sb_hi, sb_lo, pre2, head_v, head_hi, head_lo, hb_v, land_v, ok_v, err_v,
    band_v, cell_v, count_v, value_v, val_hi, val_lo, masked, ok_rows, inv_row,
    oh, oht, oht_msg, pmt, from_land, own_weight, land_send, land_recv, term_send, term_recv,
    g_ext, sg_hi, sg_lo, p_ext, sp_hi, sp_lo,
    load_sem, h_send, h_recv, g_send, g_recv, l_send, l_recv, t_send, t_recv,
):
    lon, lat = lax.axis_index("lon"), lax.axis_index("lat")
    north = 1 - lax.div(lat + n_lat - 1, n_lat)
    south = lax.div(lat + 1, n_lat)
    northf, southf = north.astype(F32), south.astype(F32)
    hid = w1_v.shape[1]
    k1 = latent.shape[2]

    loads = [
        (band, band_v.at[:, 0:n_lat * slots]),
        (cell, cell_v.at[:, 0:n_lat * slots]),
        (count, count_v.at[:, 0:n_lat * slots]),
        (land, land_v),
        (latent, lat_ext.at[0, 2:10, SIDE:SIDE + 64, :]),
        (w1, w1_v),
        (b1, b1_v),
        (ok, ok_v),
        (err, err_v),
        (hbias, hb_v),
        (w2, w2_v),
        (b2, b2_v),
        (value, value_v),
        (head, head_v),
    ]
    copies = [pltpu.make_async_copy(s, d, load_sem.at[i]) for i, (s, d) in enumerate(loads)]
    (ld_band, ld_cell, ld_count, ld_land, ld_lat, ld_w1, ld_b1, ld_ok, ld_err, ld_hb, ld_w2, ld_b2, ld_value,
     ld_head) = copies
    for copy in copies[:5]:
        copy.start()

    half = n_lon // 2
    up_lat, down_lat = lat - 1 + north, lat + 1 - south
    around = []
    for dr in (-1, 0, 1):
        for dc in (-1, 0, 1):
            if dr == 0 and dc == 0:
                continue
            turn = half * north if dr < 0 else half * south if dr > 0 else 0
            to_lon = lax.rem(lon + dc + turn + n_lon, n_lon)
            to_lat = up_lat if dr < 0 else down_lat if dr > 0 else lat
            around.append((dr, dc, (to_lon, to_lat)))

    deep = n_lat // 2
    steps = [(far, step) for far in range(2) for step in range(deep) if far or step]
    steps.sort(key=lambda s: -(2 * s[0] + min(s[1], deep - s[1])))
    peers = [lax.rem(lax.div(lat, deep) + far, 2) * deep + lax.rem(lax.rem(lat, deep) + step, deep)
             for far, step in steps]

    barrier = pltpu.get_barrier_semaphore()
    for peer in peers:
        pl.semaphore_signal(barrier, inc=1, device_id=(lon, peer), device_id_type=MESH)
    for _, _, device in around:
        pl.semaphore_signal(barrier, inc=1, device_id=device, device_id_type=MESH)
    for copy in copies[5:]:
        copy.start()

    near_rows, far_rows, corners, sides = range(4)
    parts = []
    for dr, dc, device in around:
        if dr and not dc:
            parts += [(near_rows, dr, dc, device), (far_rows, dr, dc, device)]
        else:
            parts.append((corners if dr else sides, dr, dc, device))

    def rim(buf, send_sem, recv_sem, kinds):
        sent = []
        for kind in kinds:
            for number, (its, dr, dc, device) in enumerate(parts):
                if its != kind:
                    continue
                src_c = (SIDE, SIDE) if dc < 0 else (SIDE + 56, SIDE) if dc > 0 else (SIDE, 64)
                dst_c = 72 if dc < 0 else 0 if dc > 0 else SIDE
                second = 1 if kind == far_rows else 0
                if dr < 0:
                    src_r, dst_r, side = 2 + second, 10 - 10 * north + second, 2 - 2 * north
                elif dr > 0:
                    src_r, dst_r, side = 9 - second, 1 + 10 * south - second, 2 * south
                else:
                    src_r, dst_r, side = 2, 2, 1
                length = 8 if kind == sides else 1
                if kind == corners:
                    length = 2
                    if dr > 0:
                        src_r, dst_r = 8, 10 * south
                slot = 9 * second + side * 3 + (1 - dc)
                src = buf.at[:, pl.ds(src_r, length), pl.ds(src_c[0], src_c[1]), :]
                dst = buf.at[:, pl.ds(dst_r, length), pl.ds(dst_c, src_c[1]), :]
                copy = pltpu.make_async_remote_copy(
                    src_ref=src, dst_ref=dst, send_sem=send_sem.at[number], recv_sem=recv_sem.at[slot],
                    device_id=device, device_id_type=MESH)
                copy.start()
                sent.append(copy)
        return sent

    def rim_arrived(buf, recv_sem, send_sem, kinds):
        for number, (kind, dr, dc, device) in enumerate(parts):
            if kind not in kinds:
                continue
            cols_ = (0, SIDE) if dc < 0 else (72, SIDE) if dc > 0 else (SIDE, 64)
            second = 1 if kind == far_rows else 0
            if kind == sides:
                at, length = 2, 8
            elif kind == corners:
                at, length = (0 if dr < 0 else 10), 2
            else:
                at, length = (1 - north if dr < 0 else 10 + south), 1
                if second:
                    at = north if dr < 0 else 11 - south
            ref = buf.at[:, pl.ds(at, length), pl.ds(cols_[0], cols_[1]), :]
            slot = 9 * second + (dr + 1) * 3 + dc + 1
            pltpu.make_async_remote_copy(
                src_ref=ref, dst_ref=ref, send_sem=send_sem.at[number], recv_sem=recv_sem.at[slot],
                device_id=device, device_id_type=MESH).wait_recv()

    def exchange(src, dst, send_sem, recv_sem):
        sent = []
        for number, peer in enumerate(peers):
            copy = pltpu.make_async_remote_copy(
                src_ref=src.at[peer], dst_ref=dst.at[lat], send_sem=send_sem.at[number], recv_sem=recv_sem.at[lat],
                device_id=(lon, peer), device_id_type=MESH)
            copy.start()
            sent.append(copy)
        dst[pl.ds(lat, 1)] = src[pl.ds(lat, 1)]
        return sent

    def arrived(dst, send_sem, recv_sem):
        for number, peer in enumerate(peers):
            pltpu.make_async_remote_copy(
                src_ref=dst.at[peer], dst_ref=dst.at[peer], send_sem=send_sem.at[number], recv_sem=recv_sem.at[peer],
                device_id=(lon, peer), device_id_type=MESH).wait_recv()

    def split(src, high_ref, low_ref, step):
        def body(i, carry):
            at = pl.ds(pl.multiple_of(i * step, step), step)
            high_ref[at, :], low_ref[at, :] = halves(src[at, :])
            return carry
        lax.fori_loop(0, src.shape[0] // step, body, 0)

    def split_taps(src, high_ref, low_ref, depth, step):
        for i in range(3):
            def body(n, carry):
                g0, g1, g2 = (src[pl.ds(pl.multiple_of((3 * i + j) * depth + n * step, step), step), :] for j in range(3))
                outer, inner = 0.5 * (g0 + g2), 0.5 * g1
                at = pl.ds(pl.multiple_of(i * depth + n * step, step), step)
                for m, factor in enumerate((g0, outer + inner, outer - inner, g2)):
                    high_ref[m, at, :], low_ref[m, at, :] = halves(factor)
                return carry
            lax.fori_loop(0, depth // step, body, 0)

    def factors(d0, d1, d2, d3):
        return d0 - d2, d1 + d2, d2 - d1, d1 - d3

    def pair_rows(buf, at, length=1):
        def column(d):
            lanes = [buf[h, pl.ds(at, length), pl.ds(SIDE - 2 + d, PAIRS, stride=2), :] for h in range(buf.shape[0])]
            return jnp.concatenate(lanes, axis=2)
        return factors(*[column(d) for d in range(4)])

    def put_rows(high_ref, low_ref, at, pieces):
        for m, piece in enumerate(pieces):
            count_ = piece.shape[0] // 2
            high_ref[m, at:at + count_], low_ref[m, at:at + count_] = halves(
                piece.reshape(count_, 2 * PAIRS, piece.shape[2]))

    def joined(*rows_):
        return [jnp.concatenate(list(x), axis=0) for x in zip(*rows_)]

    def inner_rows(buf, high_ref, low_ref):
        pieces = pair_rows(buf, 2, 8)
        put_rows(high_ref, low_ref, 0, pieces)
        put_rows(high_ref, low_ref, 4, [x[1:7] for x in pieces])

    def pair_sums(taken_hi, taken_lo, weights):
        products = []
        for m in range(4):
            lhs, (wh, wl, dot) = taken_hi(m), weights(m)
            products.append(dot(lhs, wh) + dot(lhs, wl) + dot(taken_lo(m), wh))
        m0, m1, m2, m3 = products
        return m0 + m1 + m2, m1 - m2 - m3

    def taps(ref, chosen):
        def lhs(m):
            rows_ = [jnp.concatenate([ref[m, a:b] for a, b in part], axis=0) for part in chosen]
            return jnp.concatenate([x.reshape(x.shape[0] * x.shape[1], x.shape[2]) for x in rows_], axis=1)
        return lhs

    lat_ext[:, :, 80:88, :] = jnp.zeros((k1 // 128, 12, 8, 128), F32)
    g_ext[:, :, 80:88, :] = jnp.zeros((hid // 128, 12, 8, 128), F32)

    ld_band.wait()
    ld_cell.wait()
    ld_count.wait()
    lane = lax.broadcasted_iota(jnp.int32, (n_lat, 128), 1)
    live = lane < slots

    def blocks(ref):
        row = ref[...]
        return jnp.concatenate([row[:, slots * a:slots * a + 128] for a in range(n_lat)], axis=0)

    bands, cells, counts = blocks(band_v), blocks(cell_v), blocks(count_v)
    below = (lax.broadcasted_iota(jnp.int32, (128, 128), 0) < lax.broadcasted_iota(jnp.int32, (128, 128), 1))
    below = below.astype(F32).astype(BF16)
    mine = jnp.where(live & (bands == lat), 1.0, 0.0)
    pick = jnp.where(mine > 0.0, nn(mine.astype(BF16), below), -1.0)
    cells = ((cells >> 6) << 5) + ((cells & 63) >> 1) + ((cells & 1) << 8)
    cellsf = cells.astype(F32) + 1.0
    countsf = counts.astype(F32) * 0.125
    msg_k = lax.rem(lax.broadcasted_iota(jnp.int32, (MSG, 128), 0), CAP).astype(F32)
    first = lax.broadcasted_iota(jnp.int32, (MSG, 128), 0) < CAP
    taken = n_lat * CAP
    named, merged = [], []
    for q in range(n_lat // 2):
        def two(x):
            return jnp.where(first, x[2 * q:2 * q + 1], x[2 * q + 1:2 * q + 2])
        hit = two(pick) == msg_k
        named.append(jnp.sum(jnp.where(hit, two(cellsf), 0.0), axis=1, keepdims=True))
        merged.append(jnp.sum(jnp.where(hit, two(countsf), 0.0), axis=1, keepdims=True))
    wanted = jnp.concatenate(named, axis=0).astype(jnp.int32) - 1
    weight = jnp.concatenate(merged, axis=0)
    oh[...] = jnp.where(wanted == lax.broadcasted_iota(jnp.int32, (taken, 512), 1), 1.0, 0.0).astype(BF16)

    ld_land.wait()
    column = lax.broadcasted_iota(jnp.int32, (64, 512), 0)
    column = ((column & 31) << 1) + (column >> 5)
    fold = (lax.broadcasted_iota(jnp.int32, (64, 512), 1) >> 3) == column
    fold = jnp.where(fold, 1.0, 0.0).astype(BF16)
    kept = (lax.broadcasted_iota(jnp.int32, (8, 512), 1) & 7) == lax.broadcasted_iota(jnp.int32, (8, 512), 0)
    tiles = []
    for r in range(8):
        strip = land_v[8 * r:8 * r + 8, :].astype(F32)
        spread = jnp.concatenate([jnp.where(kept, strip[p:p + 1], 0.0) for p in range(8)], axis=0)
        tiles.append(nt(fold, spread.astype(BF16)))
    tiles = jnp.concatenate([x[:32] for x in tiles] + [x[32:] for x in tiles], axis=0)
    tiles = jnp.concatenate([tiles, 1.0 - tiles], axis=1).astype(BF16)
    flags = nn(oh[...], tiles)
    lrows = n_lat * LCAP
    row = lax.broadcasted_iota(jnp.int32, (lrows, taken), 0)
    into = (row & (LCAP - 1)) + (row >> 4) * CAP == lax.broadcasted_iota(jnp.int32, (lrows, taken), 1)
    into = into & ((row & (LCAP - 1)) < CAP)
    land_send[...] = nn(jnp.where(into, 1.0, 0.0).astype(BF16), flags.astype(BF16)).reshape(n_lat, LCAP, 128)
    flags_w = (flags * weight).astype(BF16)

    pl.semaphore_wait(barrier, len(around) + len(peers))
    land_sent = exchange(land_send, land_recv, l_send, l_recv)
    ld_lat.wait()
    rim1 = rim(lat_ext, h_send, h_recv, (sides, near_rows, corners, far_rows))

    ld_w1.wait()
    split_taps(w1_v, w1_hi, w1_lo, k1, 64)

    own = lax.broadcasted_iota(jnp.int32, (n_lat, 128), 0) == lat
    own_band = jnp.sum(jnp.where(own, bands, 0), axis=0, keepdims=True)
    own_count = jnp.sum(jnp.where(own, countsf, 0.0), axis=0, keepdims=True)
    theirs = jnp.where(live & (own_band == lax.broadcasted_iota(jnp.int32, (n_lat, 128), 0)), 1.0, 0.0)
    place = jnp.where(theirs > 0.0, nn(theirs.astype(BF16), below), -1.0)
    land_k = lax.broadcasted_iota(jnp.int32, (LCAP, 128), 0).astype(F32)
    pmt[...] = jnp.concatenate(
        [jnp.where(place[b:b + 1] == msg_k, 1.0, 0.0) for b in range(n_lat)], axis=0).astype(BF16)
    pml = jnp.concatenate([jnp.where(place[b:b + 1] == land_k, 1.0, 0.0) for b in range(n_lat)], axis=0)
    from_land[...] = jnp.transpose(pml).astype(BF16)
    own_weight[...] = jnp.transpose(jnp.broadcast_to(own_count, (128, 128)))

    ld_ok.wait()
    ld_err.wait()
    ld_hb.wait()
    ld_w2.wait()
    split_taps(w2_v, w2_hi, w2_lo, hid, 64)
    inv = 1.0 / (err_v[...] * err_v[...])
    inv_hi = inv.astype(BF16).astype(F32)
    inv_mid = (inv - inv_hi).astype(BF16).astype(F32)
    inv_lo = inv - inv_hi - inv_mid
    okf = ok_v[...].astype(F32)
    kind = lax.broadcasted_iota(jnp.int32, (16, variables), 0)
    table = jnp.where(kind == 0, inv_hi, jnp.where(kind == 1, inv_mid, jnp.where(kind == 2, inv_lo, 0.0)))
    table = table + jnp.where(kind == 3, okf[1:2], 0.0) + jnp.where(kind == 4, okf[0:1], 0.0)
    table = table.astype(BF16)
    spans = [(at, min(CHUNK, patch - at)) for at in range(0, patch, CHUNK)]
    for at, size in spans:
        place_ = lax.broadcasted_iota(jnp.int32, (1, size), 1) + at
        pixel = ((place_.astype(F32) + 0.5) * (1.0 / variables)).astype(jnp.int32)
        variable = place_ - pixel * variables
        chosen = lax.broadcasted_iota(jnp.int32, (variables, size), 0) == variable
        spread = nn(table, jnp.where(chosen, 1.0, 0.0).astype(BF16))
        inv_row[:, at:at + size] = spread[0:1] + spread[1:2] + spread[2:3]
        which = lax.broadcasted_iota(jnp.int32, (128, size), 0)
        seen = jnp.where(which == pixel, spread[3:4], jnp.where(which == pixel + 64, spread[4:5], 0.0))
        ok_rows[:, at:at + size] = seen.astype(BF16)
    ld_b1.wait()
    ld_b2.wait()
    ld_value.wait()
    for at, size in spans:
        span = slice(at, at + size)
        shifted = (value_v[:, span] - hb_v[span].reshape(1, size)) * inv_row[:, span]
        val_hi[:, span], val_lo[:, span] = halves(shifted)
    ld_head.wait()
    split(head_v, head_hi, head_lo, 96)

    rim_arrived(lat_ext, h_recv, h_send, (sides,))

    def forward1(m):
        return w1_hi[m], w1_lo[m], nn

    def put1(chosen, groups):
        for parity, summed in enumerate(pair_sums(taps(sa_hi, chosen), taps(sa_lo, chosen), forward1)):
            summed = summed + b1_v[...]
            act = gelu_parts(summed)[0]
            for source, target, length in groups:
                part = slice(source * PAIRS, (source + length) * PAIRS)
                pre1[parity, target:target + length] = summed[part].reshape(length, PAIRS, hid)
                act1[parity, target:target + length] = act[part].reshape(length, PAIRS, hid)

    inner_rows(lat_ext, sa_hi, sa_lo)
    put1((((0, 3),), ((4, 7),), ((1, 4),)), ((0, 2, 6),))
    rim_arrived(lat_ext, h_recv, h_send, (near_rows, corners, far_rows))
    for at, one, other in (
        (7, 1 - north, 2), (8, 9, 10 + south),
        (9, 2 * north, 1 - north), (10, 8, 9 + south),
        (11, 2 - north, 3), (12, 10 + south, 11 - 2 * south),
    ):
        put_rows(sa_hi, sa_lo, at, joined(pair_rows(lat_ext, one), pair_rows(lat_ext, other)))
    put1((((9, 11),), ((7, 9),), ((11, 13),)), ((0, 0, 2), (2, 8, 2)))

    arrived(land_recv, l_send, l_recv)
    flags_own = nn(from_land[...], land_recv[...].reshape(lrows, 128).astype(BF16))
    flags_own = flags_own[:slots].astype(BF16)

    def back(high, low, at, size, total):
        count_ = high.shape[0]
        hh, hl = head_hi[at:at + size, :], head_lo[at:at + size, :]
        both = nn(jnp.concatenate([high, low], axis=0), hh)
        return total + both[:count_] + both[count_:] + nn(high, hl)

    for at, size in spans:
        span = slice(at, at + size)
        seen = nn(flags_own, ok_rows[:, span]).astype(BF16)
        masked[0:slots, span] = val_hi[:, span] * seen
        masked[slots:2 * slots, span] = val_lo[:, span] * seen
    cut = patch // 256 * 128
    shares = jnp.concatenate([own_weight[0:slots, :]] * (hid // 128), axis=1)
    terms = jnp.zeros((slots, hid), F32)
    for a, b in ((0, cut), (cut, patch)):
        both = nn(masked[:, a:b], head_hi[a:b, :])
        terms = terms + (both[:slots] + both[slots:] + nn(masked[0:slots, a:b], head_lo[a:b, :])) * shares
    high, low = halves(terms)
    both = jnp.concatenate([high, low], axis=1)
    if slots < 128:
        both = jnp.concatenate([both, jnp.zeros((128 - slots, 2 * hid), BF16)], axis=0)
    rows = n_lat * MSG
    upper = lax.rem(lax.broadcasted_iota(jnp.int32, (rows, 128), 0), MSG) < CAP
    sent_terms = nn(pmt[...], both)
    sent_terms = sent_terms[:, :hid] + sent_terms[:, hid:]
    term_send[...] = jnp.where(upper, sent_terms[:, :128], sent_terms[:, 128:]).reshape(n_lat, MSG, 128)
    terms_sent = exchange(term_send, term_recv, t_send, t_recv)

    def near(ref, rows_=slice(0, 10)):
        return factors(ref[0, rows_, 0:32], ref[1, rows_, 0:32], ref[0, rows_, 1:33], ref[1, rows_, 1:33])

    for m, piece in enumerate(near(act1)):
        sb_hi[m], sb_lo[m] = halves(piece)

    def forward2(m):
        return w2_hi[m], w2_lo[m], nn

    chosen = tuple(((i, i + 8),) for i in range(3))
    summed = jnp.concatenate(pair_sums(taps(sb_hi, chosen), taps(sb_lo, chosen), forward2), axis=0) + b2_v[...]
    pre2[...] = summed
    act2, _ = gelu_parts(summed)

    high, low = halves(act2)
    cols = nn(oh[...], jnp.concatenate([high, low], axis=1)).astype(BF16)
    cols_hi, cols_lo = cols[:, :hid], cols[:, hid:]
    cols_both = jnp.concatenate([cols_hi, cols_lo], axis=0)
    terms = jnp.zeros((taken, hid), F32)
    for at, size in spans:
        span = slice(at, at + size)
        both = nt(cols_both, head_hi[span, :])
        decoded = both[:taken] + both[taken:] + nt(cols_hi, head_lo[span, :])
        high, low = halves(nn(flags_w, ok_rows[:, span]) * inv_row[:, span] * decoded)
        terms = back(high, low, at, size, terms)

    wanted_row = jnp.transpose(jnp.broadcast_to(wanted.astype(F32), (taken, 128)))[0:1, :].astype(jnp.int32)
    oht[...] = jnp.where(wanted_row == lax.broadcasted_iota(jnp.int32, (512, taken), 0), 1.0, 0.0).astype(BF16)
    named = [jnp.sum(jnp.where(pick[a:a + 1] == msg_k, cellsf[a:a + 1], 0.0), axis=1, keepdims=True)
             for a in range(n_lat)]
    named = jnp.broadcast_to(jnp.concatenate(named, axis=0), (rows, 128))
    wanted_row = jnp.transpose(named)[0:1, :].astype(jnp.int32) - 1
    oht_msg[...] = jnp.where(wanted_row == lax.broadcasted_iota(jnp.int32, (512, rows), 0), 1.0, 0.0).astype(BF16)
    high, low = halves(terms)
    hidden = nn(oht[...], jnp.concatenate([high, low], axis=1))
    hidden = hidden[:, :hid] + hidden[:, hid:]
    pre2[...] = gelu_slope(pre2[...])
    pre1[...] = gelu_slope(pre1[...])
    for copy in rim1 + land_sent:
        copy.wait_send()

    arrived(term_recv, t_send, t_recv)

    came = term_recv[...].reshape(rows, 128)
    came = jnp.concatenate([jnp.where(upper, came, 0.0), jnp.where(upper, 0.0, came)], axis=1)
    high, low = halves(came)
    came = jnp.concatenate([high, low], axis=1)

    def put_grad(groups):
        for first_, last in groups:
            for parity in range(2):
                cells_ = slice(256 * parity + 32 * first_, 256 * parity + 32 * last)
                moved = nn(oht_msg[cells_, :], came)
                grad2 = (hidden[cells_] - moved[:, :hid] - moved[:, hid:]) * pre2[cells_, :]
                for h in range(hid // 128):
                    g_ext[h, 2 + first_:2 + last, pl.ds(SIDE + parity, 32, stride=2), :] = (
                        grad2[:, 128 * h:128 * h + 128].reshape(last - first_, 32, 128))

    put_grad(((0, 2), (6, 8)))
    rim2 = rim(g_ext, g_send, g_recv, (near_rows, corners, far_rows))
    put_grad(((2, 6),))
    rim2 += rim(g_ext, g_send, g_recv, (sides,))
    for copy in terms_sent:
        copy.wait_send()

    rim_arrived(g_ext, g_recv, g_send, (sides,))

    def backward(high_ref, low_ref, depth):
        def weights(m):
            at = (3, 1, 2, 0)[m]
            return tuple(jnp.concatenate([ref[at, i * depth:(i + 1) * depth] for i in range(3)], axis=1)
                         for ref in (high_ref, low_ref)) + (nt,)
        return weights

    def put2(chosen, groups):
        sums = pair_sums(taps(sg_hi, chosen), taps(sg_lo, chosen), backward(w2_hi, w2_lo, hid))
        for parity, grad1 in enumerate(sums):
            for source, target, length in groups:
                part = grad1[source * PAIRS:(source + length) * PAIRS].reshape(length, PAIRS, hid)
                p_ext[parity, target:target + length] = part * pre1[parity, target:target + length]

    def scaled_by(x, factor):
        return [y * factor for y in x]

    def plus(x, y, factor):
        return [u + v * factor for u, v in zip(x, y)]

    def near_pairs(first_, last):
        rows_ = slice(first_, last)
        return factors(p_ext[0, rows_, 0:32], p_ext[1, rows_, 0:32], p_ext[0, rows_, 1:33], p_ext[1, rows_, 1:33])

    def put_pairs(first_, last, at):
        for m, piece in enumerate(near_pairs(first_, last)):
            sp_hi[m, at:at + last - first_], sp_lo[m, at:at + last - first_] = halves(piece)

    def put3(chosen, rows_):
        products = []
        for m in range(4):
            wh, wl, dot = backward(w1_hi, w1_lo, k1)(m)
            both_ = dot(taps(sp_hi, chosen)(m), jnp.concatenate([wh, wl], axis=0))
            products.append(both_[:, :k1] + both_[:, k1:] + dot(taps(sp_lo, chosen)(m), wh))
        m0, m1, m2, m3 = products
        for parity, part in enumerate((m0 + m1 + m2, m1 - m2 - m3)):
            part = part.reshape(part.shape[0] // 32, 32, k1)
            done = 0
            for first_, last in rows_:
                out[first_:last, pl.ds(parity, 32, stride=2), :] = part[done:done + last - first_]
                done += last - first_

    inner_rows(g_ext, sg_hi, sg_lo)
    put2((((1, 4),), ((4, 7),), ((0, 3),)), ((0, 2, 6),))
    put_pairs(2, 8, 2)
    put3((((4, 8),), ((3, 7),), ((2, 6),)), ((2, 6),))
    rim_arrived(g_ext, g_recv, g_send, (near_rows, corners, far_rows))
    r0, r1 = pair_rows(g_ext, north), pair_rows(g_ext, 1 - north)
    r10, r11 = pair_rows(g_ext, 10 + south), pair_rows(g_ext, 11 - south)
    put_rows(sg_hi, sg_lo, 7, joined(r1, pair_rows(g_ext, 2)))
    put_rows(sg_hi, sg_lo, 8, joined(pair_rows(g_ext, 9), r10))
    put_rows(sg_hi, sg_lo, 9, joined(plus(pair_rows(g_ext, 2), r0, northf), plus(pair_rows(g_ext, 3), r1, northf)))
    put_rows(sg_hi, sg_lo, 10, joined(scaled_by(r10, 1.0 - southf), scaled_by(r11, 1.0 - southf)))
    put_rows(sg_hi, sg_lo, 11, joined(scaled_by(r0, 1.0 - northf), scaled_by(r1, 1.0 - northf)))
    put_rows(sg_hi, sg_lo, 12, joined(plus(pair_rows(g_ext, 8), r10, southf), plus(pair_rows(g_ext, 9), r11, southf)))
    put2((((9, 11),), ((7, 9),), ((11, 13),)), ((0, 0, 2), (2, 8, 2)))

    for m, (q0, q1, q2, q7, q8, q9) in enumerate(zip(*[near_pairs(at, at + 1) for at in (0, 1, 2, 7, 8, 9)])):
        for at, piece in ((1, q1), (8, q8), (10, q2 + northf * q0), (11, q9 * (1.0 - southf)),
                          (12, q0 * (1.0 - northf)), (13, q7 + southf * q9)):
            sp_hi[m, at:at + 1], sp_lo[m, at:at + 1] = halves(piece)
    put3((((10, 11), (3, 4), (8, 9), (11, 12)), ((1, 3), (7, 9)), ((12, 13), (1, 2), (6, 7), (13, 14))),
         ((0, 2), (6, 8)))
    for copy in rim2:
        copy.wait_send()


def shards(n_lon, n_lat, latent, conv1_weight, conv1_bias, conv2_weight, conv2_bias, head_weight, head_bias, land_sea,
           var_ok, obs_error, obs_band, obs_cell, obs_count, obs_value):
    lc, hid = conv1_weight.shape[2], conv1_weight.shape[3]
    slots, patch = obs_value.shape[1], obs_value.shape[2]
    variables = var_ok.shape[1]
    listed = n_lat * slots
    padded = -(-(listed + 128) // 128) * 128
    vmem = pltpu.VMEM
    rows = n_lat * MSG
    scratch = [
        vmem((lc // 128, 12, BUF, 128), F32),
        vmem((4, 13, 2 * PAIRS, lc), BF16), vmem((4, 13, 2 * PAIRS, lc), BF16),
        vmem((9 * lc, hid), F32), vmem((4, 3 * lc, hid), BF16), vmem((4, 3 * lc, hid), BF16),
        vmem((9 * hid, hid), F32), vmem((4, 3 * hid, hid), BF16), vmem((4, 3 * hid, hid), BF16),
        vmem((1, hid), F32), vmem((1, hid), F32),
        vmem((2, 10, PAIRS, hid), F32), vmem((2, 10, PAIRS, hid), F32),
        vmem((4, 10, 32, hid), BF16), vmem((4, 10, 32, hid), BF16),
        vmem((512, hid), F32),
        vmem((patch, hid), F32), vmem((patch, hid), BF16), vmem((patch, hid), BF16),
        vmem((patch,), F32), vmem(land_sea.shape, jnp.int32), vmem(var_ok.shape, jnp.int32),
        vmem((1, variables), F32),
        vmem((1, padded), jnp.int32), vmem((1, padded), jnp.int32), vmem((1, padded), jnp.int32),
        vmem((slots, patch), F32), vmem((slots, patch), BF16), vmem((slots, patch), BF16),
        vmem((2 * slots, patch), BF16),
        vmem((128, patch), BF16), vmem((1, patch), F32),
        vmem((n_lat * CAP, 512), BF16), vmem((512, n_lat * CAP), BF16), vmem((512, rows), BF16),
        vmem((rows, 128), BF16),
        vmem((128, n_lat * LCAP), BF16), vmem((128, 128), F32),
        vmem((n_lat, LCAP, 128), F32), vmem((n_lat, LCAP, 128), F32),
        vmem((n_lat, MSG, 128), F32), vmem((n_lat, MSG, 128), F32),
        vmem((hid // 128, 12, BUF, 128), F32),
        vmem((4, 13, 2 * PAIRS, hid), BF16), vmem((4, 13, 2 * PAIRS, hid), BF16),
        vmem((2, 10, PAIRS, hid), F32),
        vmem((4, 14, 32, hid), BF16), vmem((4, 14, 32, hid), BF16),
        pltpu.SemaphoreType.DMA((14,)),
        pltpu.SemaphoreType.DMA((10,)), pltpu.SemaphoreType.DMA((18,)),
        pltpu.SemaphoreType.DMA((10,)), pltpu.SemaphoreType.DMA((18,)),
    ] + [pltpu.SemaphoreType.DMA((n_lat,))] * 4
    return pl.pallas_call(
        functools.partial(kernel, n_lon, n_lat, slots, patch, variables),
        out_shape=jax.ShapeDtypeStruct(latent.shape, F32),
        in_specs=[pl.BlockSpec(memory_space=pl.ANY)] * 14,
        out_specs=pl.BlockSpec(memory_space=pltpu.VMEM),
        scratch_shapes=scratch,
        compiler_params=pltpu.CompilerParams(
            collective_id=0, has_side_effects=True, vmem_limit_bytes=48 * 1024 * 1024),
    )(*(pltpu.with_memory_space_constraint(x, pltpu.HBM) for x in (
        latent, conv1_weight.reshape(9 * lc, hid), conv1_bias.reshape(1, hid), conv2_weight.reshape(9 * hid, hid),
      conv2_bias.reshape(1, hid), head_weight.T, head_bias, land_sea, var_ok,
      obs_error.reshape(1, variables), obs_band.reshape(1, listed), obs_cell, obs_count, obs_value[0])))


def solution(mesh):
    in_specs = (
        P("lat", "lon", None),
        P(),
        P(),
        P(),
        P(),
        P(),
        P(),
        P("lat", "lon"),
        P(),
        P(),
        P("lon", None, None),
        P("lon", None),
        P("lon", None),
        P("lon", "lat", None),
    )
    out_specs = P("lat", "lon", None)
    body = functools.partial(shards, mesh.shape["lon"], mesh.shape["lat"])
    return jax.shard_map(body, mesh=mesh, in_specs=in_specs, out_specs=out_specs, check_vma=False)
```

```python
import functools

import jax
import jax.numpy as jnp
from jax import lax
from jax.experimental import pallas as pl
from jax.experimental.pallas import tpu as pltpu
from jax.sharding import PartitionSpec as P

F32 = jnp.float32
BF16 = jnp.bfloat16
CAP = 12
MSG = 2 * CAP
LCAP = 16
SIDE = 8
PAIRS = 40
BUF = 88
CHUNK = 512
MESH = pl.DeviceIdType.MESH


def halves(x):
    high = x.astype(BF16)
    return high, (x - high.astype(F32)).astype(BF16)


def nn(a, b):
    return lax.dot_general(a, b, (((1,), (0,)), ((), ())), preferred_element_type=F32)


def nt(a, b):
    return lax.dot_general(a, b, (((1,), (1,)), ((), ())), preferred_element_type=F32)


def gelu_parts(x):
    c = 0.7978845608028654
    t = jnp.tanh(c * (x + 0.044715 * x * x * x))
    return 0.5 * x * (1.0 + t), t


def gelu_slope(x):
    c = 0.7978845608028654
    t = jnp.tanh(c * (x + 0.044715 * x * x * x))
    return 0.5 * (1.0 + t) + 0.5 * x * (1.0 - t * t) * (c * (1.0 + 3.0 * 0.044715 * x * x))


def kernel(
    n_lon, n_lat, slots, patch, variables,
    latent, w1, b1, w2, b2, head, hbias, land, ok, err, band, cell, count, value,
    out,
    lat_ext, sa_hi, sa_lo, w1_v, w1_hi, w1_lo, w2_v, w2_hi, w2_lo, b1_v, b2_v,
    pre1, act1, sb_hi, sb_lo, pre2, head_v, head_hi, head_lo, hb_v, land_v, ok_v, err_v,
    band_v, cell_v, count_v, value_v, val_hi, val_lo, masked, ok_rows, inv_row,
    oh, oht, oht_msg, pmt, from_land, own_weight, land_send, land_recv, term_send, term_recv,
    g_ext, side_send, side_recv, corner_send, corner_recv, sg_hi, sg_lo, p_ext, sp_hi, sp_lo,
    load_sem, h_send, h_recv, g_send, g_recv, l_send, l_recv, t_send, t_recv,
):
    lon, lat = lax.axis_index("lon"), lax.axis_index("lat")
    north = 1 - lax.div(lat + n_lat - 1, n_lat)
    south = lax.div(lat + 1, n_lat)
    northf, southf = north.astype(F32), south.astype(F32)
    hid = w1_v.shape[1]
    k1 = latent.shape[2]

    loads = [
        (band, band_v.at[:, 0:n_lat * slots]),
        (cell, cell_v.at[:, 0:n_lat * slots]),
        (count, count_v.at[:, 0:n_lat * slots]),
        (land, land_v),
        (latent, lat_ext.at[0, 2:10, SIDE:SIDE + 64, :]),
        (w1, w1_v),
        (b1, b1_v),
        (ok, ok_v),
        (err, err_v),
        (hbias, hb_v),
        (w2, w2_v),
        (b2, b2_v),
        (value, value_v),
        (head, head_v),
    ]
    copies = [pltpu.make_async_copy(s, d, load_sem.at[i]) for i, (s, d) in enumerate(loads)]
    (ld_band, ld_cell, ld_count, ld_land, ld_lat, ld_w1, ld_b1, ld_ok, ld_err, ld_hb, ld_w2, ld_b2, ld_value,
     ld_head) = copies
    for copy in copies[:5]:
        copy.start()

    half = n_lon // 2
    up_lat, down_lat = lat - 1 + north, lat + 1 - south
    around = []
    for dr in (-1, 0, 1):
        for dc in (-1, 0, 1):
            if dr == 0 and dc == 0:
                continue
            turn = half * north if dr < 0 else half * south if dr > 0 else 0
            to_lon = lax.rem(lon + dc + turn + n_lon, n_lon)
            to_lat = up_lat if dr < 0 else down_lat if dr > 0 else lat
            around.append((dr, dc, (to_lon, to_lat)))

    deep = n_lat // 2
    steps = [(far, step) for far in range(2) for step in range(deep) if far or step]
    steps.sort(key=lambda s: -(2 * s[0] + min(s[1], deep - s[1])))
    peers = [lax.rem(lax.div(lat, deep) + far, 2) * deep + lax.rem(lax.rem(lat, deep) + step, deep)
             for far, step in steps]

    barrier = pltpu.get_barrier_semaphore()
    for peer in peers:
        pl.semaphore_signal(barrier, inc=1, device_id=(lon, peer), device_id_type=MESH)
    for _, _, device in around:
        pl.semaphore_signal(barrier, inc=1, device_id=device, device_id_type=MESH)
    for copy in copies[5:]:
        copy.start()

    near_rows, far_rows, corners, sides = range(4)
    parts = []
    for dr, dc, device in around:
        if dr and not dc:
            parts += [(near_rows, dr, dc, device), (far_rows, dr, dc, device)]
        else:
            parts.append((corners if dr else sides, dr, dc, device))

    def rim(buf, send_sem, recv_sem, kinds):
        sent = []
        for kind in kinds:
            for number, (its, dr, dc, device) in enumerate(parts):
                if its != kind:
                    continue
                src_c = (SIDE, SIDE) if dc < 0 else (SIDE + 56, SIDE) if dc > 0 else (SIDE, 64)
                dst_c = 72 if dc < 0 else 0 if dc > 0 else SIDE
                second = 1 if kind == far_rows else 0
                if dr < 0:
                    src_r, dst_r, side = 2 + second, 10 - 10 * north + second, 2 - 2 * north
                elif dr > 0:
                    src_r, dst_r, side = 9 - second, 1 + 10 * south - second, 2 * south
                else:
                    src_r, dst_r, side = 2, 2, 1
                length = 8 if kind == sides else 1
                if kind == corners:
                    length = 2
                    if dr > 0:
                        src_r, dst_r = 8, 10 * south
                slot = 9 * second + side * 3 + (1 - dc)
                src = buf.at[:, pl.ds(src_r, length), pl.ds(src_c[0], src_c[1]), :]
                dst = buf.at[:, pl.ds(dst_r, length), pl.ds(dst_c, src_c[1]), :]
                copy = pltpu.make_async_remote_copy(
                    src_ref=src, dst_ref=dst, send_sem=send_sem.at[number], recv_sem=recv_sem.at[slot],
                    device_id=device, device_id_type=MESH)
                copy.start()
                sent.append(copy)
        return sent

    def rim_arrived(buf, recv_sem, send_sem, kinds, drs=(-1, 0, 1)):
        for number, (kind, dr, dc, device) in enumerate(parts):
            if kind not in kinds or dr not in drs:
                continue
            cols_ = (0, SIDE) if dc < 0 else (72, SIDE) if dc > 0 else (SIDE, 64)
            second = 1 if kind == far_rows else 0
            if kind == sides:
                at, length = 2, 8
            elif kind == corners:
                at, length = (0 if dr < 0 else 10), 2
            else:
                at, length = (1 - north if dr < 0 else 10 + south), 1
                if second:
                    at = north if dr < 0 else 11 - south
            ref = buf.at[:, pl.ds(at, length), pl.ds(cols_[0], cols_[1]), :]
            slot = 9 * second + (dr + 1) * 3 + dc + 1
            pltpu.make_async_remote_copy(
                src_ref=ref, dst_ref=ref, send_sem=send_sem.at[number], recv_sem=recv_sem.at[slot],
                device_id=device, device_id_type=MESH).wait_recv()

    def last_columns(dc):
        return SIDE if dc < 0 else SIDE + 62

    def halo_columns(dc):
        return SIDE - 2 if dc < 0 else 72

    def packed_rim(kind, send_sem, recv_sem):
        sent = []
        for number, (its, dr, dc, device) in enumerate(parts):
            if its != kind:
                continue
            at = last_columns(dc)
            if kind == sides:
                mine_, theirs_, ref, into_ref = (dc + 1) // 2, (1 - dc) // 2, side_send, side_recv
                for h in range(hid // 128):
                    for j in range(2):
                        ref[mine_, h, 8 * j:8 * j + 8, :] = g_ext[h, 2:10, at + j:at + j + 1, :].reshape(8, 128)
                slot = 3 + (1 - dc)
            else:
                side = 2 - 2 * north if dr < 0 else 2 * south
                mine_, theirs_, ref, into_ref = dr + 1 + (dc + 1) // 2, side + (1 - dc) // 2, corner_send, corner_recv
                for h in range(hid // 128):
                    for r in range(2):
                        row_ = (2 if dr < 0 else 8) + r
                        ref[mine_, h, 2 * r:2 * r + 2, :] = g_ext[h, row_, at:at + 2, :]
                slot = side * 3 + (1 - dc)
            copy = pltpu.make_async_remote_copy(
                src_ref=ref.at[mine_], dst_ref=into_ref.at[theirs_], send_sem=send_sem.at[number],
                recv_sem=recv_sem.at[slot], device_id=device, device_id_type=MESH)
            copy.start()
            sent.append(copy)
        return sent

    def packed_arrived(kind, its_dr, send_sem, recv_sem):
        for number, (its, dr, dc, device) in enumerate(parts):
            if its != kind or dr != its_dr:
                continue
            at, slot = halo_columns(dc), (dr + 1) * 3 + dc + 1
            mine_ = (dc + 1) // 2 if kind == sides else dr + 1 + (dc + 1) // 2
            ref = side_recv if kind == sides else corner_recv
            pltpu.make_async_remote_copy(
                src_ref=ref.at[mine_], dst_ref=ref.at[mine_], send_sem=send_sem.at[number],
                recv_sem=recv_sem.at[slot], device_id=device, device_id_type=MESH).wait_recv()
            for h in range(hid // 128):
                for j in range(2):
                    if kind == sides:
                        g_ext[h, 2:10, at + j:at + j + 1, :] = ref[mine_, h, 8 * j:8 * j + 8, :].reshape(8, 1, 128)
                    else:
                        g_ext[h, (0 if dr < 0 else 10) + j, at:at + 2, :] = ref[mine_, h, 2 * j:2 * j + 2, :]

    def exchange(src, dst, send_sem, recv_sem):
        sent = []
        for number, peer in enumerate(peers):
            copy = pltpu.make_async_remote_copy(
                src_ref=src.at[peer], dst_ref=dst.at[lat], send_sem=send_sem.at[number], recv_sem=recv_sem.at[lat],
                device_id=(lon, peer), device_id_type=MESH)
            copy.start()
            sent.append(copy)
        dst[pl.ds(lat, 1)] = src[pl.ds(lat, 1)]
        return sent

    def arrived(dst, send_sem, recv_sem):
        for number, peer in enumerate(peers):
            pltpu.make_async_remote_copy(
                src_ref=dst.at[peer], dst_ref=dst.at[peer], send_sem=send_sem.at[number], recv_sem=recv_sem.at[peer],
                device_id=(lon, peer), device_id_type=MESH).wait_recv()

    def split(src, high_ref, low_ref, step):
        def body(i, carry):
            at = pl.ds(pl.multiple_of(i * step, step), step)
            high_ref[at, :], low_ref[at, :] = halves(src[at, :])
            return carry
        lax.fori_loop(0, src.shape[0] // step, body, 0)

    def split_taps(src, high_ref, low_ref, depth, step):
        for i in range(3):
            def body(n, carry):
                g0, g1, g2 = (src[pl.ds(pl.multiple_of((3 * i + j) * depth + n * step, step), step), :] for j in range(3))
                outer, inner = 0.5 * (g0 + g2), 0.5 * g1
                at = pl.ds(pl.multiple_of(i * depth + n * step, step), step)
                for m, factor in enumerate((g0, outer + inner, outer - inner, g2)):
                    high_ref[m, at, :], low_ref[m, at, :] = halves(factor)
                return carry
            lax.fori_loop(0, depth // step, body, 0)

    def factors(d0, d1, d2, d3):
        return d0 - d2, d1 + d2, d2 - d1, d1 - d3

    def pair_rows(buf, at, length=1):
        def column(d):
            lanes = [buf[h, pl.ds(at, length), pl.ds(SIDE - 2 + d, PAIRS, stride=2), :] for h in range(buf.shape[0])]
            return jnp.concatenate(lanes, axis=2)
        return factors(*[column(d) for d in range(4)])

    def put_rows(high_ref, low_ref, at, pieces):
        for m, piece in enumerate(pieces):
            count_ = piece.shape[0] // 2
            high_ref[m, at:at + count_], low_ref[m, at:at + count_] = halves(
                piece.reshape(count_, 2 * PAIRS, piece.shape[2]))

    def joined(*rows_):
        return [jnp.concatenate(list(x), axis=0) for x in zip(*rows_)]

    def inner_rows(buf, high_ref, low_ref):
        pieces = pair_rows(buf, 2, 8)
        put_rows(high_ref, low_ref, 0, pieces)
        put_rows(high_ref, low_ref, 4, [x[1:7] for x in pieces])

    def pair_sums(taken_hi, taken_lo, weights, stacked=False):
        products = []
        for m in range(4):
            lhs, (wh, wl, dot) = taken_hi(m), weights(m)
            if stacked:
                both_ = dot(jnp.concatenate([lhs, taken_lo(m)], axis=0), wh)
                products.append(both_[:lhs.shape[0]] + both_[lhs.shape[0]:] + dot(lhs, wl))
            else:
                products.append(dot(lhs, wh) + dot(lhs, wl) + dot(taken_lo(m), wh))
        m0, m1, m2, m3 = products
        return m0 + m1 + m2, m1 - m2 - m3

    def taps(ref, chosen):
        def lhs(m):
            rows_ = [jnp.concatenate([ref[m, a:b] for a, b in part], axis=0) for part in chosen]
            return jnp.concatenate([x.reshape(x.shape[0] * x.shape[1], x.shape[2]) for x in rows_], axis=1)
        return lhs

    lat_ext[:, :, 80:88, :] = jnp.zeros((k1 // 128, 12, 8, 128), F32)
    g_ext[:, :, 72:88, :] = jnp.zeros((hid // 128, 12, 16, 128), F32)

    ld_band.wait()
    ld_cell.wait()
    ld_count.wait()
    lane = lax.broadcasted_iota(jnp.int32, (n_lat, 128), 1)
    live = lane < slots

    def blocks(ref):
        row = ref[...]
        return jnp.concatenate([row[:, slots * a:slots * a + 128] for a in range(n_lat)], axis=0)

    bands, cells, counts = blocks(band_v), blocks(cell_v), blocks(count_v)
    below = (lax.broadcasted_iota(jnp.int32, (128, 128), 0) < lax.broadcasted_iota(jnp.int32, (128, 128), 1))
    below = below.astype(F32).astype(BF16)
    mine = jnp.where(live & (bands == lat), 1.0, 0.0)
    pick = jnp.where(mine > 0.0, nn(mine.astype(BF16), below), -1.0)
    cells = ((cells >> 6) << 5) + ((cells & 63) >> 1) + ((cells & 1) << 8)
    cellsf = cells.astype(F32) + 1.0
    countsf = counts.astype(F32) * 0.125
    msg_k = lax.rem(lax.broadcasted_iota(jnp.int32, (MSG, 128), 0), CAP).astype(F32)
    first = lax.broadcasted_iota(jnp.int32, (MSG, 128), 0) < CAP
    taken = n_lat * CAP
    named, merged = [], []
    for q in range(n_lat // 2):
        def two(x):
            return jnp.where(first, x[2 * q:2 * q + 1], x[2 * q + 1:2 * q + 2])
        hit = two(pick) == msg_k
        named.append(jnp.sum(jnp.where(hit, two(cellsf), 0.0), axis=1, keepdims=True))
        merged.append(jnp.sum(jnp.where(hit, two(countsf), 0.0), axis=1, keepdims=True))
    wanted = jnp.concatenate(named, axis=0).astype(jnp.int32) - 1
    weight = jnp.concatenate(merged, axis=0)
    oh[...] = jnp.where(wanted == lax.broadcasted_iota(jnp.int32, (taken, 512), 1), 1.0, 0.0).astype(BF16)

    ld_land.wait()
    column = lax.broadcasted_iota(jnp.int32, (64, 512), 0)
    column = ((column & 31) << 1) + (column >> 5)
    fold = (lax.broadcasted_iota(jnp.int32, (64, 512), 1) >> 3) == column
    fold = jnp.where(fold, 1.0, 0.0).astype(BF16)
    kept = (lax.broadcasted_iota(jnp.int32, (8, 512), 1) & 7) == lax.broadcasted_iota(jnp.int32, (8, 512), 0)
    tiles = []
    for r in range(8):
        strip = land_v[8 * r:8 * r + 8, :].astype(F32)
        spread = jnp.concatenate([jnp.where(kept, strip[p:p + 1], 0.0) for p in range(8)], axis=0)
        tiles.append(nt(fold, spread.astype(BF16)))
    tiles = jnp.concatenate([x[:32] for x in tiles] + [x[32:] for x in tiles], axis=0)
    tiles = jnp.concatenate([tiles, 1.0 - tiles], axis=1).astype(BF16)
    flags = nn(oh[...], tiles)
    lrows = n_lat * LCAP
    row = lax.broadcasted_iota(jnp.int32, (lrows, taken), 0)
    into = (row & (LCAP - 1)) + (row >> 4) * CAP == lax.broadcasted_iota(jnp.int32, (lrows, taken), 1)
    into = into & ((row & (LCAP - 1)) < CAP)
    land_send[...] = nn(jnp.where(into, 1.0, 0.0).astype(BF16), flags.astype(BF16)).reshape(n_lat, LCAP, 128)
    flags_w = (flags * weight).astype(BF16)

    pl.semaphore_wait(barrier, len(around) + len(peers))
    land_sent = exchange(land_send, land_recv, l_send, l_recv)
    ld_lat.wait()
    rim1 = rim(lat_ext, h_send, h_recv, (sides, near_rows, corners, far_rows))

    ld_w1.wait()
    split_taps(w1_v, w1_hi, w1_lo, k1, 64)

    own = lax.broadcasted_iota(jnp.int32, (n_lat, 128), 0) == lat
    own_band = jnp.sum(jnp.where(own, bands, 0), axis=0, keepdims=True)
    own_count = jnp.sum(jnp.where(own, countsf, 0.0), axis=0, keepdims=True)
    theirs = jnp.where(live & (own_band == lax.broadcasted_iota(jnp.int32, (n_lat, 128), 0)), 1.0, 0.0)
    place = jnp.where(theirs > 0.0, nn(theirs.astype(BF16), below), -1.0)
    land_k = lax.broadcasted_iota(jnp.int32, (LCAP, 128), 0).astype(F32)
    pmt[...] = jnp.concatenate(
        [jnp.where(place[b:b + 1] == msg_k, 1.0, 0.0) for b in range(n_lat)], axis=0).astype(BF16)
    pml = jnp.concatenate([jnp.where(place[b:b + 1] == land_k, 1.0, 0.0) for b in range(n_lat)], axis=0)
    from_land[...] = jnp.transpose(pml).astype(BF16)
    own_weight[...] = jnp.transpose(jnp.broadcast_to(own_count, (128, 128)))

    ld_ok.wait()
    ld_err.wait()
    ld_hb.wait()
    ld_w2.wait()
    split_taps(w2_v, w2_hi, w2_lo, hid, 64)
    inv = 1.0 / (err_v[...] * err_v[...])
    inv_hi = inv.astype(BF16).astype(F32)
    inv_mid = (inv - inv_hi).astype(BF16).astype(F32)
    inv_lo = inv - inv_hi - inv_mid
    okf = ok_v[...].astype(F32)
    kind = lax.broadcasted_iota(jnp.int32, (16, variables), 0)
    table = jnp.where(kind == 0, inv_hi, jnp.where(kind == 1, inv_mid, jnp.where(kind == 2, inv_lo, 0.0)))
    table = table + jnp.where(kind == 3, okf[1:2], 0.0) + jnp.where(kind == 4, okf[0:1], 0.0)
    table = table.astype(BF16)
    spans = [(at, min(CHUNK, patch - at)) for at in range(0, patch, CHUNK)]
    for at, size in spans:
        place_ = lax.broadcasted_iota(jnp.int32, (1, size), 1) + at
        pixel = ((place_.astype(F32) + 0.5) * (1.0 / variables)).astype(jnp.int32)
        variable = place_ - pixel * variables
        chosen = lax.broadcasted_iota(jnp.int32, (variables, size), 0) == variable
        spread = nn(table, jnp.where(chosen, 1.0, 0.0).astype(BF16))
        inv_row[:, at:at + size] = spread[0:1] + spread[1:2] + spread[2:3]
        which = lax.broadcasted_iota(jnp.int32, (128, size), 0)
        seen = jnp.where(which == pixel, spread[3:4], jnp.where(which == pixel + 64, spread[4:5], 0.0))
        ok_rows[:, at:at + size] = seen.astype(BF16)
    ld_b1.wait()
    ld_b2.wait()
    ld_value.wait()
    for at, size in spans:
        span = slice(at, at + size)
        shifted = (value_v[:, span] - hb_v[span].reshape(1, size)) * inv_row[:, span]
        val_hi[:, span], val_lo[:, span] = halves(shifted)
    ld_head.wait()
    split(head_v, head_hi, head_lo, 96)

    rim_arrived(lat_ext, h_recv, h_send, (sides,))

    def forward1(m):
        return w1_hi[m], w1_lo[m], nn

    def put1(chosen, groups):
        for parity, summed in enumerate(pair_sums(taps(sa_hi, chosen), taps(sa_lo, chosen), forward1)):
            summed = summed + b1_v[...]
            act = gelu_parts(summed)[0]
            for source, target, length in groups:
                part = slice(source * PAIRS, (source + length) * PAIRS)
                pre1[parity, target:target + length] = summed[part].reshape(length, PAIRS, hid)
                act1[parity, target:target + length] = act[part].reshape(length, PAIRS, hid)

    inner_rows(lat_ext, sa_hi, sa_lo)
    put1((((0, 3),), ((4, 7),), ((1, 4),)), ((0, 2, 6),))

    arrived(land_recv, l_send, l_recv)
    flags_own = nn(from_land[...], land_recv[...].reshape(lrows, 128).astype(BF16))
    flags_own = flags_own[:slots].astype(BF16)

    def back(high, low, at, size, total):
        count_ = high.shape[0]
        hh, hl = head_hi[at:at + size, :], head_lo[at:at + size, :]
        both = nn(jnp.concatenate([high, low], axis=0), hh)
        return total + both[:count_] + both[count_:] + nn(high, hl)

    for at, size in spans:
        span = slice(at, at + size)
        seen = nn(flags_own, ok_rows[:, span]).astype(BF16)
        masked[0:slots, span] = val_hi[:, span] * seen
        masked[slots:2 * slots, span] = val_lo[:, span] * seen
    cut = patch // 256 * 128
    shares = jnp.concatenate([own_weight[0:slots, :]] * (hid // 128), axis=1)
    terms = jnp.zeros((slots, hid), F32)
    for a, b in ((0, cut), (cut, patch)):
        both = nn(masked[:, a:b], head_hi[a:b, :])
        terms = terms + (both[:slots] + both[slots:] + nn(masked[0:slots, a:b], head_lo[a:b, :])) * shares
    high, low = halves(terms)
    both = jnp.concatenate([high, low], axis=1)
    if slots < 128:
        both = jnp.concatenate([both, jnp.zeros((128 - slots, 2 * hid), BF16)], axis=0)
    rows = n_lat * MSG
    upper = lax.rem(lax.broadcasted_iota(jnp.int32, (rows, 128), 0), MSG) < CAP
    sent_terms = nn(pmt[...], both)
    sent_terms = sent_terms[:, :hid] + sent_terms[:, hid:]
    term_send[...] = jnp.where(upper, sent_terms[:, :128], sent_terms[:, 128:]).reshape(n_lat, MSG, 128)
    terms_sent = exchange(term_send, term_recv, t_send, t_recv)

    rim_arrived(lat_ext, h_recv, h_send, (near_rows, corners, far_rows))
    for at, one, other in (
        (7, 1 - north, 2), (8, 9, 10 + south),
        (9, 2 * north, 1 - north), (10, 8, 9 + south),
        (11, 2 - north, 3), (12, 10 + south, 11 - 2 * south),
    ):
        put_rows(sa_hi, sa_lo, at, joined(pair_rows(lat_ext, one), pair_rows(lat_ext, other)))
    put1((((9, 11),), ((7, 9),), ((11, 13),)), ((0, 0, 2), (2, 8, 2)))

    def near(ref, rows_=slice(0, 10)):
        return factors(ref[0, rows_, 0:32], ref[1, rows_, 0:32], ref[0, rows_, 1:33], ref[1, rows_, 1:33])

    for m, piece in enumerate(near(act1)):
        sb_hi[m], sb_lo[m] = halves(piece)

    def forward2(m):
        return w2_hi[m], w2_lo[m], nn

    chosen = tuple(((i, i + 8),) for i in range(3))
    summed = jnp.concatenate(pair_sums(taps(sb_hi, chosen), taps(sb_lo, chosen), forward2), axis=0) + b2_v[...]
    pre2[...] = summed
    act2, _ = gelu_parts(summed)

    high, low = halves(act2)
    cols = nn(oh[...], jnp.concatenate([high, low], axis=1)).astype(BF16)
    cols_hi, cols_lo = cols[:, :hid], cols[:, hid:]
    cols_both = jnp.concatenate([cols_hi, cols_lo], axis=0)
    terms = jnp.zeros((taken, hid), F32)
    for at, size in spans:
        span = slice(at, at + size)
        both = nt(cols_both, head_hi[span, :])
        decoded = both[:taken] + both[taken:] + nt(cols_hi, head_lo[span, :])
        high, low = halves(nn(flags_w, ok_rows[:, span]) * inv_row[:, span] * decoded)
        terms = back(high, low, at, size, terms)

    wanted_row = jnp.transpose(jnp.broadcast_to(wanted.astype(F32), (taken, 128)))[0:1, :].astype(jnp.int32)
    oht[...] = jnp.where(wanted_row == lax.broadcasted_iota(jnp.int32, (512, taken), 0), 1.0, 0.0).astype(BF16)
    named = [jnp.sum(jnp.where(pick[a:a + 1] == msg_k, cellsf[a:a + 1], 0.0), axis=1, keepdims=True)
             for a in range(n_lat)]
    named = jnp.broadcast_to(jnp.concatenate(named, axis=0), (rows, 128))
    wanted_row = jnp.transpose(named)[0:1, :].astype(jnp.int32) - 1
    oht_msg[...] = jnp.where(wanted_row == lax.broadcasted_iota(jnp.int32, (512, rows), 0), 1.0, 0.0).astype(BF16)
    high, low = halves(terms)
    hidden = nn(oht[...], jnp.concatenate([high, low], axis=1))
    hidden = hidden[:, :hid] + hidden[:, hid:]
    pre2[...] = gelu_slope(pre2[...])
    pre1[...] = gelu_slope(pre1[...])
    for copy in rim1 + land_sent:
        copy.wait_send()

    arrived(term_recv, t_send, t_recv)

    came = term_recv[...].reshape(rows, 128)
    came = jnp.concatenate([jnp.where(upper, came, 0.0), jnp.where(upper, 0.0, came)], axis=1)
    high, low = halves(came)
    came = jnp.concatenate([high, low], axis=1)

    def put_grad(groups):
        for first_, last in groups:
            for parity in range(2):
                cells_ = slice(256 * parity + 32 * first_, 256 * parity + 32 * last)
                moved = nn(oht_msg[cells_, :], came)
                grad2 = (hidden[cells_] - moved[:, :hid] - moved[:, hid:]) * pre2[cells_, :]
                for h in range(hid // 128):
                    g_ext[h, 2 + first_:2 + last, pl.ds(SIDE + parity, 32, stride=2), :] = (
                        grad2[:, 128 * h:128 * h + 128].reshape(last - first_, 32, 128))

    put_grad(((0, 2), (6, 8)))
    rim2 = rim(g_ext, g_send, g_recv, (near_rows, far_rows))
    rim2 += packed_rim(corners, g_send, g_recv)
    put_grad(((2, 6),))
    rim2 += packed_rim(sides, g_send, g_recv)
    for copy in terms_sent:
        copy.wait_send()

    packed_arrived(sides, 0, g_send, g_recv)

    def backward(high_ref, low_ref, depth):
        def weights(m):
            at = (3, 1, 2, 0)[m]
            return tuple(jnp.concatenate([ref[at, i * depth:(i + 1) * depth] for i in range(3)], axis=1)
                         for ref in (high_ref, low_ref)) + (nt,)
        return weights

    def put2(chosen, groups, stacked=False):
        sums = pair_sums(taps(sg_hi, chosen), taps(sg_lo, chosen), backward(w2_hi, w2_lo, hid), stacked)
        for parity, grad1 in enumerate(sums):
            for source, target, length in groups:
                part = grad1[source * PAIRS:(source + length) * PAIRS].reshape(length, PAIRS, hid)
                p_ext[parity, target:target + length] = part * pre1[parity, target:target + length]

    def scaled_by(x, factor):
        return [y * factor for y in x]

    def plus(x, y, factor):
        return [u + v * factor for u, v in zip(x, y)]

    def near_pairs(first_, last):
        rows_ = slice(first_, last)
        return factors(p_ext[0, rows_, 0:32], p_ext[1, rows_, 0:32], p_ext[0, rows_, 1:33], p_ext[1, rows_, 1:33])

    def put_pairs(first_, last, at):
        for m, piece in enumerate(near_pairs(first_, last)):
            sp_hi[m, at:at + last - first_], sp_lo[m, at:at + last - first_] = halves(piece)

    def put3(chosen, rows_):
        products = []
        for m in range(4):
            wh, wl, dot = backward(w1_hi, w1_lo, k1)(m)
            lhs = taps(sp_hi, chosen)(m)
            count_ = lhs.shape[0]
            both_ = dot(jnp.concatenate([lhs, taps(sp_lo, chosen)(m)], axis=0), jnp.concatenate([wh, wl], axis=0))
            products.append(both_[:count_, :k1] + both_[:count_, k1:] + both_[count_:, :k1])
        m0, m1, m2, m3 = products
        for parity, part in enumerate((m0 + m1 + m2, m1 - m2 - m3)):
            part = part.reshape(part.shape[0] // 32, 32, k1)
            done = 0
            for first_, last in rows_:
                out[first_:last, pl.ds(parity, 32, stride=2), :] = part[done:done + last - first_]
                done += last - first_

    inner_rows(g_ext, sg_hi, sg_lo)
    put2((((1, 4),), ((4, 7),), ((0, 3),)), ((0, 2, 6),))
    put_pairs(2, 8, 2)
    put3((((4, 8),), ((3, 7),), ((2, 6),)), ((2, 6),))
    rim_arrived(g_ext, g_recv, g_send, (near_rows, far_rows), (1,))
    packed_arrived(corners, 1, g_send, g_recv)
    r10, r11 = pair_rows(g_ext, 10 + south), pair_rows(g_ext, 11 - south)
    put_rows(sg_hi, sg_lo, 8, joined(pair_rows(g_ext, 9), r10))
    put_rows(sg_hi, sg_lo, 10, joined(scaled_by(r10, 1.0 - southf), scaled_by(r11, 1.0 - southf)))
    put_rows(sg_hi, sg_lo, 12, joined(plus(pair_rows(g_ext, 8), r10, southf), plus(pair_rows(g_ext, 9), r11, southf)))
    put2((((10, 11),), ((8, 9),), ((12, 13),)), ((0, 8, 2),), True)
    for m, (q7, q8, q9) in enumerate(zip(*[near_pairs(at, at + 1) for at in (7, 8, 9)])):
        for at, piece in ((8, q8), (11, q9 * (1.0 - southf)), (13, q7 + southf * q9)):
            sp_hi[m, at:at + 1], sp_lo[m, at:at + 1] = halves(piece)
    put3((((8, 9), (11, 12)), ((7, 9),), ((6, 7), (13, 14))), ((6, 8),))

    rim_arrived(g_ext, g_recv, g_send, (near_rows, far_rows), (-1,))
    packed_arrived(corners, -1, g_send, g_recv)
    r0, r1 = pair_rows(g_ext, north), pair_rows(g_ext, 1 - north)
    put_rows(sg_hi, sg_lo, 7, joined(r1, pair_rows(g_ext, 2)))
    put_rows(sg_hi, sg_lo, 9, joined(plus(pair_rows(g_ext, 2), r0, northf), plus(pair_rows(g_ext, 3), r1, northf)))
    put_rows(sg_hi, sg_lo, 11, joined(scaled_by(r0, 1.0 - northf), scaled_by(r1, 1.0 - northf)))
    put2((((9, 10),), ((7, 8),), ((11, 12),)), ((0, 0, 2),), True)
    for m, (q0, q1, q2) in enumerate(zip(*[near_pairs(at, at + 1) for at in (0, 1, 2)])):
        for at, piece in ((1, q1), (10, q2 + northf * q0), (12, q0 * (1.0 - northf))):
            sp_hi[m, at:at + 1], sp_lo[m, at:at + 1] = halves(piece)
    put3((((10, 11), (3, 4)), ((1, 3),), ((12, 13), (1, 2))), ((0, 2),))
    for copy in rim2:
        copy.wait_send()


def shards(n_lon, n_lat, latent, conv1_weight, conv1_bias, conv2_weight, conv2_bias, head_weight, head_bias, land_sea,
           var_ok, obs_error, obs_band, obs_cell, obs_count, obs_value):
    lc, hid = conv1_weight.shape[2], conv1_weight.shape[3]
    slots, patch = obs_value.shape[1], obs_value.shape[2]
    variables = var_ok.shape[1]
    listed = n_lat * slots
    padded = -(-(listed + 128) // 128) * 128
    vmem = pltpu.VMEM
    rows = n_lat * MSG
    scratch = [
        vmem((lc // 128, 12, BUF, 128), F32),
        vmem((4, 13, 2 * PAIRS, lc), BF16), vmem((4, 13, 2 * PAIRS, lc), BF16),
        vmem((9 * lc, hid), F32), vmem((4, 3 * lc, hid), BF16), vmem((4, 3 * lc, hid), BF16),
        vmem((9 * hid, hid), F32), vmem((4, 3 * hid, hid), BF16), vmem((4, 3 * hid, hid), BF16),
        vmem((1, hid), F32), vmem((1, hid), F32),
        vmem((2, 10, PAIRS, hid), F32), vmem((2, 10, PAIRS, hid), F32),
        vmem((4, 10, 32, hid), BF16), vmem((4, 10, 32, hid), BF16),
        vmem((512, hid), F32),
        vmem((patch, hid), F32), vmem((patch, hid), BF16), vmem((patch, hid), BF16),
        vmem((patch,), F32), vmem(land_sea.shape, jnp.int32), vmem(var_ok.shape, jnp.int32),
        vmem((1, variables), F32),
        vmem((1, padded), jnp.int32), vmem((1, padded), jnp.int32), vmem((1, padded), jnp.int32),
        vmem((slots, patch), F32), vmem((slots, patch), BF16), vmem((slots, patch), BF16),
        vmem((2 * slots, patch), BF16),
        vmem((128, patch), BF16), vmem((1, patch), F32),
        vmem((n_lat * CAP, 512), BF16), vmem((512, n_lat * CAP), BF16), vmem((512, rows), BF16),
        vmem((rows, 128), BF16),
        vmem((128, n_lat * LCAP), BF16), vmem((128, 128), F32),
        vmem((n_lat, LCAP, 128), F32), vmem((n_lat, LCAP, 128), F32),
        vmem((n_lat, MSG, 128), F32), vmem((n_lat, MSG, 128), F32),
        vmem((hid // 128, 12, BUF, 128), F32),
        vmem((2, hid // 128, 16, 128), F32), vmem((2, hid // 128, 16, 128), F32),
        vmem((4, hid // 128, 4, 128), F32), vmem((4, hid // 128, 4, 128), F32),
        vmem((4, 13, 2 * PAIRS, hid), BF16), vmem((4, 13, 2 * PAIRS, hid), BF16),
        vmem((2, 10, PAIRS, hid), F32),
        vmem((4, 14, 32, hid), BF16), vmem((4, 14, 32, hid), BF16),
        pltpu.SemaphoreType.DMA((14,)),
        pltpu.SemaphoreType.DMA((10,)), pltpu.SemaphoreType.DMA((18,)),
        pltpu.SemaphoreType.DMA((10,)), pltpu.SemaphoreType.DMA((18,)),
    ] + [pltpu.SemaphoreType.DMA((n_lat,))] * 4
    return pl.pallas_call(
        functools.partial(kernel, n_lon, n_lat, slots, patch, variables),
        out_shape=jax.ShapeDtypeStruct(latent.shape, F32),
        in_specs=[pl.BlockSpec(memory_space=pl.ANY)] * 14,
        out_specs=pl.BlockSpec(memory_space=pltpu.VMEM),
        scratch_shapes=scratch,
        compiler_params=pltpu.CompilerParams(
            collective_id=0, has_side_effects=True, vmem_limit_bytes=48 * 1024 * 1024),
    )(*(pltpu.with_memory_space_constraint(x, pltpu.HBM) for x in (
        latent, conv1_weight.reshape(9 * lc, hid), conv1_bias.reshape(1, hid), conv2_weight.reshape(9 * hid, hid),
      conv2_bias.reshape(1, hid), head_weight.T, head_bias, land_sea, var_ok,
      obs_error.reshape(1, variables), obs_band.reshape(1, listed), obs_cell, obs_count, obs_value[0])))


def solution(mesh):
    in_specs = (
        P("lat", "lon", None),
        P(),
        P(),
        P(),
        P(),
        P(),
        P(),
        P("lat", "lon"),
        P(),
        P(),
        P("lon", None, None),
        P("lon", None),
        P("lon", None),
        P("lon", "lat", None),
    )
    out_specs = P("lat", "lon", None)
    body = functools.partial(shards, mesh.shape["lon"], mesh.shape["lat"])
    return jax.shard_map(body, mesh=mesh, in_specs=in_specs, out_specs=out_specs, check_vma=False)
```

```python
import functools

import jax
import jax.numpy as jnp
from jax import lax
from jax.experimental import pallas as pl
from jax.experimental.pallas import tpu as pltpu
from jax.sharding import PartitionSpec as P

F32 = jnp.float32
BF16 = jnp.bfloat16
CAP = 12
MSG = 2 * CAP
LCAP = 16
GROUPS = ((0, 2, 0), (6, 8, 128), (2, 6, 256))
SIDE = 8
PAIRS = 40
BUF = 88
CHUNK = 512
MESH = pl.DeviceIdType.MESH


def halves(x):
    high = x.astype(BF16)
    return high, (x - high.astype(F32)).astype(BF16)


def nn(a, b):
    return lax.dot_general(a, b, (((1,), (0,)), ((), ())), preferred_element_type=F32)


def nt(a, b):
    return lax.dot_general(a, b, (((1,), (1,)), ((), ())), preferred_element_type=F32)


def gelu_parts(x):
    c = 0.7978845608028654
    t = jnp.tanh(c * (x + 0.044715 * x * x * x))
    return 0.5 * x * (1.0 + t), t


def gelu_slope(x):
    c = 0.7978845608028654
    t = jnp.tanh(c * (x + 0.044715 * x * x * x))
    return 0.5 * (1.0 + t) + 0.5 * x * (1.0 - t * t) * (c * (1.0 + 3.0 * 0.044715 * x * x))


def kernel(
    n_lon, n_lat, slots, patch, variables,
    latent, w1, b1, w2, b2, head, hbias, land, ok, err, band, cell, count, value,
    out,
    lat_ext, sa_hi, sa_lo, w1_v, w1_hi, w1_lo, w2_v, w2_hi, w2_lo, b1_v, b2_v,
    pre1, act1, sb_hi, sb_lo, pre2, head_v, head_hi, head_lo, hb_v, land_v, ok_v, err_v,
    band_v, cell_v, count_v, value_v, val_hi, val_lo, masked, ok_rows, inv_row,
    tiles_v, flags_w, oh, oht, oht_msg, pmt, from_land, own_weight, land_send, land_recv, term_send, term_recv,
    g_ext, side_send, side_recv, corner_send, corner_recv, sg_hi, sg_lo, p_ext, sp_hi, sp_lo,
    load_sem, h_send, h_recv, g_send, g_recv, l_send, l_recv, t_send, t_recv,
):
    lon, lat = lax.axis_index("lon"), lax.axis_index("lat")
    north = 1 - lax.div(lat + n_lat - 1, n_lat)
    south = lax.div(lat + 1, n_lat)
    northf, southf = north.astype(F32), south.astype(F32)
    hid = w1_v.shape[1]
    k1 = latent.shape[2]

    loads = [
        (band, band_v.at[:, 0:n_lat * slots]),
        (cell, cell_v.at[:, 0:n_lat * slots]),
        (count, count_v.at[:, 0:n_lat * slots]),
        (land, land_v),
        (latent, lat_ext.at[0, 2:10, SIDE:SIDE + 64, :]),
        (w1, w1_v),
        (b1, b1_v),
        (ok, ok_v),
        (err, err_v),
        (hbias, hb_v),
        (w2, w2_v),
        (b2, b2_v),
        (value, value_v),
        (head, head_v),
    ]
    copies = [pltpu.make_async_copy(s, d, load_sem.at[i]) for i, (s, d) in enumerate(loads)]
    (ld_band, ld_cell, ld_count, ld_land, ld_lat, ld_w1, ld_b1, ld_ok, ld_err, ld_hb, ld_w2, ld_b2, ld_value,
     ld_head) = copies
    for copy in copies[:5]:
        copy.start()

    half = n_lon // 2
    up_lat, down_lat = lat - 1 + north, lat + 1 - south
    around = []
    for dr in (-1, 0, 1):
        for dc in (-1, 0, 1):
            if dr == 0 and dc == 0:
                continue
            turn = half * north if dr < 0 else half * south if dr > 0 else 0
            to_lon = lax.rem(lon + dc + turn + n_lon, n_lon)
            to_lat = up_lat if dr < 0 else down_lat if dr > 0 else lat
            around.append((dr, dc, (to_lon, to_lat)))

    deep = n_lat // 2
    steps = [(far, step) for far in range(2) for step in range(deep) if far or step]
    steps.sort(key=lambda s: -(2 * s[0] + min(s[1], deep - s[1])))
    peers = [lax.rem(lax.div(lat, deep) + far, 2) * deep + lax.rem(lax.rem(lat, deep) + step, deep)
             for far, step in steps]

    barrier = pltpu.get_barrier_semaphore()
    for peer in peers:
        pl.semaphore_signal(barrier, inc=1, device_id=(lon, peer), device_id_type=MESH)
    for _, _, device in around:
        pl.semaphore_signal(barrier, inc=1, device_id=device, device_id_type=MESH)
    for copy in copies[5:]:
        copy.start()

    near_rows, far_rows, corners, sides = range(4)
    parts = []
    for dr, dc, device in around:
        if dr and not dc:
            parts += [(near_rows, dr, dc, device), (far_rows, dr, dc, device)]
        else:
            parts.append((corners if dr else sides, dr, dc, device))

    def rim(buf, send_sem, recv_sem, kinds, drs=(-1, 0, 1)):
        sent = []
        for kind in kinds:
            for number, (its, dr, dc, device) in enumerate(parts):
                if its != kind or dr not in drs:
                    continue
                src_c = (SIDE, SIDE) if dc < 0 else (SIDE + 56, SIDE) if dc > 0 else (SIDE, 64)
                dst_c = 72 if dc < 0 else 0 if dc > 0 else SIDE
                second = 1 if kind == far_rows else 0
                if dr < 0:
                    src_r, dst_r, side = 2 + second, 10 - 10 * north + second, 2 * (1 - north)
                elif dr > 0:
                    src_r, dst_r, side = 9 - second, 1 + 10 * south - second, 2 * south
                else:
                    src_r, dst_r, side = 2, 2, 1
                length = 8 if kind == sides else 1
                if kind == corners:
                    length = 2
                    if dr > 0:
                        src_r, dst_r = 8, 10 * south
                slot = 9 + (1 - north if dr < 0 else south) if second else side * 3 + (1 - dc)
                src = buf.at[:, pl.ds(src_r, length), pl.ds(src_c[0], src_c[1]), :]
                dst = buf.at[:, pl.ds(dst_r, length), pl.ds(dst_c, src_c[1]), :]
                copy = pltpu.make_async_remote_copy(
                    src_ref=src, dst_ref=dst, send_sem=send_sem.at[number], recv_sem=recv_sem.at[slot],
                    device_id=device, device_id_type=MESH)
                copy.start()
                sent.append(copy)
        return sent

    def rim_arrived(buf, recv_sem, send_sem, kinds, drs=(-1, 0, 1)):
        for number, (kind, dr, dc, device) in enumerate(parts):
            if kind not in kinds or dr not in drs:
                continue
            cols_ = (0, SIDE) if dc < 0 else (72, SIDE) if dc > 0 else (SIDE, 64)
            second = 1 if kind == far_rows else 0
            if kind == sides:
                at, length = 2, 8
            elif kind == corners:
                at, length = (0 if dr < 0 else 10), 2
            else:
                at, length = (1 - north if dr < 0 else 10 + south), 1
                if second:
                    at = north if dr < 0 else 11 - south
            ref = buf.at[:, pl.ds(at, length), pl.ds(cols_[0], cols_[1]), :]
            slot = 9 + (dr + 1) // 2 if second else (dr + 1) * 3 + dc + 1
            pltpu.make_async_remote_copy(
                src_ref=ref, dst_ref=ref, send_sem=send_sem.at[number], recv_sem=recv_sem.at[slot],
                device_id=device, device_id_type=MESH).wait_recv()

    def last_columns(dc):
        return SIDE if dc < 0 else SIDE + 62

    def halo_columns(dc):
        return SIDE - 2 if dc < 0 else 72

    def packed_rim(kind, its_dr, send_sem, recv_sem):
        sent = []
        for number, (its, dr, dc, device) in enumerate(parts):
            if its != kind or dr != its_dr:
                continue
            at = last_columns(dc)
            if kind == sides:
                mine_, theirs_, ref, into_ref = (dc + 1) // 2, (1 - dc) // 2, side_send, side_recv
                for h in range(hid // 128):
                    for j in range(2):
                        ref[mine_, h, 8 * j:8 * j + 8, :] = g_ext[h, 2:10, at + j:at + j + 1, :].reshape(8, 128)
                slot = 3 + (1 - dc)
            else:
                side = 2 - 2 * north if dr < 0 else 2 * south
                mine_, theirs_, ref, into_ref = dr + 1 + (dc + 1) // 2, side + (1 - dc) // 2, corner_send, corner_recv
                for h in range(hid // 128):
                    for r in range(2):
                        row_ = (2 if dr < 0 else 8) + r
                        ref[mine_, h, 2 * r:2 * r + 2, :] = g_ext[h, row_, at:at + 2, :]
                slot = side * 3 + (1 - dc)
            copy = pltpu.make_async_remote_copy(
                src_ref=ref.at[mine_], dst_ref=into_ref.at[theirs_], send_sem=send_sem.at[number],
                recv_sem=recv_sem.at[slot], device_id=device, device_id_type=MESH)
            copy.start()
            sent.append(copy)
        return sent

    def packed_arrived(kind, its_dr, send_sem, recv_sem):
        for number, (its, dr, dc, device) in enumerate(parts):
            if its != kind or dr != its_dr:
                continue
            at, slot = halo_columns(dc), (dr + 1) * 3 + dc + 1
            mine_ = (dc + 1) // 2 if kind == sides else dr + 1 + (dc + 1) // 2
            ref = side_recv if kind == sides else corner_recv
            pltpu.make_async_remote_copy(
                src_ref=ref.at[mine_], dst_ref=ref.at[mine_], send_sem=send_sem.at[number],
                recv_sem=recv_sem.at[slot], device_id=device, device_id_type=MESH).wait_recv()
            for h in range(hid // 128):
                for j in range(2):
                    if kind == sides:
                        g_ext[h, 2:10, at + j:at + j + 1, :] = ref[mine_, h, 8 * j:8 * j + 8, :].reshape(8, 1, 128)
                    else:
                        g_ext[h, (0 if dr < 0 else 10) + j, at:at + 2, :] = ref[mine_, h, 2 * j:2 * j + 2, :]

    def exchange(src, dst, send_sem, recv_sem):
        for peer in peers:
            pltpu.make_async_remote_copy(
                src_ref=src.at[peer], dst_ref=dst.at[lat], send_sem=send_sem.at[0], recv_sem=recv_sem.at[0],
                device_id=(lon, peer), device_id_type=MESH).start()
        dst[pl.ds(lat, 1)] = src[pl.ds(lat, 1)]
        every = pl.ds(0, len(peers))
        return pltpu.make_async_remote_copy(
            src_ref=src.at[every], dst_ref=dst.at[every], send_sem=send_sem.at[0], recv_sem=recv_sem.at[0],
            device_id=(lon, peers[0]), device_id_type=MESH)

    def split(src, high_ref, low_ref, step):
        def body(i, carry):
            at = pl.ds(pl.multiple_of(i * step, step), step)
            high_ref[at, :], low_ref[at, :] = halves(src[at, :])
            return carry
        lax.fori_loop(0, src.shape[0] // step, body, 0)

    def split_taps(src, high_ref, low_ref, depth, step):
        for i in range(3):
            def body(n, carry):
                g0, g1, g2 = (src[pl.ds(pl.multiple_of((3 * i + j) * depth + n * step, step), step), :] for j in range(3))
                outer, inner = 0.5 * (g0 + g2), 0.5 * g1
                at = pl.ds(pl.multiple_of(i * depth + n * step, step), step)
                for m, factor in enumerate((g0, outer + inner, outer - inner, g2)):
                    high_ref[m, at, :], low_ref[m, at, :] = halves(factor)
                return carry
            lax.fori_loop(0, depth // step, body, 0)

    def factors(d0, d1, d2, d3):
        return d0 - d2, d1 + d2, d2 - d1, d1 - d3

    def pair_rows(buf, at, length=1):
        def column(d):
            lanes = [buf[h, pl.ds(at, length), pl.ds(SIDE - 2 + d, PAIRS, stride=2), :] for h in range(buf.shape[0])]
            return jnp.concatenate(lanes, axis=2)
        return factors(*[column(d) for d in range(4)])

    def put_rows(high_ref, low_ref, at, pieces):
        for m, piece in enumerate(pieces):
            count_ = piece.shape[0] // 2
            high_ref[m, at:at + count_], low_ref[m, at:at + count_] = halves(
                piece.reshape(count_, 2 * PAIRS, piece.shape[2]))

    def joined(*rows_):
        return [jnp.concatenate(list(x), axis=0) for x in zip(*rows_)]

    def inner_rows(buf, high_ref, low_ref):
        pieces = pair_rows(buf, 2, 8)
        put_rows(high_ref, low_ref, 0, pieces)
        put_rows(high_ref, low_ref, 4, [x[1:7] for x in pieces])

    def pair_sums(taken_hi, taken_lo, weights, stacked=False):
        products = []
        for m in range(4):
            lhs, (wh, wl, dot) = taken_hi(m), weights(m)
            if stacked:
                both_ = dot(jnp.concatenate([lhs, taken_lo(m)], axis=0), wh)
                products.append(both_[:lhs.shape[0]] + both_[lhs.shape[0]:] + dot(lhs, wl))
            else:
                products.append(dot(lhs, wh) + dot(lhs, wl) + dot(taken_lo(m), wh))
        m0, m1, m2, m3 = products
        return m0 + m1 + m2, m1 - m2 - m3

    def taps(ref, chosen):
        def lhs(m):
            rows_ = [jnp.concatenate([ref[m, a:b] for a, b in part], axis=0) for part in chosen]
            return jnp.concatenate([x.reshape(x.shape[0] * x.shape[1], x.shape[2]) for x in rows_], axis=1)
        return lhs

    lat_ext[:, :, 80:88, :] = jnp.zeros((k1 // 128, 12, 8, 128), F32)
    g_ext[:, :, 72:88, :] = jnp.zeros((hid // 128, 12, 16, 128), F32)

    ld_band.wait()
    ld_cell.wait()
    ld_count.wait()
    lane = lax.broadcasted_iota(jnp.int32, (n_lat, 128), 1)
    live = lane < slots

    def blocks(ref):
        row = ref[...]
        return jnp.concatenate([row[:, slots * a:slots * a + 128] for a in range(n_lat)], axis=0)

    bands, cells, counts = blocks(band_v), blocks(cell_v), blocks(count_v)
    below = (lax.broadcasted_iota(jnp.int32, (128, 128), 0) < lax.broadcasted_iota(jnp.int32, (128, 128), 1))
    below = below.astype(F32).astype(BF16)
    mine = jnp.where(live & (bands == lat), 1.0, 0.0)
    pick = jnp.where(mine > 0.0, nn(mine.astype(BF16), below), -1.0)
    cell_row, odd, pair = cells >> 6, cells & 1, (cells & 63) >> 1
    edge = (cell_row << 5) + (odd << 6) + jnp.where(cell_row > 5, 128 - 6 * 32, 0)
    inner = (cell_row << 5) + (odd << 7) + (256 - 2 * 32)
    cells = pair + jnp.where((cell_row < 2) | (cell_row > 5), edge, inner)
    cellsf = cells.astype(F32) + 1.0
    countsf = counts.astype(F32) * 0.125
    msg_k = lax.rem(lax.broadcasted_iota(jnp.int32, (MSG, 128), 0), CAP).astype(F32)
    land_k = lax.broadcasted_iota(jnp.int32, (LCAP, 128), 0).astype(F32)
    named = [jnp.sum(jnp.where(pick[a:a + 1] == land_k, cellsf[a:a + 1], 0.0), axis=1, keepdims=True)
             for a in range(n_lat)]
    wanted = jnp.concatenate(named, axis=0).astype(jnp.int32) - 1
    lrows = n_lat * LCAP
    messages = jnp.where(wanted == lax.broadcasted_iota(jnp.int32, (lrows, 512), 1), 1.0, 0.0).astype(BF16)

    ld_land.wait()
    column = lax.broadcasted_iota(jnp.int32, (64, 512), 0)
    column = ((column & 31) << 1) + (column >> 5)
    fold = (lax.broadcasted_iota(jnp.int32, (64, 512), 1) >> 3) == column
    fold = jnp.where(fold, 1.0, 0.0).astype(BF16)
    kept = (lax.broadcasted_iota(jnp.int32, (8, 512), 1) & 7) == lax.broadcasted_iota(jnp.int32, (8, 512), 0)
    tiles = []
    for r in range(8):
        strip = land_v[8 * r:8 * r + 8, :].astype(F32)
        spread = jnp.concatenate([jnp.where(kept, strip[p:p + 1], 0.0) for p in range(8)], axis=0)
        tiles.append(nt(fold, spread.astype(BF16)))
    tiles = [tiles[r][32 * parity:32 * parity + 32] for first_, last, _ in GROUPS for parity in range(2) for r in range(first_, last)]
    tiles = jnp.concatenate(tiles, axis=0)
    tiles = jnp.concatenate([tiles, 1.0 - tiles], axis=1).astype(BF16)
    tiles_v[...] = tiles
    land_send[...] = nn(messages, tiles).reshape(n_lat, LCAP, 128)

    pl.semaphore_wait(barrier, len(around) + len(peers))
    land_sent = exchange(land_send, land_recv, l_send, l_recv)
    ld_lat.wait()
    rim1 = rim(lat_ext, h_send, h_recv, (sides, near_rows, corners, far_rows))

    ld_w1.wait()
    split_taps(w1_v, w1_hi, w1_lo, k1, 64)

    first = lax.broadcasted_iota(jnp.int32, (MSG, 128), 0) < CAP
    taken = n_lat * CAP
    named, merged = [], []
    for q in range(n_lat // 2):
        def two(x):
            return jnp.where(first, x[2 * q:2 * q + 1], x[2 * q + 1:2 * q + 2])
        hit = two(pick) == msg_k
        named.append(jnp.sum(jnp.where(hit, two(cellsf), 0.0), axis=1, keepdims=True))
        merged.append(jnp.sum(jnp.where(hit, two(countsf), 0.0), axis=1, keepdims=True))
    wanted = jnp.concatenate(named, axis=0).astype(jnp.int32) - 1
    weight = jnp.concatenate(merged, axis=0)
    oh[...] = jnp.where(wanted == lax.broadcasted_iota(jnp.int32, (taken, 512), 1), 1.0, 0.0).astype(BF16)
    flags_w[...] = (nn(oh[...], tiles_v[...]) * weight).astype(BF16)

    own = lax.broadcasted_iota(jnp.int32, (n_lat, 128), 0) == lat
    own_band = jnp.sum(jnp.where(own, bands, 0), axis=0, keepdims=True)
    own_count = jnp.sum(jnp.where(own, countsf, 0.0), axis=0, keepdims=True)
    theirs = jnp.where(live & (own_band == lax.broadcasted_iota(jnp.int32, (n_lat, 128), 0)), 1.0, 0.0)
    place = jnp.where(theirs > 0.0, nn(theirs.astype(BF16), below), -1.0)
    pmt[...] = jnp.concatenate(
        [jnp.where(place[b:b + 1] == msg_k, 1.0, 0.0) for b in range(n_lat)], axis=0).astype(BF16)
    pml = jnp.concatenate([jnp.where(place[b:b + 1] == land_k, 1.0, 0.0) for b in range(n_lat)], axis=0)
    from_land[...] = jnp.transpose(pml).astype(BF16)
    own_weight[...] = jnp.transpose(jnp.broadcast_to(own_count, (128, 128)))

    ld_ok.wait()
    ld_err.wait()
    ld_hb.wait()
    ld_w2.wait()
    split_taps(w2_v, w2_hi, w2_lo, hid, 64)
    inv = 1.0 / (err_v[...] * err_v[...])
    inv_hi = inv.astype(BF16).astype(F32)
    inv_mid = (inv - inv_hi).astype(BF16).astype(F32)
    inv_lo = inv - inv_hi - inv_mid
    okf = ok_v[...].astype(F32)
    kind = lax.broadcasted_iota(jnp.int32, (16, variables), 0)
    table = jnp.where(kind == 0, inv_hi, jnp.where(kind == 1, inv_mid, jnp.where(kind == 2, inv_lo, 0.0)))
    table = table + jnp.where(kind == 3, okf[1:2], 0.0) + jnp.where(kind == 4, okf[0:1], 0.0)
    table = table.astype(BF16)
    spans = [(at, min(CHUNK, patch - at)) for at in range(0, patch, CHUNK)]
    for at, size in spans:
        place_ = lax.broadcasted_iota(jnp.int32, (1, size), 1) + at
        pixel = ((place_.astype(F32) + 0.5) * (1.0 / variables)).astype(jnp.int32)
        variable = place_ - pixel * variables
        chosen = lax.broadcasted_iota(jnp.int32, (variables, size), 0) == variable
        spread = nn(table, jnp.where(chosen, 1.0, 0.0).astype(BF16))
        inv_row[:, at:at + size] = spread[0:1] + spread[1:2] + spread[2:3]
        which = lax.broadcasted_iota(jnp.int32, (128, size), 0)
        seen = jnp.where(which == pixel, spread[3:4], jnp.where(which == pixel + 64, spread[4:5], 0.0))
        ok_rows[:, at:at + size] = seen.astype(BF16)
    ld_b1.wait()
    ld_b2.wait()
    ld_value.wait()
    for at, size in spans:
        span = slice(at, at + size)
        shifted = (value_v[:, span] - hb_v[span].reshape(1, size)) * inv_row[:, span]
        val_hi[:, span], val_lo[:, span] = halves(shifted)
    ld_head.wait()
    split(head_v, head_hi, head_lo, 96)

    rim_arrived(lat_ext, h_recv, h_send, (sides,))

    def forward1(m):
        return w1_hi[m], w1_lo[m], nn

    def put1(chosen, groups):
        for parity, summed in enumerate(pair_sums(taps(sa_hi, chosen), taps(sa_lo, chosen), forward1)):
            summed = summed + b1_v[...]
            act = gelu_parts(summed)[0]
            for source, target, length in groups:
                part = slice(source * PAIRS, (source + length) * PAIRS)
                pre1[parity, target:target + length] = summed[part].reshape(length, PAIRS, hid)
                act1[parity, target:target + length] = act[part].reshape(length, PAIRS, hid)

    inner_rows(lat_ext, sa_hi, sa_lo)
    put1((((0, 3),), ((4, 7),), ((1, 4),)), ((0, 2, 6),))

    land_sent.wait_recv()
    flags_own = nn(from_land[...], land_recv[...].reshape(lrows, 128).astype(BF16))
    flags_own = flags_own[:slots].astype(BF16)

    def back(high, low, at, size, total):
        count_ = high.shape[0]
        hh, hl = head_hi[at:at + size, :], head_lo[at:at + size, :]
        both = nn(jnp.concatenate([high, low], axis=0), hh)
        return total + both[:count_] + both[count_:] + nn(high, hl)

    for at, size in spans:
        span = slice(at, at + size)
        seen = nn(flags_own, ok_rows[:, span]).astype(BF16)
        masked[0:slots, span] = val_hi[:, span] * seen
        masked[slots:2 * slots, span] = val_lo[:, span] * seen
    cut = patch // 256 * 128
    shares = jnp.concatenate([own_weight[0:slots, :]] * (hid // 128), axis=1)
    terms = jnp.zeros((slots, hid), F32)
    for a, b in ((0, cut), (cut, patch)):
        both = nn(masked[:, a:b], head_hi[a:b, :])
        terms = terms + (both[:slots] + both[slots:] + nn(masked[0:slots, a:b], head_lo[a:b, :])) * shares
    high, low = halves(terms)
    both = jnp.concatenate([high, low], axis=1)
    if slots < 128:
        both = jnp.concatenate([both, jnp.zeros((128 - slots, 2 * hid), BF16)], axis=0)
    rows = n_lat * MSG
    upper = lax.rem(lax.broadcasted_iota(jnp.int32, (rows, 128), 0), MSG) < CAP
    sent_terms = nn(pmt[...], both)
    sent_terms = sent_terms[:, :hid] + sent_terms[:, hid:]
    term_send[...] = jnp.where(upper, sent_terms[:, :128], sent_terms[:, 128:]).reshape(n_lat, MSG, 128)
    terms_sent = exchange(term_send, term_recv, t_send, t_recv)

    rim_arrived(lat_ext, h_recv, h_send, (near_rows, corners, far_rows))
    for at, one, other in (
        (7, 1 - north, 2), (8, 9, 10 + south),
        (9, 2 * north, 1 - north), (10, 8, 9 + south),
        (11, 2 - north, 3), (12, 10 + south, 11 - 2 * south),
    ):
        put_rows(sa_hi, sa_lo, at, joined(pair_rows(lat_ext, one), pair_rows(lat_ext, other)))
    put1((((9, 11),), ((7, 9),), ((11, 13),)), ((0, 0, 2), (2, 8, 2)))

    def near(ref, rows_=slice(0, 10)):
        return factors(ref[0, rows_, 0:32], ref[1, rows_, 0:32], ref[0, rows_, 1:33], ref[1, rows_, 1:33])

    for m, piece in enumerate(near(act1)):
        sb_hi[m], sb_lo[m] = halves(piece)

    def forward2(m):
        return w2_hi[m], w2_lo[m], nn

    chosen = tuple(((i, i + 8),) for i in range(3))
    summed = pair_sums(taps(sb_hi, chosen), taps(sb_lo, chosen), forward2)
    summed = [x[32 * first_:32 * last] for first_, last, _ in GROUPS for x in summed]
    summed = jnp.concatenate(summed, axis=0) + b2_v[...]
    pre2[...] = summed
    act2, _ = gelu_parts(summed)

    high, low = halves(act2)
    cols = nn(oh[...], jnp.concatenate([high, low], axis=1)).astype(BF16)
    cols_hi, cols_lo = cols[:, :hid], cols[:, hid:]
    cols_both = jnp.concatenate([cols_hi, cols_lo], axis=0)
    terms = jnp.zeros((taken, hid), F32)
    for at, size in spans:
        span = slice(at, at + size)
        both = nt(cols_both, head_hi[span, :])
        decoded = both[:taken] + both[taken:] + nt(cols_hi, head_lo[span, :])
        high, low = halves(nn(flags_w[...], ok_rows[:, span]) * inv_row[:, span] * decoded)
        terms = back(high, low, at, size, terms)

    wanted_row = jnp.transpose(jnp.broadcast_to(wanted.astype(F32), (taken, 128)))[0:1, :].astype(jnp.int32)
    oht[...] = jnp.where(wanted_row == lax.broadcasted_iota(jnp.int32, (512, taken), 0), 1.0, 0.0).astype(BF16)
    named = [jnp.sum(jnp.where(pick[a:a + 1] == msg_k, cellsf[a:a + 1], 0.0), axis=1, keepdims=True)
             for a in range(n_lat)]
    named = jnp.broadcast_to(jnp.concatenate(named, axis=0), (rows, 128))
    wanted_row = jnp.transpose(named)[0:1, :].astype(jnp.int32) - 1
    oht_msg[...] = jnp.where(wanted_row == lax.broadcasted_iota(jnp.int32, (512, rows), 0), 1.0, 0.0).astype(BF16)
    high, low = halves(terms)
    hidden = nn(oht[...], jnp.concatenate([high, low], axis=1))
    hidden = hidden[:, :hid] + hidden[:, hid:]
    pre2[...] = gelu_slope(pre2[...])
    pre1[...] = gelu_slope(pre1[...])
    for copy in rim1:
        copy.wait_send()
    land_sent.wait_send()

    terms_sent.wait_recv()

    came = term_recv[...].reshape(rows, 128)
    came = jnp.concatenate([jnp.where(upper, came, 0.0), jnp.where(upper, 0.0, came)], axis=1)
    high, low = halves(came)
    came = jnp.concatenate([high, low], axis=1)

    rim2 = []
    for (first_, last, base), dr in zip(GROUPS, (-1, 1, 0)):
        held = 32 * (last - first_)
        cells_ = slice(base, base + 2 * held)
        moved = nn(oht_msg[cells_, :], came)
        grad2 = (hidden[cells_] - moved[:, :hid] - moved[:, hid:]) * pre2[cells_, :]
        for parity in range(2):
            for h in range(hid // 128):
                g_ext[h, 2 + first_:2 + last, pl.ds(SIDE + parity, 32, stride=2), :] = (
                    grad2[held * parity:held * parity + held, 128 * h:128 * h + 128].reshape(last - first_, 32, 128))
        if dr:
            rim2 += rim(g_ext, g_send, g_recv, (near_rows, far_rows), (dr,))
            rim2 += packed_rim(corners, dr, g_send, g_recv)
        else:
            rim2 += packed_rim(sides, dr, g_send, g_recv)
    terms_sent.wait_send()

    packed_arrived(sides, 0, g_send, g_recv)

    def backward(high_ref, low_ref, depth):
        def weights(m):
            at = (3, 1, 2, 0)[m]
            return tuple(jnp.concatenate([ref[at, i * depth:(i + 1) * depth] for i in range(3)], axis=1)
                         for ref in (high_ref, low_ref)) + (nt,)
        return weights

    def put2(chosen, groups, stacked=False):
        sums = pair_sums(taps(sg_hi, chosen), taps(sg_lo, chosen), backward(w2_hi, w2_lo, hid), stacked)
        for parity, grad1 in enumerate(sums):
            for source, target, length in groups:
                part = grad1[source * PAIRS:(source + length) * PAIRS].reshape(length, PAIRS, hid)
                p_ext[parity, target:target + length] = part * pre1[parity, target:target + length]

    def scaled_by(x, factor):
        return [y * factor for y in x]

    def plus(x, y, factor):
        return [u + v * factor for u, v in zip(x, y)]

    def near_pairs(first_, last):
        rows_ = slice(first_, last)
        return factors(p_ext[0, rows_, 0:32], p_ext[1, rows_, 0:32], p_ext[0, rows_, 1:33], p_ext[1, rows_, 1:33])

    def put_pairs(first_, last, at):
        for m, piece in enumerate(near_pairs(first_, last)):
            sp_hi[m, at:at + last - first_], sp_lo[m, at:at + last - first_] = halves(piece)

    def put3(chosen, rows_):
        products = []
        for m in range(4):
            wh, wl, dot = backward(w1_hi, w1_lo, k1)(m)
            lhs = taps(sp_hi, chosen)(m)
            count_ = lhs.shape[0]
            both_ = dot(jnp.concatenate([lhs, taps(sp_lo, chosen)(m)], axis=0), jnp.concatenate([wh, wl], axis=0))
            products.append(both_[:count_, :k1] + both_[:count_, k1:] + both_[count_:, :k1])
        m0, m1, m2, m3 = products
        for parity, part in enumerate((m0 + m1 + m2, m1 - m2 - m3)):
            part = part.reshape(part.shape[0] // 32, 32, k1)
            done = 0
            for first_, last in rows_:
                out[first_:last, pl.ds(parity, 32, stride=2), :] = part[done:done + last - first_]
                done += last - first_

    inner_rows(g_ext, sg_hi, sg_lo)
    put2((((1, 4),), ((4, 7),), ((0, 3),)), ((0, 2, 6),))
    put_pairs(2, 8, 2)
    put3((((4, 8),), ((3, 7),), ((2, 6),)), ((2, 6),))
    rim_arrived(g_ext, g_recv, g_send, (near_rows, far_rows), (1,))
    packed_arrived(corners, 1, g_send, g_recv)
    r10, r11 = pair_rows(g_ext, 10 + south), pair_rows(g_ext, 11 - south)
    put_rows(sg_hi, sg_lo, 8, joined(pair_rows(g_ext, 9), r10))
    put_rows(sg_hi, sg_lo, 10, joined(scaled_by(r10, 1.0 - southf), scaled_by(r11, 1.0 - southf)))
    put_rows(sg_hi, sg_lo, 12, joined(plus(pair_rows(g_ext, 8), r10, southf), plus(pair_rows(g_ext, 9), r11, southf)))
    put2((((10, 11),), ((8, 9),), ((12, 13),)), ((0, 8, 2),), True)
    for m, (q7, q8, q9) in enumerate(zip(*[near_pairs(at, at + 1) for at in (7, 8, 9)])):
        for at, piece in ((8, q8), (11, q9 * (1.0 - southf)), (13, q7 + southf * q9)):
            sp_hi[m, at:at + 1], sp_lo[m, at:at + 1] = halves(piece)
    put3((((8, 9), (11, 12)), ((7, 9),), ((6, 7), (13, 14))), ((6, 8),))

    rim_arrived(g_ext, g_recv, g_send, (near_rows, far_rows), (-1,))
    packed_arrived(corners, -1, g_send, g_recv)
    r0, r1 = pair_rows(g_ext, north), pair_rows(g_ext, 1 - north)
    put_rows(sg_hi, sg_lo, 7, joined(r1, pair_rows(g_ext, 2)))
    put_rows(sg_hi, sg_lo, 9, joined(plus(pair_rows(g_ext, 2), r0, northf), plus(pair_rows(g_ext, 3), r1, northf)))
    put_rows(sg_hi, sg_lo, 11, joined(scaled_by(r0, 1.0 - northf), scaled_by(r1, 1.0 - northf)))
    put2((((9, 10),), ((7, 8),), ((11, 12),)), ((0, 0, 2),), True)
    for m, (q0, q1, q2) in enumerate(zip(*[near_pairs(at, at + 1) for at in (0, 1, 2)])):
        for at, piece in ((1, q1), (10, q2 + northf * q0), (12, q0 * (1.0 - northf))):
            sp_hi[m, at:at + 1], sp_lo[m, at:at + 1] = halves(piece)
    put3((((10, 11), (3, 4)), ((1, 3),), ((12, 13), (1, 2))), ((0, 2),))
    for copy in rim2:
        copy.wait_send()


def shards(n_lon, n_lat, latent, conv1_weight, conv1_bias, conv2_weight, conv2_bias, head_weight, head_bias, land_sea,
           var_ok, obs_error, obs_band, obs_cell, obs_count, obs_value):
    lc, hid = conv1_weight.shape[2], conv1_weight.shape[3]
    slots, patch = obs_value.shape[1], obs_value.shape[2]
    variables = var_ok.shape[1]
    listed = n_lat * slots
    padded = -(-(listed + 128) // 128) * 128
    vmem = pltpu.VMEM
    rows = n_lat * MSG
    scratch = [
        vmem((lc // 128, 12, BUF, 128), F32),
        vmem((4, 13, 2 * PAIRS, lc), BF16), vmem((4, 13, 2 * PAIRS, lc), BF16),
        vmem((9 * lc, hid), F32), vmem((4, 3 * lc, hid), BF16), vmem((4, 3 * lc, hid), BF16),
        vmem((9 * hid, hid), F32), vmem((4, 3 * hid, hid), BF16), vmem((4, 3 * hid, hid), BF16),
        vmem((1, hid), F32), vmem((1, hid), F32),
        vmem((2, 10, PAIRS, hid), F32), vmem((2, 10, PAIRS, hid), F32),
        vmem((4, 10, 32, hid), BF16), vmem((4, 10, 32, hid), BF16),
        vmem((512, hid), F32),
        vmem((patch, hid), F32), vmem((patch, hid), BF16), vmem((patch, hid), BF16),
        vmem((patch,), F32), vmem(land_sea.shape, jnp.int32), vmem(var_ok.shape, jnp.int32),
        vmem((1, variables), F32),
        vmem((1, padded), jnp.int32), vmem((1, padded), jnp.int32), vmem((1, padded), jnp.int32),
        vmem((slots, patch), F32), vmem((slots, patch), BF16), vmem((slots, patch), BF16),
        vmem((2 * slots, patch), BF16),
        vmem((128, patch), BF16), vmem((1, patch), F32),
        vmem((512, 128), BF16), vmem((n_lat * CAP, 128), BF16),
        vmem((n_lat * CAP, 512), BF16), vmem((512, n_lat * CAP), BF16), vmem((512, rows), BF16),
        vmem((rows, 128), BF16),
        vmem((128, n_lat * LCAP), BF16), vmem((128, 128), F32),
        vmem((n_lat, LCAP, 128), F32), vmem((n_lat, LCAP, 128), F32),
        vmem((n_lat, MSG, 128), F32), vmem((n_lat, MSG, 128), F32),
        vmem((hid // 128, 12, BUF, 128), F32),
        vmem((2, hid // 128, 16, 128), F32), vmem((2, hid // 128, 16, 128), F32),
        vmem((4, hid // 128, 4, 128), F32), vmem((4, hid // 128, 4, 128), F32),
        vmem((4, 13, 2 * PAIRS, hid), BF16), vmem((4, 13, 2 * PAIRS, hid), BF16),
        vmem((2, 10, PAIRS, hid), F32),
        vmem((4, 14, 32, hid), BF16), vmem((4, 14, 32, hid), BF16),
        pltpu.SemaphoreType.DMA((14,)),
        pltpu.SemaphoreType.DMA((10,)), pltpu.SemaphoreType.DMA((11,)),
        pltpu.SemaphoreType.DMA((10,)), pltpu.SemaphoreType.DMA((11,)),
    ] + [pltpu.SemaphoreType.DMA((1,))] * 4
    return pl.pallas_call(
        functools.partial(kernel, n_lon, n_lat, slots, patch, variables),
        out_shape=jax.ShapeDtypeStruct(latent.shape, F32),
        in_specs=[pl.BlockSpec(memory_space=pl.ANY)] * 14,
        out_specs=pl.BlockSpec(memory_space=pltpu.VMEM),
        scratch_shapes=scratch,
        compiler_params=pltpu.CompilerParams(
            collective_id=0, has_side_effects=True, vmem_limit_bytes=48 * 1024 * 1024),
    )(*(pltpu.with_memory_space_constraint(x, pltpu.HBM) for x in (
        latent, conv1_weight.reshape(9 * lc, hid), conv1_bias.reshape(1, hid), conv2_weight.reshape(9 * hid, hid),
      conv2_bias.reshape(1, hid), head_weight.T, head_bias, land_sea, var_ok,
      obs_error.reshape(1, variables), obs_band.reshape(1, listed), obs_cell, obs_count, obs_value[0])))


def solution(mesh):
    in_specs = (
        P("lat", "lon", None),
        P(),
        P(),
        P(),
        P(),
        P(),
        P(),
        P("lat", "lon"),
        P(),
        P(),
        P("lon", None, None),
        P("lon", None),
        P("lon", None),
        P("lon", "lat", None),
    )
    out_specs = P("lat", "lon", None)
    body = functools.partial(shards, mesh.shape["lon"], mesh.shape["lat"])
    return jax.shard_map(body, mesh=mesh, in_specs=in_specs, out_specs=out_specs, check_vma=False)
```

```python
import functools

import jax
import jax.numpy as jnp
from jax import lax
from jax.experimental import pallas as pl
from jax.experimental.pallas import tpu as pltpu
from jax.sharding import PartitionSpec as P

F32 = jnp.float32
BF16 = jnp.bfloat16
CAP = 12
MSG = 2 * CAP
LCAP = 16
GROUPS = ((0, 2, 0), (6, 8, 128), (2, 6, 256))
SIDE = 8
PAIRS = 40
BUF = 88
CHUNK = 512
MESH = pl.DeviceIdType.MESH


def halves(x):
    high = x.astype(BF16)
    return high, (x - high.astype(F32)).astype(BF16)


def nn(a, b):
    return lax.dot_general(a, b, (((1,), (0,)), ((), ())), preferred_element_type=F32)


def nt(a, b):
    return lax.dot_general(a, b, (((1,), (1,)), ((), ())), preferred_element_type=F32)


def gelu_parts(x):
    c = 0.7978845608028654
    t = jnp.tanh(c * (x + 0.044715 * x * x * x))
    return 0.5 * x * (1.0 + t), t


def gelu_slope(x):
    c = 0.7978845608028654
    t = jnp.tanh(c * (x + 0.044715 * x * x * x))
    return 0.5 * (1.0 + t) + 0.5 * x * (1.0 - t * t) * (c * (1.0 + 3.0 * 0.044715 * x * x))


def kernel(
    n_lon, n_lat, slots, patch, variables,
    latent, w1, b1, w2, b2, head, hbias, land, ok, err, band, cell, count, value,
    out,
    lat_ext, sa_hi, sa_lo, w1_v, w1_hi, w1_lo, w2_v, w2_hi, w2_lo, b1_v, b2_v,
    pre1, act1, sb_hi, sb_lo, pre2, head_v, head_hi, head_lo, hb_v, land_v, ok_v, err_v,
    band_v, cell_v, count_v, value_v, val_hi, val_lo, masked, ok_rows, inv_row,
    tiles_v, flags_w, oh, oht, oht_msg, pmt, from_land, own_weight, land_send, land_recv, term_send, term_recv,
    g_ext, side_send, side_recv, corner_send, corner_recv, sg_hi, sg_lo, p_ext, sp_hi, sp_lo,
    load_sem, h_send, h_recv, g_send, g_recv, l_send, l_recv, t_send, t_recv,
):
    lon, lat = lax.axis_index("lon"), lax.axis_index("lat")
    north = 1 - lax.div(lat + n_lat - 1, n_lat)
    south = lax.div(lat + 1, n_lat)
    northf, southf = north.astype(F32), south.astype(F32)
    hid = w1_v.shape[1]
    k1 = latent.shape[2]

    loads = [
        (band, band_v.at[:, 0:n_lat * slots]),
        (cell, cell_v.at[:, 0:n_lat * slots]),
        (count, count_v.at[:, 0:n_lat * slots]),
        (land, land_v),
        (latent, lat_ext.at[0, 2:10, SIDE:SIDE + 64, :]),
        (w1, w1_v),
        (b1, b1_v),
        (ok, ok_v),
        (err, err_v),
        (hbias, hb_v),
        (w2, w2_v),
        (b2, b2_v),
        (value, value_v),
        (head, head_v),
    ]
    copies = [pltpu.make_async_copy(s, d, load_sem.at[i]) for i, (s, d) in enumerate(loads)]
    (ld_band, ld_cell, ld_count, ld_land, ld_lat, ld_w1, ld_b1, ld_ok, ld_err, ld_hb, ld_w2, ld_b2, ld_value,
     ld_head) = copies
    for copy in copies[:5]:
        copy.start()

    half = n_lon // 2
    up_lat, down_lat = lat - 1 + north, lat + 1 - south
    around = []
    for dr in (-1, 0, 1):
        for dc in (-1, 0, 1):
            if dr == 0 and dc == 0:
                continue
            turn = half * north if dr < 0 else half * south if dr > 0 else 0
            to_lon = lax.rem(lon + dc + turn + n_lon, n_lon)
            to_lat = up_lat if dr < 0 else down_lat if dr > 0 else lat
            around.append((dr, dc, (to_lon, to_lat)))

    deep = n_lat // 2
    steps = [(far, step) for far in range(2) for step in range(deep) if far or step]
    steps.sort(key=lambda s: -(2 * s[0] + min(s[1], deep - s[1])))
    peers = [lax.rem(lax.div(lat, deep) + far, 2) * deep + lax.rem(lax.rem(lat, deep) + step, deep)
             for far, step in steps]

    barrier = pltpu.get_barrier_semaphore()
    for peer in peers:
        pl.semaphore_signal(barrier, inc=1, device_id=(lon, peer), device_id_type=MESH)
    for _, _, device in around:
        pl.semaphore_signal(barrier, inc=1, device_id=device, device_id_type=MESH)
    for copy in copies[5:]:
        copy.start()

    edges, corners, sides = range(3)
    parts = []
    for dr, dc, device in around:
        parts.append((corners if dr and dc else edges if dr else sides, dr, dc, device))

    def rim(buf, send_sem, recv_sem, kinds, drs=(-1, 0, 1)):
        sent = []
        for kind in kinds:
            for number, (its, dr, dc, device) in enumerate(parts):
                if its != kind or dr not in drs:
                    continue
                src_c = (SIDE, SIDE) if dc < 0 else (SIDE + 56, SIDE) if dc > 0 else (SIDE, 64)
                dst_c = 72 if dc < 0 else 0 if dc > 0 else SIDE
                if dr < 0:
                    src_r, dst_r, side = 2, 10 - 10 * north, 2 * (1 - north)
                elif dr > 0:
                    src_r, dst_r, side = 8, 10 * south, 2 * south
                else:
                    src_r, dst_r, side = 2, 2, 1
                length = 8 if kind == sides else 2
                slot = side * 3 + (1 - dc)
                src = buf.at[:, pl.ds(src_r, length), pl.ds(src_c[0], src_c[1]), :]
                dst = buf.at[:, pl.ds(dst_r, length), pl.ds(dst_c, src_c[1]), :]
                copy = pltpu.make_async_remote_copy(
                    src_ref=src, dst_ref=dst, send_sem=send_sem.at[number], recv_sem=recv_sem.at[slot],
                    device_id=device, device_id_type=MESH)
                copy.start()
                sent.append(copy)
        return sent

    def rim_arrived(buf, recv_sem, send_sem, kinds, drs=(-1, 0, 1)):
        for number, (kind, dr, dc, device) in enumerate(parts):
            if kind not in kinds or dr not in drs:
                continue
            cols_ = (0, SIDE) if dc < 0 else (72, SIDE) if dc > 0 else (SIDE, 64)
            at, length = (2, 8) if kind == sides else (0 if dr < 0 else 10, 2)
            ref = buf.at[:, pl.ds(at, length), pl.ds(cols_[0], cols_[1]), :]
            slot = (dr + 1) * 3 + dc + 1
            pltpu.make_async_remote_copy(
                src_ref=ref, dst_ref=ref, send_sem=send_sem.at[number], recv_sem=recv_sem.at[slot],
                device_id=device, device_id_type=MESH).wait_recv()

    def last_columns(dc):
        return SIDE if dc < 0 else SIDE + 62

    def halo_columns(dc):
        return SIDE - 2 if dc < 0 else 72

    def packed_rim(kind, its_dr, send_sem, recv_sem):
        sent = []
        for number, (its, dr, dc, device) in enumerate(parts):
            if its != kind or dr != its_dr:
                continue
            at = last_columns(dc)
            if kind == sides:
                mine_, theirs_, ref, into_ref = (dc + 1) // 2, (1 - dc) // 2, side_send, side_recv
                for h in range(hid // 128):
                    for j in range(2):
                        ref[mine_, h, 8 * j:8 * j + 8, :] = g_ext[h, 2:10, at + j:at + j + 1, :].reshape(8, 128)
                slot = 3 + (1 - dc)
            else:
                side = 2 - 2 * north if dr < 0 else 2 * south
                mine_, theirs_, ref, into_ref = dr + 1 + (dc + 1) // 2, side + (1 - dc) // 2, corner_send, corner_recv
                for h in range(hid // 128):
                    for r in range(2):
                        row_ = (2 if dr < 0 else 8) + r
                        ref[mine_, h, 2 * r:2 * r + 2, :] = g_ext[h, row_, at:at + 2, :]
                slot = side * 3 + (1 - dc)
            copy = pltpu.make_async_remote_copy(
                src_ref=ref.at[mine_], dst_ref=into_ref.at[theirs_], send_sem=send_sem.at[number],
                recv_sem=recv_sem.at[slot], device_id=device, device_id_type=MESH)
            copy.start()
            sent.append(copy)
        return sent

    def packed_arrived(kind, its_dr, send_sem, recv_sem):
        for number, (its, dr, dc, device) in enumerate(parts):
            if its != kind or dr != its_dr:
                continue
            at, slot = halo_columns(dc), (dr + 1) * 3 + dc + 1
            mine_ = (dc + 1) // 2 if kind == sides else dr + 1 + (dc + 1) // 2
            ref = side_recv if kind == sides else corner_recv
            pltpu.make_async_remote_copy(
                src_ref=ref.at[mine_], dst_ref=ref.at[mine_], send_sem=send_sem.at[number],
                recv_sem=recv_sem.at[slot], device_id=device, device_id_type=MESH).wait_recv()
            for h in range(hid // 128):
                for j in range(2):
                    if kind == sides:
                        g_ext[h, 2:10, at + j:at + j + 1, :] = ref[mine_, h, 8 * j:8 * j + 8, :].reshape(8, 1, 128)
                    else:
                        g_ext[h, (0 if dr < 0 else 10) + j, at:at + 2, :] = ref[mine_, h, 2 * j:2 * j + 2, :]

    def exchange(src, dst, send_sem, recv_sem):
        for peer in peers:
            pltpu.make_async_remote_copy(
                src_ref=src.at[peer], dst_ref=dst.at[lat], send_sem=send_sem.at[0], recv_sem=recv_sem.at[0],
                device_id=(lon, peer), device_id_type=MESH).start()
        dst[pl.ds(lat, 1)] = src[pl.ds(lat, 1)]
        every = pl.ds(0, len(peers))
        return pltpu.make_async_remote_copy(
            src_ref=src.at[every], dst_ref=dst.at[every], send_sem=send_sem.at[0], recv_sem=recv_sem.at[0],
            device_id=(lon, peers[0]), device_id_type=MESH)

    def split(src, high_ref, low_ref, step):
        def body(i, carry):
            at = pl.ds(pl.multiple_of(i * step, step), step)
            high_ref[at, :], low_ref[at, :] = halves(src[at, :])
            return carry
        lax.fori_loop(0, src.shape[0] // step, body, 0)

    def split_taps(src, high_ref, low_ref, depth, step):
        for i in range(3):
            def body(n, carry):
                g0, g1, g2 = (src[pl.ds(pl.multiple_of((3 * i + j) * depth + n * step, step), step), :] for j in range(3))
                outer, inner = 0.5 * (g0 + g2), 0.5 * g1
                at = pl.ds(pl.multiple_of(i * depth + n * step, step), step)
                for m, factor in enumerate((g0, outer + inner, outer - inner, g2)):
                    high_ref[m, at, :], low_ref[m, at, :] = halves(factor)
                return carry
            lax.fori_loop(0, depth // step, body, 0)

    def factors(d0, d1, d2, d3):
        return d0 - d2, d1 + d2, d2 - d1, d1 - d3

    def pair_rows(buf, at, length=1):
        def column(d):
            lanes = [buf[h, pl.ds(at, length), pl.ds(SIDE - 2 + d, PAIRS, stride=2), :] for h in range(buf.shape[0])]
            return jnp.concatenate(lanes, axis=2)
        return factors(*[column(d) for d in range(4)])

    def put_rows(high_ref, low_ref, at, pieces):
        for m, piece in enumerate(pieces):
            count_ = piece.shape[0] // 2
            high_ref[m, at:at + count_], low_ref[m, at:at + count_] = halves(
                piece.reshape(count_, 2 * PAIRS, piece.shape[2]))

    def joined(*rows_):
        return [jnp.concatenate(list(x), axis=0) for x in zip(*rows_)]

    def inner_rows(buf, high_ref, low_ref):
        pieces = pair_rows(buf, 2, 8)
        put_rows(high_ref, low_ref, 0, pieces)
        put_rows(high_ref, low_ref, 4, [x[1:7] for x in pieces])

    def pair_sums(taken_hi, taken_lo, weights, stacked=False):
        products = []
        for m in range(4):
            lhs, (wh, wl, dot) = taken_hi(m), weights(m)
            if stacked:
                both_ = dot(jnp.concatenate([lhs, taken_lo(m)], axis=0), wh)
                products.append(both_[:lhs.shape[0]] + both_[lhs.shape[0]:] + dot(lhs, wl))
            else:
                products.append(dot(lhs, wh) + dot(lhs, wl) + dot(taken_lo(m), wh))
        m0, m1, m2, m3 = products
        return m0 + m1 + m2, m1 - m2 - m3

    def taps(ref, chosen):
        def lhs(m):
            rows_ = [jnp.concatenate([ref[m, a:b] for a, b in part], axis=0) for part in chosen]
            return jnp.concatenate([x.reshape(x.shape[0] * x.shape[1], x.shape[2]) for x in rows_], axis=1)
        return lhs

    lat_ext[:, :, 80:88, :] = jnp.zeros((k1 // 128, 12, 8, 128), F32)
    g_ext[:, :, 72:88, :] = jnp.zeros((hid // 128, 12, 16, 128), F32)

    ld_band.wait()
    ld_cell.wait()
    ld_count.wait()
    lane = lax.broadcasted_iota(jnp.int32, (n_lat, 128), 1)
    live = lane < slots

    def blocks(ref):
        row = ref[...]
        return jnp.concatenate([row[:, slots * a:slots * a + 128] for a in range(n_lat)], axis=0)

    bands, cells, counts = blocks(band_v), blocks(cell_v), blocks(count_v)
    below = (lax.broadcasted_iota(jnp.int32, (128, 128), 0) < lax.broadcasted_iota(jnp.int32, (128, 128), 1))
    below = below.astype(F32).astype(BF16)
    mine = jnp.where(live & (bands == lat), 1.0, 0.0)
    pick = jnp.where(mine > 0.0, nn(mine.astype(BF16), below), -1.0)
    cell_row, odd, pair = cells >> 6, cells & 1, (cells & 63) >> 1
    edge = (cell_row << 5) + (odd << 6) + jnp.where(cell_row > 5, 128 - 6 * 32, 0)
    inner = (cell_row << 5) + (odd << 7) + (256 - 2 * 32)
    cells = pair + jnp.where((cell_row < 2) | (cell_row > 5), edge, inner)
    cellsf = cells.astype(F32) + 1.0
    countsf = counts.astype(F32) * 0.125
    msg_k = lax.rem(lax.broadcasted_iota(jnp.int32, (MSG, 128), 0), CAP).astype(F32)
    land_k = lax.broadcasted_iota(jnp.int32, (LCAP, 128), 0).astype(F32)
    named = [jnp.sum(jnp.where(pick[a:a + 1] == land_k, cellsf[a:a + 1], 0.0), axis=1, keepdims=True)
             for a in range(n_lat)]
    wanted = jnp.concatenate(named, axis=0).astype(jnp.int32) - 1
    lrows = n_lat * LCAP
    messages = jnp.where(wanted == lax.broadcasted_iota(jnp.int32, (lrows, 512), 1), 1.0, 0.0).astype(BF16)

    ld_land.wait()
    column = lax.broadcasted_iota(jnp.int32, (64, 512), 0)
    column = ((column & 31) << 1) + (column >> 5)
    fold = (lax.broadcasted_iota(jnp.int32, (64, 512), 1) >> 3) == column
    fold = jnp.where(fold, 1.0, 0.0).astype(BF16)
    kept = (lax.broadcasted_iota(jnp.int32, (8, 512), 1) & 7) == lax.broadcasted_iota(jnp.int32, (8, 512), 0)
    tiles = []
    for r in range(8):
        strip = land_v[8 * r:8 * r + 8, :].astype(F32)
        spread = jnp.concatenate([jnp.where(kept, strip[p:p + 1], 0.0) for p in range(8)], axis=0)
        tiles.append(nt(fold, spread.astype(BF16)))
    tiles = [tiles[r][32 * parity:32 * parity + 32] for first_, last, _ in GROUPS for parity in range(2) for r in range(first_, last)]
    tiles = jnp.concatenate(tiles, axis=0)
    tiles = jnp.concatenate([tiles, 1.0 - tiles], axis=1).astype(BF16)
    tiles_v[...] = tiles
    land_send[...] = nn(messages, tiles).reshape(n_lat, LCAP, 128)

    pl.semaphore_wait(barrier, len(around) + len(peers))
    land_sent = exchange(land_send, land_recv, l_send, l_recv)
    ld_lat.wait()
    rim1 = rim(lat_ext, h_send, h_recv, (sides, edges, corners))

    ld_w1.wait()
    split_taps(w1_v, w1_hi, w1_lo, k1, 64)

    first = lax.broadcasted_iota(jnp.int32, (MSG, 128), 0) < CAP
    taken = n_lat * CAP
    named, merged = [], []
    for q in range(n_lat // 2):
        def two(x):
            return jnp.where(first, x[2 * q:2 * q + 1], x[2 * q + 1:2 * q + 2])
        hit = two(pick) == msg_k
        named.append(jnp.sum(jnp.where(hit, two(cellsf), 0.0), axis=1, keepdims=True))
        merged.append(jnp.sum(jnp.where(hit, two(countsf), 0.0), axis=1, keepdims=True))
    wanted = jnp.concatenate(named, axis=0).astype(jnp.int32) - 1
    weight = jnp.concatenate(merged, axis=0)
    oh[...] = jnp.where(wanted == lax.broadcasted_iota(jnp.int32, (taken, 512), 1), 1.0, 0.0).astype(BF16)
    flags_w[...] = (nn(oh[...], tiles_v[...]) * weight).astype(BF16)

    own = lax.broadcasted_iota(jnp.int32, (n_lat, 128), 0) == lat
    own_band = jnp.sum(jnp.where(own, bands, 0), axis=0, keepdims=True)
    own_count = jnp.sum(jnp.where(own, countsf, 0.0), axis=0, keepdims=True)
    theirs = jnp.where(live & (own_band == lax.broadcasted_iota(jnp.int32, (n_lat, 128), 0)), 1.0, 0.0)
    place = jnp.where(theirs > 0.0, nn(theirs.astype(BF16), below), -1.0)
    pmt[...] = jnp.concatenate(
        [jnp.where(place[b:b + 1] == msg_k, 1.0, 0.0) for b in range(n_lat)], axis=0).astype(BF16)
    pml = jnp.concatenate([jnp.where(place[b:b + 1] == land_k, 1.0, 0.0) for b in range(n_lat)], axis=0)
    from_land[...] = jnp.transpose(pml).astype(BF16)
    own_weight[...] = jnp.transpose(jnp.broadcast_to(own_count, (128, 128)))

    ld_ok.wait()
    ld_err.wait()
    ld_hb.wait()
    ld_w2.wait()
    split_taps(w2_v, w2_hi, w2_lo, hid, 64)
    inv = 1.0 / (err_v[...] * err_v[...])
    inv_hi = inv.astype(BF16).astype(F32)
    inv_mid = (inv - inv_hi).astype(BF16).astype(F32)
    inv_lo = inv - inv_hi - inv_mid
    okf = ok_v[...].astype(F32)
    kind = lax.broadcasted_iota(jnp.int32, (16, variables), 0)
    table = jnp.where(kind == 0, inv_hi, jnp.where(kind == 1, inv_mid, jnp.where(kind == 2, inv_lo, 0.0)))
    table = table + jnp.where(kind == 3, okf[1:2], 0.0) + jnp.where(kind == 4, okf[0:1], 0.0)
    table = table.astype(BF16)
    spans = [(at, min(CHUNK, patch - at)) for at in range(0, patch, CHUNK)]
    for at, size in spans:
        place_ = lax.broadcasted_iota(jnp.int32, (1, size), 1) + at
        pixel = ((place_.astype(F32) + 0.5) * (1.0 / variables)).astype(jnp.int32)
        variable = place_ - pixel * variables
        chosen = lax.broadcasted_iota(jnp.int32, (variables, size), 0) == variable
        spread = nn(table, jnp.where(chosen, 1.0, 0.0).astype(BF16))
        inv_row[:, at:at + size] = spread[0:1] + spread[1:2] + spread[2:3]
        which = lax.broadcasted_iota(jnp.int32, (128, size), 0)
        seen = jnp.where(which == pixel, spread[3:4], jnp.where(which == pixel + 64, spread[4:5], 0.0))
        ok_rows[:, at:at + size] = seen.astype(BF16)
    ld_b1.wait()
    ld_b2.wait()
    ld_value.wait()
    for at, size in spans:
        span = slice(at, at + size)
        shifted = (value_v[:, span] - hb_v[span].reshape(1, size)) * inv_row[:, span]
        val_hi[:, span], val_lo[:, span] = halves(shifted)
    ld_head.wait()
    split(head_v, head_hi, head_lo, 96)

    rim_arrived(lat_ext, h_recv, h_send, (sides,))

    def forward1(m):
        return w1_hi[m], w1_lo[m], nn

    def put1(chosen, groups):
        for parity, summed in enumerate(pair_sums(taps(sa_hi, chosen), taps(sa_lo, chosen), forward1)):
            summed = summed + b1_v[...]
            act = gelu_parts(summed)[0]
            for source, target, length in groups:
                part = slice(source * PAIRS, (source + length) * PAIRS)
                pre1[parity, target:target + length] = summed[part].reshape(length, PAIRS, hid)
                act1[parity, target:target + length] = act[part].reshape(length, PAIRS, hid)

    inner_rows(lat_ext, sa_hi, sa_lo)
    put1((((0, 3),), ((4, 7),), ((1, 4),)), ((0, 2, 6),))

    land_sent.wait_recv()
    flags_own = nn(from_land[...], land_recv[...].reshape(lrows, 128).astype(BF16))
    flags_own = flags_own[:slots].astype(BF16)

    def back(high, low, at, size, total):
        count_ = high.shape[0]
        hh, hl = head_hi[at:at + size, :], head_lo[at:at + size, :]
        both = nn(jnp.concatenate([high, low], axis=0), hh)
        return total + both[:count_] + both[count_:] + nn(high, hl)

    for at, size in spans:
        span = slice(at, at + size)
        seen = nn(flags_own, ok_rows[:, span]).astype(BF16)
        masked[0:slots, span] = val_hi[:, span] * seen
        masked[slots:2 * slots, span] = val_lo[:, span] * seen
    cut = patch // 256 * 128
    shares = jnp.concatenate([own_weight[0:slots, :]] * (hid // 128), axis=1)
    terms = jnp.zeros((slots, hid), F32)
    for a, b in ((0, cut), (cut, patch)):
        both = nn(masked[:, a:b], head_hi[a:b, :])
        terms = terms + (both[:slots] + both[slots:] + nn(masked[0:slots, a:b], head_lo[a:b, :])) * shares
    high, low = halves(terms)
    both = jnp.concatenate([high, low], axis=1)
    if slots < 128:
        both = jnp.concatenate([both, jnp.zeros((128 - slots, 2 * hid), BF16)], axis=0)
    rows = n_lat * MSG
    upper = lax.rem(lax.broadcasted_iota(jnp.int32, (rows, 128), 0), MSG) < CAP
    sent_terms = nn(pmt[...], both)
    sent_terms = sent_terms[:, :hid] + sent_terms[:, hid:]
    term_send[...] = jnp.where(upper, sent_terms[:, :128], sent_terms[:, 128:]).reshape(n_lat, MSG, 128)
    terms_sent = exchange(term_send, term_recv, t_send, t_recv)

    rim_arrived(lat_ext, h_recv, h_send, (edges, corners))
    for at, one, other in (
        (7, 1 - north, 2), (8, 9, 10 + south),
        (9, 2 * north, 1 - north), (10, 8, 9 + south),
        (11, 2 - north, 3), (12, 10 + south, 11 - 2 * south),
    ):
        put_rows(sa_hi, sa_lo, at, joined(pair_rows(lat_ext, one), pair_rows(lat_ext, other)))
    put1((((9, 11),), ((7, 9),), ((11, 13),)), ((0, 0, 2), (2, 8, 2)))

    def near(ref, rows_=slice(0, 10)):
        return factors(ref[0, rows_, 0:32], ref[1, rows_, 0:32], ref[0, rows_, 1:33], ref[1, rows_, 1:33])

    for m, piece in enumerate(near(act1)):
        sb_hi[m], sb_lo[m] = halves(piece)

    def forward2(m):
        return w2_hi[m], w2_lo[m], nn

    chosen = tuple(((i, i + 8),) for i in range(3))
    summed = pair_sums(taps(sb_hi, chosen), taps(sb_lo, chosen), forward2)
    summed = [x[32 * first_:32 * last] for first_, last, _ in GROUPS for x in summed]
    summed = jnp.concatenate(summed, axis=0) + b2_v[...]
    pre2[...] = summed
    act2, _ = gelu_parts(summed)

    high, low = halves(act2)
    cols = nn(oh[...], jnp.concatenate([high, low], axis=1)).astype(BF16)
    cols_hi, cols_lo = cols[:, :hid], cols[:, hid:]
    cols_both = jnp.concatenate([cols_hi, cols_lo], axis=0)
    terms = jnp.zeros((taken, hid), F32)
    for at, size in spans:
        span = slice(at, at + size)
        both = nt(cols_both, head_hi[span, :])
        decoded = both[:taken] + both[taken:] + nt(cols_hi, head_lo[span, :])
        high, low = halves(nn(flags_w[...], ok_rows[:, span]) * inv_row[:, span] * decoded)
        terms = back(high, low, at, size, terms)

    wanted_row = jnp.transpose(jnp.broadcast_to(wanted.astype(F32), (taken, 128)))[0:1, :].astype(jnp.int32)
    oht[...] = jnp.where(wanted_row == lax.broadcasted_iota(jnp.int32, (512, taken), 0), 1.0, 0.0).astype(BF16)
    named = [jnp.sum(jnp.where(pick[a:a + 1] == msg_k, cellsf[a:a + 1], 0.0), axis=1, keepdims=True)
             for a in range(n_lat)]
    named = jnp.broadcast_to(jnp.concatenate(named, axis=0), (rows, 128))
    wanted_row = jnp.transpose(named)[0:1, :].astype(jnp.int32) - 1
    oht_msg[...] = jnp.where(wanted_row == lax.broadcasted_iota(jnp.int32, (512, rows), 0), 1.0, 0.0).astype(BF16)
    high, low = halves(terms)
    hidden = nn(oht[...], jnp.concatenate([high, low], axis=1))
    hidden = hidden[:, :hid] + hidden[:, hid:]
    pre2[...] = gelu_slope(pre2[...])
    pre1[...] = gelu_slope(pre1[...])
    for copy in rim1:
        copy.wait_send()
    land_sent.wait_send()

    terms_sent.wait_recv()

    came = term_recv[...].reshape(rows, 128)
    came = jnp.concatenate([jnp.where(upper, came, 0.0), jnp.where(upper, 0.0, came)], axis=1)
    high, low = halves(came)
    came = jnp.concatenate([high, low], axis=1)

    rim2 = []
    for (first_, last, base), dr in zip(GROUPS, (-1, 1, 0)):
        held = 32 * (last - first_)
        cells_ = slice(base, base + 2 * held)
        moved = nn(oht_msg[cells_, :], came)
        grad2 = (hidden[cells_] - moved[:, :hid] - moved[:, hid:]) * pre2[cells_, :]
        for parity in range(2):
            for h in range(hid // 128):
                g_ext[h, 2 + first_:2 + last, pl.ds(SIDE + parity, 32, stride=2), :] = (
                    grad2[held * parity:held * parity + held, 128 * h:128 * h + 128].reshape(last - first_, 32, 128))
        if dr:
            rim2 += rim(g_ext, g_send, g_recv, (edges,), (dr,))
            rim2 += packed_rim(corners, dr, g_send, g_recv)
        else:
            rim2 += packed_rim(sides, dr, g_send, g_recv)
    terms_sent.wait_send()

    packed_arrived(sides, 0, g_send, g_recv)

    def backward(high_ref, low_ref, depth):
        def weights(m):
            at = (3, 1, 2, 0)[m]
            return tuple(jnp.concatenate([ref[at, i * depth:(i + 1) * depth] for i in range(3)], axis=1)
                         for ref in (high_ref, low_ref)) + (nt,)
        return weights

    def put2(chosen, groups, stacked=False):
        sums = pair_sums(taps(sg_hi, chosen), taps(sg_lo, chosen), backward(w2_hi, w2_lo, hid), stacked)
        for parity, grad1 in enumerate(sums):
            for source, target, length in groups:
                part = grad1[source * PAIRS:(source + length) * PAIRS].reshape(length, PAIRS, hid)
                p_ext[parity, target:target + length] = part * pre1[parity, target:target + length]

    def scaled_by(x, factor):
        return [y * factor for y in x]

    def plus(x, y, factor):
        return [u + v * factor for u, v in zip(x, y)]

    def near_pairs(first_, last):
        rows_ = slice(first_, last)
        return factors(p_ext[0, rows_, 0:32], p_ext[1, rows_, 0:32], p_ext[0, rows_, 1:33], p_ext[1, rows_, 1:33])

    def put_pairs(first_, last, at):
        for m, piece in enumerate(near_pairs(first_, last)):
            sp_hi[m, at:at + last - first_], sp_lo[m, at:at + last - first_] = halves(piece)

    def put3(chosen, rows_):
        products = []
        for m in range(4):
            wh, wl, dot = backward(w1_hi, w1_lo, k1)(m)
            lhs = taps(sp_hi, chosen)(m)
            count_ = lhs.shape[0]
            both_ = dot(jnp.concatenate([lhs, taps(sp_lo, chosen)(m)], axis=0), jnp.concatenate([wh, wl], axis=0))
            products.append(both_[:count_, :k1] + both_[:count_, k1:] + both_[count_:, :k1])
        m0, m1, m2, m3 = products
        for parity, part in enumerate((m0 + m1 + m2, m1 - m2 - m3)):
            part = part.reshape(part.shape[0] // 32, 32, k1)
            done = 0
            for first_, last in rows_:
                out[first_:last, pl.ds(parity, 32, stride=2), :] = part[done:done + last - first_]
                done += last - first_

    inner_rows(g_ext, sg_hi, sg_lo)
    put2((((1, 4),), ((4, 7),), ((0, 3),)), ((0, 2, 6),))
    put_pairs(2, 8, 2)
    put3((((4, 8),), ((3, 7),), ((2, 6),)), ((2, 6),))
    rim_arrived(g_ext, g_recv, g_send, (edges,))
    packed_arrived(corners, 1, g_send, g_recv)
    packed_arrived(corners, -1, g_send, g_recv)
    r0, r1 = pair_rows(g_ext, north), pair_rows(g_ext, 1 - north)
    r10, r11 = pair_rows(g_ext, 10 + south), pair_rows(g_ext, 11 - south)
    put_rows(sg_hi, sg_lo, 7, joined(r1, pair_rows(g_ext, 2)))
    put_rows(sg_hi, sg_lo, 8, joined(pair_rows(g_ext, 9), r10))
    put_rows(sg_hi, sg_lo, 9, joined(plus(pair_rows(g_ext, 2), r0, northf), plus(pair_rows(g_ext, 3), r1, northf)))
    put_rows(sg_hi, sg_lo, 10, joined(scaled_by(r10, 1.0 - southf), scaled_by(r11, 1.0 - southf)))
    put_rows(sg_hi, sg_lo, 11, joined(scaled_by(r0, 1.0 - northf), scaled_by(r1, 1.0 - northf)))
    put_rows(sg_hi, sg_lo, 12, joined(plus(pair_rows(g_ext, 8), r10, southf), plus(pair_rows(g_ext, 9), r11, southf)))
    put2((((9, 11),), ((7, 9),), ((11, 13),)), ((0, 0, 2), (2, 8, 2)), True)

    for m, (q0, q1, q2, q7, q8, q9) in enumerate(zip(*[near_pairs(at, at + 1) for at in (0, 1, 2, 7, 8, 9)])):
        for at, piece in ((1, q1), (8, q8), (10, q2 + northf * q0), (11, q9 * (1.0 - southf)),
                          (12, q0 * (1.0 - northf)), (13, q7 + southf * q9)):
            sp_hi[m, at:at + 1], sp_lo[m, at:at + 1] = halves(piece)
    put3((((10, 11), (3, 4), (8, 9), (11, 12)), ((1, 3), (7, 9)), ((12, 13), (1, 2), (6, 7), (13, 14))),
         ((0, 2), (6, 8)))
    for copy in rim2:
        copy.wait_send()


def shards(n_lon, n_lat, latent, conv1_weight, conv1_bias, conv2_weight, conv2_bias, head_weight, head_bias, land_sea,
           var_ok, obs_error, obs_band, obs_cell, obs_count, obs_value):
    lc, hid = conv1_weight.shape[2], conv1_weight.shape[3]
    slots, patch = obs_value.shape[1], obs_value.shape[2]
    variables = var_ok.shape[1]
    listed = n_lat * slots
    padded = -(-(listed + 128) // 128) * 128
    vmem = pltpu.VMEM
    rows = n_lat * MSG
    scratch = [
        vmem((lc // 128, 12, BUF, 128), F32),
        vmem((4, 13, 2 * PAIRS, lc), BF16), vmem((4, 13, 2 * PAIRS, lc), BF16),
        vmem((9 * lc, hid), F32), vmem((4, 3 * lc, hid), BF16), vmem((4, 3 * lc, hid), BF16),
        vmem((9 * hid, hid), F32), vmem((4, 3 * hid, hid), BF16), vmem((4, 3 * hid, hid), BF16),
        vmem((1, hid), F32), vmem((1, hid), F32),
        vmem((2, 10, PAIRS, hid), F32), vmem((2, 10, PAIRS, hid), F32),
        vmem((4, 10, 32, hid), BF16), vmem((4, 10, 32, hid), BF16),
        vmem((512, hid), F32),
        vmem((patch, hid), F32), vmem((patch, hid), BF16), vmem((patch, hid), BF16),
        vmem((patch,), F32), vmem(land_sea.shape, jnp.int32), vmem(var_ok.shape, jnp.int32),
        vmem((1, variables), F32),
        vmem((1, padded), jnp.int32), vmem((1, padded), jnp.int32), vmem((1, padded), jnp.int32),
        vmem((slots, patch), F32), vmem((slots, patch), BF16), vmem((slots, patch), BF16),
        vmem((2 * slots, patch), BF16),
        vmem((128, patch), BF16), vmem((1, patch), F32),
        vmem((512, 128), BF16), vmem((n_lat * CAP, 128), BF16),
        vmem((n_lat * CAP, 512), BF16), vmem((512, n_lat * CAP), BF16), vmem((512, rows), BF16),
        vmem((rows, 128), BF16),
        vmem((128, n_lat * LCAP), BF16), vmem((128, 128), F32),
        vmem((n_lat, LCAP, 128), F32), vmem((n_lat, LCAP, 128), F32),
        vmem((n_lat, MSG, 128), F32), vmem((n_lat, MSG, 128), F32),
        vmem((hid // 128, 12, BUF, 128), F32),
        vmem((2, hid // 128, 16, 128), F32), vmem((2, hid // 128, 16, 128), F32),
        vmem((4, hid // 128, 4, 128), F32), vmem((4, hid // 128, 4, 128), F32),
        vmem((4, 13, 2 * PAIRS, hid), BF16), vmem((4, 13, 2 * PAIRS, hid), BF16),
        vmem((2, 10, PAIRS, hid), F32),
        vmem((4, 14, 32, hid), BF16), vmem((4, 14, 32, hid), BF16),
        pltpu.SemaphoreType.DMA((14,)),
        pltpu.SemaphoreType.DMA((8,)), pltpu.SemaphoreType.DMA((9,)),
        pltpu.SemaphoreType.DMA((8,)), pltpu.SemaphoreType.DMA((9,)),
    ] + [pltpu.SemaphoreType.DMA((1,))] * 4
    return pl.pallas_call(
        functools.partial(kernel, n_lon, n_lat, slots, patch, variables),
        out_shape=jax.ShapeDtypeStruct(latent.shape, F32),
        in_specs=[pl.BlockSpec(memory_space=pl.ANY)] * 14,
        out_specs=pl.BlockSpec(memory_space=pltpu.VMEM),
        scratch_shapes=scratch,
        compiler_params=pltpu.CompilerParams(
            collective_id=0, has_side_effects=True, vmem_limit_bytes=48 * 1024 * 1024),
    )(*(pltpu.with_memory_space_constraint(x, pltpu.HBM) for x in (
        latent, conv1_weight.reshape(9 * lc, hid), conv1_bias.reshape(1, hid), conv2_weight.reshape(9 * hid, hid),
      conv2_bias.reshape(1, hid), head_weight.T, head_bias, land_sea, var_ok,
      obs_error.reshape(1, variables), obs_band.reshape(1, listed), obs_cell, obs_count, obs_value[0])))


def solution(mesh):
    in_specs = (
        P("lat", "lon", None),
        P(),
        P(),
        P(),
        P(),
        P(),
        P(),
        P("lat", "lon"),
        P(),
        P(),
        P("lon", None, None),
        P("lon", None),
        P("lon", None),
        P("lon", "lat", None),
    )
    out_specs = P("lat", "lon", None)
    body = functools.partial(shards, mesh.shape["lon"], mesh.shape["lat"])
    return jax.shard_map(body, mesh=mesh, in_specs=in_specs, out_specs=out_specs, check_vma=False)
```

```python
import functools

import jax
import jax.numpy as jnp
from jax import lax
from jax.experimental import pallas as pl
from jax.experimental.pallas import tpu as pltpu
from jax.sharding import PartitionSpec as P

F32 = jnp.float32
BF16 = jnp.bfloat16
CAP = 12
MSG = 2 * CAP
LCAP = 16
GROUPS = ((0, 2, 0), (6, 8, 128), (2, 6, 256))
SIDE = 8
PAIRS = 40
BUF = 88
CHUNK = 512
MESH = pl.DeviceIdType.MESH


def halves(x):
    high = x.astype(BF16)
    return high, (x - high.astype(F32)).astype(BF16)


def nn(a, b):
    return lax.dot_general(a, b, (((1,), (0,)), ((), ())), preferred_element_type=F32)


def nt(a, b):
    return lax.dot_general(a, b, (((1,), (1,)), ((), ())), preferred_element_type=F32)


def gelu_parts(x):
    c = 0.7978845608028654
    t = jnp.tanh(c * (x + 0.044715 * x * x * x))
    return 0.5 * x * (1.0 + t), t


def gelu_slope(x):
    c = 0.7978845608028654
    t = jnp.tanh(c * (x + 0.044715 * x * x * x))
    return 0.5 * (1.0 + t) + 0.5 * x * (1.0 - t * t) * (c * (1.0 + 3.0 * 0.044715 * x * x))


def kernel(
    n_lon, n_lat, slots, patch, variables,
    latent, w1, b1, w2, b2, head, hbias, land, ok, err, band, cell, count, value,
    out,
    lat_ext, sa_hi, sa_lo, w1_v, w1_hi, w1_lo, w2_v, w2_hi, w2_lo, b1_v, b2_v,
    pre1, act1, sb_hi, sb_lo, pre2, head_v, head_hi, head_lo, hb_v, land_v, ok_v, err_v,
    band_v, cell_v, count_v, value_v, val_hi, val_lo, masked, ok_rows, inv_row,
    tiles_v, flags_w, oh, oht, oht_msg, pmt, from_land, own_weight, land_send, land_recv, term_send, term_recv,
    g_ext, side_send, side_recv, corner_send, corner_recv, sg_hi, sg_lo, p_ext, sp_hi, sp_lo,
    load_sem, h_send, h_recv, g_send, g_recv, l_send, l_recv, t_send, t_recv,
):
    lon, lat = lax.axis_index("lon"), lax.axis_index("lat")
    north = 1 - lax.div(lat + n_lat - 1, n_lat)
    south = lax.div(lat + 1, n_lat)
    northf, southf = north.astype(F32), south.astype(F32)
    hid = w1_v.shape[1]
    k1 = latent.shape[2]

    loads = [
        (land, land_v),
        (band, band_v.at[:, 0:n_lat * slots]),
        (cell, cell_v.at[:, 0:n_lat * slots]),
        (count, count_v.at[:, 0:n_lat * slots]),
        (latent, lat_ext.at[0, 2:10, SIDE:SIDE + 64, :]),
        (w1, w1_v),
        (b1, b1_v),
        (ok, ok_v),
        (err, err_v),
        (hbias, hb_v),
        (w2, w2_v),
        (b2, b2_v),
        (value, value_v),
        (head, head_v),
    ]
    copies = [pltpu.make_async_copy(s, d, load_sem.at[i]) for i, (s, d) in enumerate(loads)]
    (ld_land, ld_band, ld_cell, ld_count, ld_lat, ld_w1, ld_b1, ld_ok, ld_err, ld_hb, ld_w2, ld_b2, ld_value,
     ld_head) = copies
    for copy in copies[:5]:
        copy.start()

    half = n_lon // 2
    up_lat, down_lat = lat - 1 + north, lat + 1 - south
    around = []
    for dr in (-1, 0, 1):
        for dc in (-1, 0, 1):
            if dr == 0 and dc == 0:
                continue
            turn = half * north if dr < 0 else half * south if dr > 0 else 0
            to_lon = lax.rem(lon + dc + turn + n_lon, n_lon)
            to_lat = up_lat if dr < 0 else down_lat if dr > 0 else lat
            around.append((dr, dc, (to_lon, to_lat)))

    deep = n_lat // 2
    steps = [(far, step) for far in range(2) for step in range(deep) if far or step]
    steps.sort(key=lambda s: -(2 * s[0] + min(s[1], deep - s[1])))
    peers = [lax.rem(lax.div(lat, deep) + far, 2) * deep + lax.rem(lax.rem(lat, deep) + step, deep)
             for far, step in steps]

    barrier = pltpu.get_barrier_semaphore()
    for peer in peers:
        pl.semaphore_signal(barrier, inc=1, device_id=(lon, peer), device_id_type=MESH)
    for _, _, device in around:
        pl.semaphore_signal(barrier, inc=1, device_id=device, device_id_type=MESH)
    for copy in copies[5:]:
        copy.start()

    edges, corners, sides = range(3)
    parts = []
    for dr, dc, device in around:
        parts.append((corners if dr and dc else edges if dr else sides, dr, dc, device))

    def rim(buf, send_sem, recv_sem, kinds, drs=(-1, 0, 1)):
        sent = []
        for kind in kinds:
            for number, (its, dr, dc, device) in enumerate(parts):
                if its != kind or dr not in drs:
                    continue
                src_c = (SIDE, SIDE) if dc < 0 else (SIDE + 56, SIDE) if dc > 0 else (SIDE, 64)
                dst_c = 72 if dc < 0 else 0 if dc > 0 else SIDE
                if dr < 0:
                    src_r, dst_r, side = 2, 10 - 10 * north, 2 * (1 - north)
                elif dr > 0:
                    src_r, dst_r, side = 8, 10 * south, 2 * south
                else:
                    src_r, dst_r, side = 2, 2, 1
                length = 8 if kind == sides else 2
                slot = side * 3 + (1 - dc)
                src = buf.at[:, pl.ds(src_r, length), pl.ds(src_c[0], src_c[1]), :]
                dst = buf.at[:, pl.ds(dst_r, length), pl.ds(dst_c, src_c[1]), :]
                copy = pltpu.make_async_remote_copy(
                    src_ref=src, dst_ref=dst, send_sem=send_sem.at[number], recv_sem=recv_sem.at[slot],
                    device_id=device, device_id_type=MESH)
                copy.start()
                sent.append(copy)
        return sent

    def rim_arrived(buf, recv_sem, send_sem, kinds, drs=(-1, 0, 1)):
        for number, (kind, dr, dc, device) in enumerate(parts):
            if kind not in kinds or dr not in drs:
                continue
            cols_ = (0, SIDE) if dc < 0 else (72, SIDE) if dc > 0 else (SIDE, 64)
            at, length = (2, 8) if kind == sides else (0 if dr < 0 else 10, 2)
            ref = buf.at[:, pl.ds(at, length), pl.ds(cols_[0], cols_[1]), :]
            slot = (dr + 1) * 3 + dc + 1
            pltpu.make_async_remote_copy(
                src_ref=ref, dst_ref=ref, send_sem=send_sem.at[number], recv_sem=recv_sem.at[slot],
                device_id=device, device_id_type=MESH).wait_recv()

    def last_columns(dc):
        return SIDE if dc < 0 else SIDE + 62

    def halo_columns(dc):
        return SIDE - 2 if dc < 0 else 72

    def packed_rim(kind, its_dr, send_sem, recv_sem):
        sent = []
        for number, (its, dr, dc, device) in enumerate(parts):
            if its != kind or dr != its_dr:
                continue
            at = last_columns(dc)
            if kind == sides:
                mine_, theirs_, ref, into_ref = (dc + 1) // 2, (1 - dc) // 2, side_send, side_recv
                for h in range(hid // 128):
                    for j in range(2):
                        ref[mine_, h, 8 * j:8 * j + 8, :] = g_ext[h, 2:10, at + j:at + j + 1, :].reshape(8, 128)
                slot = 3 + (1 - dc)
            else:
                side = 2 - 2 * north if dr < 0 else 2 * south
                mine_, theirs_, ref, into_ref = dr + 1 + (dc + 1) // 2, side + (1 - dc) // 2, corner_send, corner_recv
                for h in range(hid // 128):
                    for r in range(2):
                        row_ = (2 if dr < 0 else 8) + r
                        ref[mine_, h, 2 * r:2 * r + 2, :] = g_ext[h, row_, at:at + 2, :]
                slot = side * 3 + (1 - dc)
            copy = pltpu.make_async_remote_copy(
                src_ref=ref.at[mine_], dst_ref=into_ref.at[theirs_], send_sem=send_sem.at[number],
                recv_sem=recv_sem.at[slot], device_id=device, device_id_type=MESH)
            copy.start()
            sent.append(copy)
        return sent

    def packed_arrived(kind, its_dr, send_sem, recv_sem):
        for number, (its, dr, dc, device) in enumerate(parts):
            if its != kind or dr != its_dr:
                continue
            at, slot = halo_columns(dc), (dr + 1) * 3 + dc + 1
            mine_ = (dc + 1) // 2 if kind == sides else dr + 1 + (dc + 1) // 2
            ref = side_recv if kind == sides else corner_recv
            pltpu.make_async_remote_copy(
                src_ref=ref.at[mine_], dst_ref=ref.at[mine_], send_sem=send_sem.at[number],
                recv_sem=recv_sem.at[slot], device_id=device, device_id_type=MESH).wait_recv()
            for h in range(hid // 128):
                for j in range(2):
                    if kind == sides:
                        g_ext[h, 2:10, at + j:at + j + 1, :] = ref[mine_, h, 8 * j:8 * j + 8, :].reshape(8, 1, 128)
                    else:
                        g_ext[h, (0 if dr < 0 else 10) + j, at:at + 2, :] = ref[mine_, h, 2 * j:2 * j + 2, :]

    def exchange(src, dst, send_sem, recv_sem):
        for peer in peers:
            pltpu.make_async_remote_copy(
                src_ref=src.at[peer], dst_ref=dst.at[lat], send_sem=send_sem.at[0], recv_sem=recv_sem.at[0],
                device_id=(lon, peer), device_id_type=MESH).start()
        dst[pl.ds(lat, 1)] = src[pl.ds(lat, 1)]
        every = pl.ds(0, len(peers))
        return pltpu.make_async_remote_copy(
            src_ref=src.at[every], dst_ref=dst.at[every], send_sem=send_sem.at[0], recv_sem=recv_sem.at[0],
            device_id=(lon, peers[0]), device_id_type=MESH)

    def split(src, high_ref, low_ref, step):
        def body(i, carry):
            at = pl.ds(pl.multiple_of(i * step, step), step)
            high_ref[at, :], low_ref[at, :] = halves(src[at, :])
            return carry
        lax.fori_loop(0, src.shape[0] // step, body, 0)

    def split_taps(src, high_ref, low_ref, depth, step):
        for i in range(3):
            def body(n, carry):
                g0, g1, g2 = (src[pl.ds(pl.multiple_of((3 * i + j) * depth + n * step, step), step), :] for j in range(3))
                outer, inner = 0.5 * (g0 + g2), 0.5 * g1
                at = pl.ds(pl.multiple_of(i * depth + n * step, step), step)
                for m, factor in enumerate((g0, outer + inner, outer - inner, g2)):
                    high_ref[m, at, :], low_ref[m, at, :] = halves(factor)
                return carry
            lax.fori_loop(0, depth // step, body, 0)

    def factors(d0, d1, d2, d3):
        return d0 - d2, d1 + d2, d2 - d1, d1 - d3

    def pair_rows(buf, at, length=1):
        def column(d):
            lanes = [buf[h, pl.ds(at, length), pl.ds(SIDE - 2 + d, PAIRS, stride=2), :] for h in range(buf.shape[0])]
            return jnp.concatenate(lanes, axis=2)
        return factors(*[column(d) for d in range(4)])

    def put_rows(high_ref, low_ref, at, pieces):
        for m, piece in enumerate(pieces):
            count_ = piece.shape[0] // 2
            high_ref[m, at:at + count_], low_ref[m, at:at + count_] = halves(
                piece.reshape(count_, 2 * PAIRS, piece.shape[2]))

    def joined(*rows_):
        return [jnp.concatenate(list(x), axis=0) for x in zip(*rows_)]

    def inner_rows(buf, high_ref, low_ref):
        pieces = pair_rows(buf, 2, 8)
        put_rows(high_ref, low_ref, 0, pieces)
        put_rows(high_ref, low_ref, 4, [x[1:7] for x in pieces])

    def pair_sums(taken_hi, taken_lo, weights, stacked=False):
        products = []
        for m in range(4):
            lhs, (wh, wl, dot) = taken_hi(m), weights(m)
            if stacked:
                both_ = dot(jnp.concatenate([lhs, taken_lo(m)], axis=0), wh)
                products.append(both_[:lhs.shape[0]] + both_[lhs.shape[0]:] + dot(lhs, wl))
            else:
                products.append(dot(lhs, wh) + dot(lhs, wl) + dot(taken_lo(m), wh))
        m0, m1, m2, m3 = products
        return m0 + m1 + m2, m1 - m2 - m3

    def taps(ref, chosen):
        def lhs(m):
            rows_ = [jnp.concatenate([ref[m, a:b] for a, b in part], axis=0) for part in chosen]
            return jnp.concatenate([x.reshape(x.shape[0] * x.shape[1], x.shape[2]) for x in rows_], axis=1)
        return lhs

    lat_ext[:, :, 80:88, :] = jnp.zeros((k1 // 128, 12, 8, 128), F32)
    g_ext[:, :, 72:88, :] = jnp.zeros((hid // 128, 12, 16, 128), F32)

    ld_band.wait()
    ld_cell.wait()
    ld_land.wait()
    lane = lax.broadcasted_iota(jnp.int32, (n_lat, 128), 1)
    live = lane < slots

    def blocks(ref):
        row = ref[...]
        return jnp.concatenate([row[:, slots * a:slots * a + 128] for a in range(n_lat)], axis=0)

    bands, cells = blocks(band_v), blocks(cell_v)
    below = (lax.broadcasted_iota(jnp.int32, (128, 128), 0) < lax.broadcasted_iota(jnp.int32, (128, 128), 1))
    below = below.astype(F32).astype(BF16)
    mine = jnp.where(live & (bands == lat), 1.0, 0.0)
    pick = jnp.where(mine > 0.0, nn(mine.astype(BF16), below), -1.0)
    cell_row, odd, pair = cells >> 6, cells & 1, (cells & 63) >> 1
    edge = (cell_row << 5) + (odd << 6) + jnp.where(cell_row > 5, 128 - 6 * 32, 0)
    inner = (cell_row << 5) + (odd << 7) + (256 - 2 * 32)
    cells = pair + jnp.where((cell_row < 2) | (cell_row > 5), edge, inner)
    cellsf = cells.astype(F32) + 1.0
    msg_k = lax.rem(lax.broadcasted_iota(jnp.int32, (MSG, 128), 0), CAP).astype(F32)
    land_k = lax.broadcasted_iota(jnp.int32, (LCAP, 128), 0).astype(F32)
    named = [jnp.sum(jnp.where(pick[a:a + 1] == land_k, cellsf[a:a + 1], 0.0), axis=1, keepdims=True)
             for a in range(n_lat)]
    wanted = jnp.concatenate(named, axis=0).astype(jnp.int32) - 1
    lrows = n_lat * LCAP
    messages = jnp.where(wanted == lax.broadcasted_iota(jnp.int32, (lrows, 512), 1), 1.0, 0.0).astype(BF16)

    column = lax.broadcasted_iota(jnp.int32, (64, 512), 0)
    column = ((column & 31) << 1) + (column >> 5)
    fold = (lax.broadcasted_iota(jnp.int32, (64, 512), 1) >> 3) == column
    fold = jnp.where(fold, 1.0, 0.0).astype(BF16)
    kept = (lax.broadcasted_iota(jnp.int32, (8, 512), 1) & 7) == lax.broadcasted_iota(jnp.int32, (8, 512), 0)
    tiles = []
    for r in range(8):
        strip = land_v[8 * r:8 * r + 8, :].astype(F32)
        spread = jnp.concatenate([jnp.where(kept, strip[p:p + 1], 0.0) for p in range(8)], axis=0)
        tiles.append(nt(fold, spread.astype(BF16)))
    tiles = [tiles[r][32 * parity:32 * parity + 32] for first_, last, _ in GROUPS for parity in range(2) for r in range(first_, last)]
    tiles = jnp.concatenate(tiles, axis=0)
    tiles = jnp.concatenate([tiles, 1.0 - tiles], axis=1).astype(BF16)
    tiles_v[...] = tiles
    land_send[...] = nn(messages, tiles).reshape(n_lat, LCAP, 128)

    pl.semaphore_wait(barrier, len(around) + len(peers))
    land_sent = exchange(land_send, land_recv, l_send, l_recv)
    ld_lat.wait()
    rim1 = rim(lat_ext, h_send, h_recv, (sides, corners, edges))

    ld_w1.wait()
    split_taps(w1_v, w1_hi, w1_lo, k1, 64)

    ld_count.wait()
    countsf = blocks(count_v).astype(F32) * 0.125
    first = lax.broadcasted_iota(jnp.int32, (MSG, 128), 0) < CAP
    taken = n_lat * CAP
    named, merged = [], []
    for q in range(n_lat // 2):
        def two(x):
            return jnp.where(first, x[2 * q:2 * q + 1], x[2 * q + 1:2 * q + 2])
        hit = two(pick) == msg_k
        named.append(jnp.sum(jnp.where(hit, two(cellsf), 0.0), axis=1, keepdims=True))
        merged.append(jnp.sum(jnp.where(hit, two(countsf), 0.0), axis=1, keepdims=True))
    wanted = jnp.concatenate(named, axis=0).astype(jnp.int32) - 1
    weight = jnp.concatenate(merged, axis=0)
    oh[...] = jnp.where(wanted == lax.broadcasted_iota(jnp.int32, (taken, 512), 1), 1.0, 0.0).astype(BF16)
    flags_w[...] = (nn(oh[...], tiles_v[...]) * weight).astype(BF16)

    own = lax.broadcasted_iota(jnp.int32, (n_lat, 128), 0) == lat
    own_band = jnp.sum(jnp.where(own, bands, 0), axis=0, keepdims=True)
    own_count = jnp.sum(jnp.where(own, countsf, 0.0), axis=0, keepdims=True)
    theirs = jnp.where(live & (own_band == lax.broadcasted_iota(jnp.int32, (n_lat, 128), 0)), 1.0, 0.0)
    place = jnp.where(theirs > 0.0, nn(theirs.astype(BF16), below), -1.0)
    pmt[...] = jnp.concatenate(
        [jnp.where(place[b:b + 1] == msg_k, 1.0, 0.0) for b in range(n_lat)], axis=0).astype(BF16)
    pml = jnp.concatenate([jnp.where(place[b:b + 1] == land_k, 1.0, 0.0) for b in range(n_lat)], axis=0)
    from_land[...] = jnp.transpose(pml).astype(BF16)
    own_weight[...] = jnp.transpose(jnp.broadcast_to(own_count, (128, 128)))

    ld_ok.wait()
    ld_err.wait()
    ld_hb.wait()
    ld_w2.wait()
    split_taps(w2_v, w2_hi, w2_lo, hid, 64)
    inv = 1.0 / (err_v[...] * err_v[...])
    inv_hi = inv.astype(BF16).astype(F32)
    inv_mid = (inv - inv_hi).astype(BF16).astype(F32)
    inv_lo = inv - inv_hi - inv_mid
    okf = ok_v[...].astype(F32)
    kind = lax.broadcasted_iota(jnp.int32, (16, variables), 0)
    table = jnp.where(kind == 0, inv_hi, jnp.where(kind == 1, inv_mid, jnp.where(kind == 2, inv_lo, 0.0)))
    table = table + jnp.where(kind == 3, okf[1:2], 0.0) + jnp.where(kind == 4, okf[0:1], 0.0)
    table = table.astype(BF16)
    spans = [(at, min(CHUNK, patch - at)) for at in range(0, patch, CHUNK)]
    for at, size in spans:
        place_ = lax.broadcasted_iota(jnp.int32, (1, size), 1) + at
        pixel = ((place_.astype(F32) + 0.5) * (1.0 / variables)).astype(jnp.int32)
        variable = place_ - pixel * variables
        chosen = lax.broadcasted_iota(jnp.int32, (variables, size), 0) == variable
        spread = nn(table, jnp.where(chosen, 1.0, 0.0).astype(BF16))
        inv_row[:, at:at + size] = spread[0:1] + spread[1:2] + spread[2:3]
        which = lax.broadcasted_iota(jnp.int32, (128, size), 0)
        seen = jnp.where(which == pixel, spread[3:4], jnp.where(which == pixel + 64, spread[4:5], 0.0))
        ok_rows[:, at:at + size] = seen.astype(BF16)
    ld_b1.wait()
    ld_b2.wait()
    ld_value.wait()
    for at, size in spans:
        span = slice(at, at + size)
        shifted = (value_v[:, span] - hb_v[span].reshape(1, size)) * inv_row[:, span]
        val_hi[:, span], val_lo[:, span] = halves(shifted)
    ld_head.wait()
    split(head_v, head_hi, head_lo, 96)

    rim_arrived(lat_ext, h_recv, h_send, (sides,))

    def forward1(m):
        return w1_hi[m], w1_lo[m], nn

    def put1(chosen, groups):
        for parity, summed in enumerate(pair_sums(taps(sa_hi, chosen), taps(sa_lo, chosen), forward1)):
            summed = summed + b1_v[...]
            act = gelu_parts(summed)[0]
            for source, target, length in groups:
                part = slice(source * PAIRS, (source + length) * PAIRS)
                pre1[parity, target:target + length] = summed[part].reshape(length, PAIRS, hid)
                act1[parity, target:target + length] = act[part].reshape(length, PAIRS, hid)

    inner_rows(lat_ext, sa_hi, sa_lo)
    put1((((0, 3),), ((4, 7),), ((1, 4),)), ((0, 2, 6),))

    land_sent.wait_recv()
    flags_own = nn(from_land[...], land_recv[...].reshape(lrows, 128).astype(BF16))
    flags_own = flags_own[:slots].astype(BF16)

    def back(high, low, at, size, total):
        count_ = high.shape[0]
        hh, hl = head_hi[at:at + size, :], head_lo[at:at + size, :]
        both = nn(jnp.concatenate([high, low], axis=0), hh)
        return total + both[:count_] + both[count_:] + nn(high, hl)

    for at, size in spans:
        span = slice(at, at + size)
        seen = nn(flags_own, ok_rows[:, span]).astype(BF16)
        masked[0:slots, span] = val_hi[:, span] * seen
        masked[slots:2 * slots, span] = val_lo[:, span] * seen
    cut = patch // 256 * 128
    shares = jnp.concatenate([own_weight[0:slots, :]] * (hid // 128), axis=1)
    terms = jnp.zeros((slots, hid), F32)
    for a, b in ((0, cut), (cut, patch)):
        both = nn(masked[:, a:b], head_hi[a:b, :])
        terms = terms + (both[:slots] + both[slots:] + nn(masked[0:slots, a:b], head_lo[a:b, :])) * shares
    high, low = halves(terms)
    both = jnp.concatenate([high, low], axis=1)
    if slots < 128:
        both = jnp.concatenate([both, jnp.zeros((128 - slots, 2 * hid), BF16)], axis=0)
    rows = n_lat * MSG
    upper = lax.rem(lax.broadcasted_iota(jnp.int32, (rows, 128), 0), MSG) < CAP
    sent_terms = nn(pmt[...], both)
    sent_terms = sent_terms[:, :hid] + sent_terms[:, hid:]
    term_send[...] = jnp.where(upper, sent_terms[:, :128], sent_terms[:, 128:]).reshape(n_lat, MSG, 128)
    terms_sent = exchange(term_send, term_recv, t_send, t_recv)

    rim_arrived(lat_ext, h_recv, h_send, (edges, corners))
    for at, one, other in (
        (7, 1 - north, 2), (8, 9, 10 + south),
        (9, 2 * north, 1 - north), (10, 8, 9 + south),
        (11, 2 - north, 3), (12, 10 + south, 11 - 2 * south),
    ):
        put_rows(sa_hi, sa_lo, at, joined(pair_rows(lat_ext, one), pair_rows(lat_ext, other)))
    put1((((9, 11),), ((7, 9),), ((11, 13),)), ((0, 0, 2), (2, 8, 2)))

    def near(ref, rows_=slice(0, 10)):
        return factors(ref[0, rows_, 0:32], ref[1, rows_, 0:32], ref[0, rows_, 1:33], ref[1, rows_, 1:33])

    for m, piece in enumerate(near(act1)):
        sb_hi[m], sb_lo[m] = halves(piece)

    def forward2(m):
        return w2_hi[m], w2_lo[m], nn

    chosen = tuple(((i, i + 8),) for i in range(3))
    summed = pair_sums(taps(sb_hi, chosen), taps(sb_lo, chosen), forward2)
    summed = [x[32 * first_:32 * last] for first_, last, _ in GROUPS for x in summed]
    summed = jnp.concatenate(summed, axis=0) + b2_v[...]
    pre2[...] = summed
    act2, _ = gelu_parts(summed)

    high, low = halves(act2)
    cols = nn(oh[...], jnp.concatenate([high, low], axis=1)).astype(BF16)
    cols_hi, cols_lo = cols[:, :hid], cols[:, hid:]
    cols_both = jnp.concatenate([cols_hi, cols_lo], axis=0)
    terms = jnp.zeros((taken, hid), F32)
    for at, size in spans:
        span = slice(at, at + size)
        both = nt(cols_both, head_hi[span, :])
        decoded = both[:taken] + both[taken:] + nt(cols_hi, head_lo[span, :])
        high, low = halves(nn(flags_w[...], ok_rows[:, span]) * inv_row[:, span] * decoded)
        terms = back(high, low, at, size, terms)

    wanted_row = jnp.transpose(jnp.broadcast_to(wanted.astype(F32), (taken, 128)))[0:1, :].astype(jnp.int32)
    oht[...] = jnp.where(wanted_row == lax.broadcasted_iota(jnp.int32, (512, taken), 0), 1.0, 0.0).astype(BF16)
    named = [jnp.sum(jnp.where(pick[a:a + 1] == msg_k, cellsf[a:a + 1], 0.0), axis=1, keepdims=True)
             for a in range(n_lat)]
    named = jnp.broadcast_to(jnp.concatenate(named, axis=0), (rows, 128))
    wanted_row = jnp.transpose(named)[0:1, :].astype(jnp.int32) - 1
    oht_msg[...] = jnp.where(wanted_row == lax.broadcasted_iota(jnp.int32, (512, rows), 0), 1.0, 0.0).astype(BF16)
    high, low = halves(terms)
    hidden = nn(oht[...], jnp.concatenate([high, low], axis=1))
    hidden = hidden[:, :hid] + hidden[:, hid:]
    pre2[...] = gelu_slope(pre2[...])
    pre1[...] = gelu_slope(pre1[...])
    for copy in rim1:
        copy.wait_send()
    land_sent.wait_send()

    terms_sent.wait_recv()

    came = term_recv[...].reshape(rows, 128)
    came = jnp.concatenate([jnp.where(upper, came, 0.0), jnp.where(upper, 0.0, came)], axis=1)
    high, low = halves(came)
    came = jnp.concatenate([high, low], axis=1)

    moved = nn(oht_msg[...], came)
    grad2 = (hidden - moved[:, :hid] - moved[:, hid:]) * pre2[...]
    for first_, last, base in GROUPS:
        held = 32 * (last - first_)
        for parity in range(2):
            at = base + held * parity
            for h in range(hid // 128):
                g_ext[h, 2 + first_:2 + last, pl.ds(SIDE + parity, 32, stride=2), :] = (
                    grad2[at:at + held, 128 * h:128 * h + 128].reshape(last - first_, 32, 128))
    rim2 = packed_rim(sides, 0, g_send, g_recv)
    rim2 += packed_rim(corners, -1, g_send, g_recv) + packed_rim(corners, 1, g_send, g_recv)
    rim2 += rim(g_ext, g_send, g_recv, (edges,))
    terms_sent.wait_send()

    packed_arrived(sides, 0, g_send, g_recv)

    def backward(high_ref, low_ref, depth):
        def weights(m):
            at = (3, 1, 2, 0)[m]
            return tuple(jnp.concatenate([ref[at, i * depth:(i + 1) * depth] for i in range(3)], axis=1)
                         for ref in (high_ref, low_ref)) + (nt,)
        return weights

    def put2(chosen, groups, stacked=False):
        sums = pair_sums(taps(sg_hi, chosen), taps(sg_lo, chosen), backward(w2_hi, w2_lo, hid), stacked)
        for parity, grad1 in enumerate(sums):
            for source, target, length in groups:
                part = grad1[source * PAIRS:(source + length) * PAIRS].reshape(length, PAIRS, hid)
                p_ext[parity, target:target + length] = part * pre1[parity, target:target + length]

    def scaled_by(x, factor):
        return [y * factor for y in x]

    def plus(x, y, factor):
        return [u + v * factor for u, v in zip(x, y)]

    def near_pairs(first_, last):
        rows_ = slice(first_, last)
        return factors(p_ext[0, rows_, 0:32], p_ext[1, rows_, 0:32], p_ext[0, rows_, 1:33], p_ext[1, rows_, 1:33])

    def put_pairs(first_, last, at):
        for m, piece in enumerate(near_pairs(first_, last)):
            sp_hi[m, at:at + last - first_], sp_lo[m, at:at + last - first_] = halves(piece)

    def put3(chosen, rows_):
        products = []
        for m in range(4):
            wh, wl, dot = backward(w1_hi, w1_lo, k1)(m)
            lhs = taps(sp_hi, chosen)(m)
            count_ = lhs.shape[0]
            both_ = dot(jnp.concatenate([lhs, taps(sp_lo, chosen)(m)], axis=0), jnp.concatenate([wh, wl], axis=0))
            products.append(both_[:count_, :k1] + both_[:count_, k1:] + both_[count_:, :k1])
        m0, m1, m2, m3 = products
        for parity, part in enumerate((m0 + m1 + m2, m1 - m2 - m3)):
            part = part.reshape(part.shape[0] // 32, 32, k1)
            done = 0
            for first_, last in rows_:
                out[first_:last, pl.ds(parity, 32, stride=2), :] = part[done:done + last - first_]
                done += last - first_

    inner_rows(g_ext, sg_hi, sg_lo)
    put2((((1, 4),), ((4, 7),), ((0, 3),)), ((0, 2, 6),))
    put_pairs(2, 8, 2)
    put3((((4, 8),), ((3, 7),), ((2, 6),)), ((2, 6),))
    rim_arrived(g_ext, g_recv, g_send, (edges,))
    packed_arrived(corners, 1, g_send, g_recv)
    packed_arrived(corners, -1, g_send, g_recv)
    r0, r1 = pair_rows(g_ext, north), pair_rows(g_ext, 1 - north)
    r10, r11 = pair_rows(g_ext, 10 + south), pair_rows(g_ext, 11 - south)
    put_rows(sg_hi, sg_lo, 7, joined(r1, pair_rows(g_ext, 2)))
    put_rows(sg_hi, sg_lo, 8, joined(pair_rows(g_ext, 9), r10))
    put_rows(sg_hi, sg_lo, 9, joined(plus(pair_rows(g_ext, 2), r0, northf), plus(pair_rows(g_ext, 3), r1, northf)))
    put_rows(sg_hi, sg_lo, 10, joined(scaled_by(r10, 1.0 - southf), scaled_by(r11, 1.0 - southf)))
    put_rows(sg_hi, sg_lo, 11, joined(scaled_by(r0, 1.0 - northf), scaled_by(r1, 1.0 - northf)))
    put_rows(sg_hi, sg_lo, 12, joined(plus(pair_rows(g_ext, 8), r10, southf), plus(pair_rows(g_ext, 9), r11, southf)))
    put2((((9, 11),), ((7, 9),), ((11, 13),)), ((0, 0, 2), (2, 8, 2)), True)

    for m, (q0, q1, q2, q7, q8, q9) in enumerate(zip(*[near_pairs(at, at + 1) for at in (0, 1, 2, 7, 8, 9)])):
        for at, piece in ((1, q1), (8, q8), (10, q2 + northf * q0), (11, q9 * (1.0 - southf)),
                          (12, q0 * (1.0 - northf)), (13, q7 + southf * q9)):
            sp_hi[m, at:at + 1], sp_lo[m, at:at + 1] = halves(piece)
    put3((((10, 11), (3, 4), (8, 9), (11, 12)), ((1, 3), (7, 9)), ((12, 13), (1, 2), (6, 7), (13, 14))),
         ((0, 2), (6, 8)))
    for copy in rim2:
        copy.wait_send()


def shards(n_lon, n_lat, latent, conv1_weight, conv1_bias, conv2_weight, conv2_bias, head_weight, head_bias, land_sea,
           var_ok, obs_error, obs_band, obs_cell, obs_count, obs_value):
    lc, hid = conv1_weight.shape[2], conv1_weight.shape[3]
    slots, patch = obs_value.shape[1], obs_value.shape[2]
    variables = var_ok.shape[1]
    listed = n_lat * slots
    padded = -(-(listed + 128) // 128) * 128
    vmem = pltpu.VMEM
    rows = n_lat * MSG
    scratch = [
        vmem((lc // 128, 12, BUF, 128), F32),
        vmem((4, 13, 2 * PAIRS, lc), BF16), vmem((4, 13, 2 * PAIRS, lc), BF16),
        vmem((9 * lc, hid), F32), vmem((4, 3 * lc, hid), BF16), vmem((4, 3 * lc, hid), BF16),
        vmem((9 * hid, hid), F32), vmem((4, 3 * hid, hid), BF16), vmem((4, 3 * hid, hid), BF16),
        vmem((1, hid), F32), vmem((1, hid), F32),
        vmem((2, 10, PAIRS, hid), F32), vmem((2, 10, PAIRS, hid), F32),
        vmem((4, 10, 32, hid), BF16), vmem((4, 10, 32, hid), BF16),
        vmem((512, hid), F32),
        vmem((patch, hid), F32), vmem((patch, hid), BF16), vmem((patch, hid), BF16),
        vmem((patch,), F32), vmem(land_sea.shape, jnp.int32), vmem(var_ok.shape, jnp.int32),
        vmem((1, variables), F32),
        vmem((1, padded), jnp.int32), vmem((1, padded), jnp.int32), vmem((1, padded), jnp.int32),
        vmem((slots, patch), F32), vmem((slots, patch), BF16), vmem((slots, patch), BF16),
        vmem((2 * slots, patch), BF16),
        vmem((128, patch), BF16), vmem((1, patch), F32),
        vmem((512, 128), BF16), vmem((n_lat * CAP, 128), BF16),
        vmem((n_lat * CAP, 512), BF16), vmem((512, n_lat * CAP), BF16), vmem((512, rows), BF16),
        vmem((rows, 128), BF16),
        vmem((128, n_lat * LCAP), BF16), vmem((128, 128), F32),
        vmem((n_lat, LCAP, 128), F32), vmem((n_lat, LCAP, 128), F32),
        vmem((n_lat, MSG, 128), F32), vmem((n_lat, MSG, 128), F32),
        vmem((hid // 128, 12, BUF, 128), F32),
        vmem((2, hid // 128, 16, 128), F32), vmem((2, hid // 128, 16, 128), F32),
        vmem((4, hid // 128, 4, 128), F32), vmem((4, hid // 128, 4, 128), F32),
        vmem((4, 13, 2 * PAIRS, hid), BF16), vmem((4, 13, 2 * PAIRS, hid), BF16),
        vmem((2, 10, PAIRS, hid), F32),
        vmem((4, 14, 32, hid), BF16), vmem((4, 14, 32, hid), BF16),
        pltpu.SemaphoreType.DMA((14,)),
        pltpu.SemaphoreType.DMA((8,)), pltpu.SemaphoreType.DMA((9,)),
        pltpu.SemaphoreType.DMA((8,)), pltpu.SemaphoreType.DMA((9,)),
    ] + [pltpu.SemaphoreType.DMA((1,))] * 4
    return pl.pallas_call(
        functools.partial(kernel, n_lon, n_lat, slots, patch, variables),
        out_shape=jax.ShapeDtypeStruct(latent.shape, F32),
        in_specs=[pl.BlockSpec(memory_space=pl.ANY)] * 14,
        out_specs=pl.BlockSpec(memory_space=pltpu.VMEM),
        scratch_shapes=scratch,
        compiler_params=pltpu.CompilerParams(
            collective_id=0, has_side_effects=True, vmem_limit_bytes=48 * 1024 * 1024),
    )(*(pltpu.with_memory_space_constraint(x, pltpu.HBM) for x in (
        latent, conv1_weight.reshape(9 * lc, hid), conv1_bias.reshape(1, hid), conv2_weight.reshape(9 * hid, hid),
      conv2_bias.reshape(1, hid), head_weight.T, head_bias, land_sea, var_ok,
      obs_error.reshape(1, variables), obs_band.reshape(1, listed), obs_cell, obs_count, obs_value[0])))


def solution(mesh):
    in_specs = (
        P("lat", "lon", None),
        P(),
        P(),
        P(),
        P(),
        P(),
        P(),
        P("lat", "lon"),
        P(),
        P(),
        P("lon", None, None),
        P("lon", None),
        P("lon", None),
        P("lon", "lat", None),
    )
    out_specs = P("lat", "lon", None)
    body = functools.partial(shards, mesh.shape["lon"], mesh.shape["lat"])
    return jax.shard_map(body, mesh=mesh, in_specs=in_specs, out_specs=out_specs, check_vma=False)
```

```python
import functools

import jax
import jax.numpy as jnp
from jax import lax
from jax.experimental import pallas as pl
from jax.experimental.pallas import tpu as pltpu
from jax.sharding import PartitionSpec as P

F32 = jnp.float32
BF16 = jnp.bfloat16
CAP = 12
MSG = 2 * CAP
LCAP = 16
GROUPS = ((0, 2, 0), (6, 8, 128), (2, 6, 256))
SIDE = 8
PAIRS = 40
BUF = 88
CHUNK = 512
MESH = pl.DeviceIdType.MESH


def halves(x):
    high = x.astype(BF16)
    return high, (x - high.astype(F32)).astype(BF16)


def nn(a, b):
    return lax.dot_general(a, b, (((1,), (0,)), ((), ())), preferred_element_type=F32)


def nt(a, b):
    return lax.dot_general(a, b, (((1,), (1,)), ((), ())), preferred_element_type=F32)


def gelu_parts(x):
    c = 0.7978845608028654
    t = jnp.tanh(c * (x + 0.044715 * x * x * x))
    return 0.5 * x * (1.0 + t), t


def gelu_slope(x):
    c = 0.7978845608028654
    t = jnp.tanh(c * (x + 0.044715 * x * x * x))
    return 0.5 * (1.0 + t) + 0.5 * x * (1.0 - t * t) * (c * (1.0 + 3.0 * 0.044715 * x * x))


def kernel(
    n_lon, n_lat, slots, patch, variables,
    latent, w1, b1, w2, b2, head, hbias, land, ok, err, band, cell, count, value,
    out,
    lat_ext, sa_hi, sa_lo, w1_v, w1_hi, w1_lo, w2_v, w2_hi, w2_lo, b1_v, b2_v,
    pre1, act1, sb_hi, sb_lo, pre2, head_v, head_hi, head_lo, hb_v, land_v, ok_v, err_v,
    band_v, cell_v, count_v, value_v, val_hi, val_lo, masked, ok_rows, inv_row,
    tiles_v, flags_w, oh, oht, oht_msg, pmt, from_land, own_weight, land_send, land_recv, term_send, term_recv,
    g_ext, side_send, side_recv, corner_send, corner_recv, sg_hi, sg_lo, p_ext, sp_hi, sp_lo,
    load_sem, h_send, h_recv, g_send, g_recv, l_send, l_recv, t_send, t_recv,
):
    lon, lat = lax.axis_index("lon"), lax.axis_index("lat")
    north = 1 - lax.div(lat + n_lat - 1, n_lat)
    south = lax.div(lat + 1, n_lat)
    northf, southf = north.astype(F32), south.astype(F32)
    hid = w1_v.shape[1]
    k1 = latent.shape[2]

    loads = [
        (land, land_v),
        (band, band_v.at[:, 0:n_lat * slots]),
        (cell, cell_v.at[:, 0:n_lat * slots]),
        (count, count_v.at[:, 0:n_lat * slots]),
        (latent, lat_ext.at[0, 2:10, SIDE:SIDE + 64, :]),
        (w1, w1_v),
        (b1, b1_v),
        (ok, ok_v),
        (err, err_v),
        (hbias, hb_v),
        (w2, w2_v),
        (b2, b2_v),
        (value, value_v),
        (head, head_v),
    ]
    copies = [pltpu.make_async_copy(s, d, load_sem.at[i]) for i, (s, d) in enumerate(loads)]
    (ld_land, ld_band, ld_cell, ld_count, ld_lat, ld_w1, ld_b1, ld_ok, ld_err, ld_hb, ld_w2, ld_b2, ld_value,
     ld_head) = copies
    for copy in copies[:5]:
        copy.start()

    half = n_lon // 2
    up_lat, down_lat = lat - 1 + north, lat + 1 - south
    around = []
    for dr in (-1, 0, 1):
        for dc in (-1, 0, 1):
            if dr == 0 and dc == 0:
                continue
            turn = half * north if dr < 0 else half * south if dr > 0 else 0
            to_lon = lax.rem(lon + dc + turn + n_lon, n_lon)
            to_lat = up_lat if dr < 0 else down_lat if dr > 0 else lat
            around.append((dr, dc, (to_lon, to_lat)))

    deep = n_lat // 2
    steps = [(far, step) for far in range(2) for step in range(deep) if far or step]
    steps.sort(key=lambda s: -(2 * s[0] + min(s[1], deep - s[1])))
    peers = [lax.rem(lax.div(lat, deep) + far, 2) * deep + lax.rem(lax.rem(lat, deep) + step, deep)
             for far, step in steps]

    barrier = pltpu.get_barrier_semaphore()
    for peer in peers:
        pl.semaphore_signal(barrier, inc=1, device_id=(lon, peer), device_id_type=MESH)
    for _, _, device in around:
        pl.semaphore_signal(barrier, inc=1, device_id=device, device_id_type=MESH)
    for copy in copies[5:]:
        copy.start()

    edges, corners, sides = range(3)
    parts = []
    for dr, dc, device in around:
        parts.append((corners if dr and dc else edges if dr else sides, dr, dc, device))

    def rim(buf, send_sem, recv_sem, kinds, drs=(-1, 0, 1)):
        sent = []
        for kind in kinds:
            for number, (its, dr, dc, device) in enumerate(parts):
                if its != kind or dr not in drs:
                    continue
                src_c = (SIDE, SIDE) if dc < 0 else (SIDE + 56, SIDE) if dc > 0 else (SIDE, 64)
                dst_c = 72 if dc < 0 else 0 if dc > 0 else SIDE
                if dr < 0:
                    src_r, dst_r, side = 2, 10 - 10 * north, 2 * (1 - north)
                elif dr > 0:
                    src_r, dst_r, side = 8, 10 * south, 2 * south
                else:
                    src_r, dst_r, side = 2, 2, 1
                length = 8 if kind == sides else 2
                slot = side * 3 + (1 - dc)
                src = buf.at[:, pl.ds(src_r, length), pl.ds(src_c[0], src_c[1]), :]
                dst = buf.at[:, pl.ds(dst_r, length), pl.ds(dst_c, src_c[1]), :]
                copy = pltpu.make_async_remote_copy(
                    src_ref=src, dst_ref=dst, send_sem=send_sem.at[number], recv_sem=recv_sem.at[slot],
                    device_id=device, device_id_type=MESH)
                copy.start()
                sent.append(copy)
        return sent

    def rim_arrived(buf, recv_sem, send_sem, kinds, drs=(-1, 0, 1)):
        for number, (kind, dr, dc, device) in enumerate(parts):
            if kind not in kinds or dr not in drs:
                continue
            cols_ = (0, SIDE) if dc < 0 else (72, SIDE) if dc > 0 else (SIDE, 64)
            at, length = (2, 8) if kind == sides else (0 if dr < 0 else 10, 2)
            ref = buf.at[:, pl.ds(at, length), pl.ds(cols_[0], cols_[1]), :]
            slot = (dr + 1) * 3 + dc + 1
            pltpu.make_async_remote_copy(
                src_ref=ref, dst_ref=ref, send_sem=send_sem.at[number], recv_sem=recv_sem.at[slot],
                device_id=device, device_id_type=MESH).wait_recv()

    def last_columns(dc):
        return SIDE if dc < 0 else SIDE + 62

    def halo_columns(dc):
        return SIDE - 2 if dc < 0 else 72

    def packed_rim(kind, its_dr, send_sem, recv_sem):
        sent = []
        for number, (its, dr, dc, device) in enumerate(parts):
            if its != kind or dr != its_dr:
                continue
            at = last_columns(dc)
            if kind == sides:
                mine_, theirs_, ref, into_ref = (dc + 1) // 2, (1 - dc) // 2, side_send, side_recv
                for h in range(hid // 128):
                    for j in range(2):
                        ref[mine_, h, 8 * j:8 * j + 8, :] = g_ext[h, 2:10, at + j:at + j + 1, :].reshape(8, 128)
                slot = 3 + (1 - dc)
            else:
                side = 2 - 2 * north if dr < 0 else 2 * south
                mine_, theirs_, ref, into_ref = dr + 1 + (dc + 1) // 2, side + (1 - dc) // 2, corner_send, corner_recv
                for h in range(hid // 128):
                    for r in range(2):
                        row_ = (2 if dr < 0 else 8) + r
                        ref[mine_, h, 2 * r:2 * r + 2, :] = g_ext[h, row_, at:at + 2, :]
                slot = side * 3 + (1 - dc)
            copy = pltpu.make_async_remote_copy(
                src_ref=ref.at[mine_], dst_ref=into_ref.at[theirs_], send_sem=send_sem.at[number],
                recv_sem=recv_sem.at[slot], device_id=device, device_id_type=MESH)
            copy.start()
            sent.append(copy)
        return sent

    def packed_arrived(kind, its_dr, send_sem, recv_sem):
        for number, (its, dr, dc, device) in enumerate(parts):
            if its != kind or dr != its_dr:
                continue
            at, slot = halo_columns(dc), (dr + 1) * 3 + dc + 1
            mine_ = (dc + 1) // 2 if kind == sides else dr + 1 + (dc + 1) // 2
            ref = side_recv if kind == sides else corner_recv
            pltpu.make_async_remote_copy(
                src_ref=ref.at[mine_], dst_ref=ref.at[mine_], send_sem=send_sem.at[number],
                recv_sem=recv_sem.at[slot], device_id=device, device_id_type=MESH).wait_recv()
            for h in range(hid // 128):
                for j in range(2):
                    if kind == sides:
                        g_ext[h, 2:10, at + j:at + j + 1, :] = ref[mine_, h, 8 * j:8 * j + 8, :].reshape(8, 1, 128)
                    else:
                        g_ext[h, (0 if dr < 0 else 10) + j, at:at + 2, :] = ref[mine_, h, 2 * j:2 * j + 2, :]

    def exchange(src, dst, send_sem, recv_sem):
        for peer in peers:
            pltpu.make_async_remote_copy(
                src_ref=src.at[peer], dst_ref=dst.at[lat], send_sem=send_sem.at[0], recv_sem=recv_sem.at[0],
                device_id=(lon, peer), device_id_type=MESH).start()
        dst[pl.ds(lat, 1)] = src[pl.ds(lat, 1)]
        every = pl.ds(0, len(peers))
        return pltpu.make_async_remote_copy(
            src_ref=src.at[every], dst_ref=dst.at[every], send_sem=send_sem.at[0], recv_sem=recv_sem.at[0],
            device_id=(lon, peers[0]), device_id_type=MESH)

    def split(src, high_ref, low_ref, step):
        def body(i, carry):
            at = pl.ds(pl.multiple_of(i * step, step), step)
            high_ref[at, :], low_ref[at, :] = halves(src[at, :])
            return carry
        lax.fori_loop(0, src.shape[0] // step, body, 0)

    def split_taps(src, high_ref, low_ref, depth, step):
        for i in range(3):
            def body(n, carry):
                g0, g1, g2 = (src[pl.ds(pl.multiple_of((3 * i + j) * depth + n * step, step), step), :] for j in range(3))
                outer, inner = 0.5 * (g0 + g2), 0.5 * g1
                at = pl.ds(pl.multiple_of(i * depth + n * step, step), step)
                for m, factor in enumerate((g0, outer + inner, outer - inner, g2)):
                    high_ref[m, at, :], low_ref[m, at, :] = halves(factor)
                return carry
            lax.fori_loop(0, depth // step, body, 0)

    def factors(d0, d1, d2, d3):
        return d0 - d2, d1 + d2, d2 - d1, d1 - d3

    def pair_rows(buf, at, length=1):
        def column(d):
            lanes = [buf[h, pl.ds(at, length), pl.ds(SIDE - 2 + d, PAIRS, stride=2), :] for h in range(buf.shape[0])]
            return jnp.concatenate(lanes, axis=2)
        return factors(*[column(d) for d in range(4)])

    def put_rows(high_ref, low_ref, at, pieces):
        for m, piece in enumerate(pieces):
            count_ = piece.shape[0] // 2
            high_ref[m, at:at + count_], low_ref[m, at:at + count_] = halves(
                piece.reshape(count_, 2 * PAIRS, piece.shape[2]))

    def joined(*rows_):
        return [jnp.concatenate(list(x), axis=0) for x in zip(*rows_)]

    def inner_rows(buf, high_ref, low_ref):
        pieces = pair_rows(buf, 2, 8)
        put_rows(high_ref, low_ref, 0, pieces)
        put_rows(high_ref, low_ref, 4, [x[1:7] for x in pieces])

    def pair_sums(taken_hi, taken_lo, weights, stacked=False):
        products = []
        for m in range(4):
            lhs, (wh, wl, dot) = taken_hi(m), weights(m)
            if stacked:
                both_ = dot(jnp.concatenate([lhs, taken_lo(m)], axis=0), wh)
                products.append(both_[:lhs.shape[0]] + both_[lhs.shape[0]:] + dot(lhs, wl))
            else:
                products.append(dot(lhs, wh) + dot(lhs, wl) + dot(taken_lo(m), wh))
        m0, m1, m2, m3 = products
        return m0 + m1 + m2, m1 - m2 - m3

    def taps(ref, chosen):
        def lhs(m):
            rows_ = [jnp.concatenate([ref[m, a:b] for a, b in part], axis=0) for part in chosen]
            return jnp.concatenate([x.reshape(x.shape[0] * x.shape[1], x.shape[2]) for x in rows_], axis=1)
        return lhs

    lat_ext[:, :, 80:88, :] = jnp.zeros((k1 // 128, 12, 8, 128), F32)
    g_ext[:, :, 72:88, :] = jnp.zeros((hid // 128, 12, 16, 128), F32)

    ld_band.wait()
    ld_cell.wait()
    ld_land.wait()
    lane = lax.broadcasted_iota(jnp.int32, (n_lat, 128), 1)
    live = lane < slots

    def blocks(ref):
        row = ref[...]
        return jnp.concatenate([row[:, slots * a:slots * a + 128] for a in range(n_lat)], axis=0)

    bands, cells = blocks(band_v), blocks(cell_v)
    below = (lax.broadcasted_iota(jnp.int32, (128, 128), 0) < lax.broadcasted_iota(jnp.int32, (128, 128), 1))
    below = below.astype(F32).astype(BF16)
    mine = jnp.where(live & (bands == lat), 1.0, 0.0)
    pick = jnp.where(mine > 0.0, nn(mine.astype(BF16), below), -1.0)
    cell_row, odd, pair = cells >> 6, cells & 1, (cells & 63) >> 1
    edge = (cell_row << 5) + (odd << 6) + jnp.where(cell_row > 5, 128 - 6 * 32, 0)
    inner = (cell_row << 5) + (odd << 7) + (256 - 2 * 32)
    cells = pair + jnp.where((cell_row < 2) | (cell_row > 5), edge, inner)
    cellsf = cells.astype(F32) + 1.0
    msg_k = lax.rem(lax.broadcasted_iota(jnp.int32, (MSG, 128), 0), CAP).astype(F32)
    land_k = lax.broadcasted_iota(jnp.int32, (LCAP, 128), 0).astype(F32)
    named = [jnp.sum(jnp.where(pick[a:a + 1] == land_k, cellsf[a:a + 1], 0.0), axis=1, keepdims=True)
             for a in range(n_lat)]
    wanted = jnp.concatenate(named, axis=0).astype(jnp.int32) - 1
    lrows = n_lat * LCAP
    messages = jnp.where(wanted == lax.broadcasted_iota(jnp.int32, (lrows, 512), 1), 1.0, 0.0).astype(BF16)

    column = lax.broadcasted_iota(jnp.int32, (64, 512), 0)
    column = ((column & 31) << 1) + (column >> 5)
    fold = (lax.broadcasted_iota(jnp.int32, (64, 512), 1) >> 3) == column
    fold = jnp.where(fold, 1.0, 0.0).astype(BF16)
    kept = (lax.broadcasted_iota(jnp.int32, (8, 512), 1) & 7) == lax.broadcasted_iota(jnp.int32, (8, 512), 0)
    tiles = []
    for r in range(8):
        strip = land_v[8 * r:8 * r + 8, :].astype(F32)
        spread = jnp.concatenate([jnp.where(kept, strip[p:p + 1], 0.0) for p in range(8)], axis=0)
        tiles.append(nt(fold, spread.astype(BF16)))
    tiles = [tiles[r][32 * parity:32 * parity + 32] for first_, last, _ in GROUPS for parity in range(2) for r in range(first_, last)]
    tiles = jnp.concatenate(tiles, axis=0)
    tiles = jnp.concatenate([tiles, 1.0 - tiles], axis=1).astype(BF16)
    tiles_v[...] = tiles
    land_send[...] = nn(messages, tiles).reshape(n_lat, LCAP, 128)

    pl.semaphore_wait(barrier, len(around) + len(peers))
    land_sent = exchange(land_send, land_recv, l_send, l_recv)
    ld_lat.wait()
    rim1 = rim(lat_ext, h_send, h_recv, (sides, corners, edges))

    ld_w1.wait()
    split_taps(w1_v, w1_hi, w1_lo, k1, 64)

    ld_count.wait()
    countsf = blocks(count_v).astype(F32) * 0.125
    first = lax.broadcasted_iota(jnp.int32, (MSG, 128), 0) < CAP
    taken = n_lat * CAP
    named, merged = [], []
    for q in range(n_lat // 2):
        def two(x):
            return jnp.where(first, x[2 * q:2 * q + 1], x[2 * q + 1:2 * q + 2])
        hit = two(pick) == msg_k
        named.append(jnp.sum(jnp.where(hit, two(cellsf), 0.0), axis=1, keepdims=True))
        merged.append(jnp.sum(jnp.where(hit, two(countsf), 0.0), axis=1, keepdims=True))
    wanted = jnp.concatenate(named, axis=0).astype(jnp.int32) - 1
    weight = jnp.concatenate(merged, axis=0)
    oh[...] = jnp.where(wanted == lax.broadcasted_iota(jnp.int32, (taken, 512), 1), 1.0, 0.0).astype(BF16)
    flags_w[...] = (nn(oh[...], tiles_v[...]) * weight).astype(BF16)

    own = lax.broadcasted_iota(jnp.int32, (n_lat, 128), 0) == lat
    own_band = jnp.sum(jnp.where(own, bands, 0), axis=0, keepdims=True)
    own_count = jnp.sum(jnp.where(own, countsf, 0.0), axis=0, keepdims=True)
    theirs = jnp.where(live & (own_band == lax.broadcasted_iota(jnp.int32, (n_lat, 128), 0)), 1.0, 0.0)
    place = jnp.where(theirs > 0.0, nn(theirs.astype(BF16), below), -1.0)
    pmt[...] = jnp.concatenate(
        [jnp.where(place[b:b + 1] == msg_k, 1.0, 0.0) for b in range(n_lat)], axis=0).astype(BF16)
    pml = jnp.concatenate([jnp.where(place[b:b + 1] == land_k, 1.0, 0.0) for b in range(n_lat)], axis=0)
    from_land[...] = jnp.transpose(pml).astype(BF16)
    own_weight[...] = jnp.transpose(jnp.broadcast_to(own_count, (128, 128)))

    ld_ok.wait()
    ld_err.wait()
    ld_hb.wait()
    ld_w2.wait()
    split_taps(w2_v, w2_hi, w2_lo, hid, 64)
    inv = 1.0 / (err_v[...] * err_v[...])
    inv_hi = inv.astype(BF16).astype(F32)
    inv_mid = (inv - inv_hi).astype(BF16).astype(F32)
    inv_lo = inv - inv_hi - inv_mid
    okf = ok_v[...].astype(F32)
    kind = lax.broadcasted_iota(jnp.int32, (16, variables), 0)
    table = jnp.where(kind == 0, inv_hi, jnp.where(kind == 1, inv_mid, jnp.where(kind == 2, inv_lo, 0.0)))
    table = table + jnp.where(kind == 3, okf[1:2], 0.0) + jnp.where(kind == 4, okf[0:1], 0.0)
    table = table.astype(BF16)
    spans = [(at, min(CHUNK, patch - at)) for at in range(0, patch, CHUNK)]
    for at, size in spans:
        place_ = lax.broadcasted_iota(jnp.int32, (1, size), 1) + at
        pixel = ((place_.astype(F32) + 0.5) * (1.0 / variables)).astype(jnp.int32)
        variable = place_ - pixel * variables
        chosen = lax.broadcasted_iota(jnp.int32, (variables, size), 0) == variable
        spread = nn(table, jnp.where(chosen, 1.0, 0.0).astype(BF16))
        inv_row[:, at:at + size] = jnp.broadcast_to(spread[0:1] + spread[1:2] + spread[2:3], (8, size))
        which = lax.broadcasted_iota(jnp.int32, (128, size), 0)
        seen = jnp.where(which == pixel, spread[3:4], jnp.where(which == pixel + 64, spread[4:5], 0.0))
        ok_rows[:, at:at + size] = seen.astype(BF16)
    ld_b1.wait()
    ld_b2.wait()
    ld_value.wait()
    for at, size in spans:
        span = slice(at, at + size)
        shifted = (value_v[:, span] - hb_v[span].reshape(1, size)) * inv_row[0:1, span]
        val_hi[:, span], val_lo[:, span] = halves(shifted)
    ld_head.wait()
    split(head_v, head_hi, head_lo, 96)

    rim_arrived(lat_ext, h_recv, h_send, (sides,))

    def forward1(m):
        return w1_hi[m], w1_lo[m], nn

    def put1(chosen, groups):
        for parity, summed in enumerate(pair_sums(taps(sa_hi, chosen), taps(sa_lo, chosen), forward1)):
            summed = summed + b1_v[...]
            act = gelu_parts(summed)[0]
            for source, target, length in groups:
                part = slice(source * PAIRS, (source + length) * PAIRS)
                pre1[parity, target:target + length] = summed[part].reshape(length, PAIRS, hid)
                act1[parity, target:target + length] = act[part].reshape(length, PAIRS, hid)

    inner_rows(lat_ext, sa_hi, sa_lo)
    put1((((0, 3),), ((4, 7),), ((1, 4),)), ((0, 2, 6),))

    land_sent.wait_recv()
    flags_own = nn(from_land[...], land_recv[...].reshape(lrows, 128).astype(BF16))
    flags_own = flags_own[:slots].astype(BF16)

    def back(high, low, at, size, total):
        count_ = high.shape[0]
        hh, hl = head_hi[at:at + size, :], head_lo[at:at + size, :]
        both = nn(jnp.concatenate([high, low], axis=0), hh)
        return total + both[:count_] + both[count_:] + nn(high, hl)

    for at, size in spans:
        span = slice(at, at + size)
        seen = nn(flags_own, ok_rows[:, span]).astype(BF16)
        masked[0:slots, span] = val_hi[:, span] * seen
        masked[slots:2 * slots, span] = val_lo[:, span] * seen
    cut = patch // 256 * 128
    shares = jnp.concatenate([own_weight[0:slots, :]] * (hid // 128), axis=1)
    terms = jnp.zeros((slots, hid), F32)
    for a, b in ((0, cut), (cut, patch)):
        both = nn(masked[:, a:b], head_hi[a:b, :])
        terms = terms + (both[:slots] + both[slots:] + nn(masked[0:slots, a:b], head_lo[a:b, :])) * shares
    high, low = halves(terms)
    both = jnp.concatenate([high, low], axis=1)
    if slots < 128:
        both = jnp.concatenate([both, jnp.zeros((128 - slots, 2 * hid), BF16)], axis=0)
    rows = n_lat * MSG
    upper = lax.rem(lax.broadcasted_iota(jnp.int32, (rows, 128), 0), MSG) < CAP
    sent_terms = nn(pmt[...], both)
    sent_terms = sent_terms[:, :hid] + sent_terms[:, hid:]
    term_send[...] = jnp.where(upper, sent_terms[:, :128], sent_terms[:, 128:]).reshape(n_lat, MSG, 128)
    terms_sent = exchange(term_send, term_recv, t_send, t_recv)

    rim_arrived(lat_ext, h_recv, h_send, (edges, corners))
    for at, one, other in (
        (7, 1 - north, 2), (8, 9, 10 + south),
        (9, 2 * north, 1 - north), (10, 8, 9 + south),
        (11, 2 - north, 3), (12, 10 + south, 11 - 2 * south),
    ):
        put_rows(sa_hi, sa_lo, at, joined(pair_rows(lat_ext, one), pair_rows(lat_ext, other)))
    put1((((9, 11),), ((7, 9),), ((11, 13),)), ((0, 0, 2), (2, 8, 2)))

    def near(ref, rows_=slice(0, 10)):
        return factors(ref[0, rows_, 0:32], ref[1, rows_, 0:32], ref[0, rows_, 1:33], ref[1, rows_, 1:33])

    for m, piece in enumerate(near(act1)):
        sb_hi[m], sb_lo[m] = halves(piece)

    def forward2(m):
        return w2_hi[m], w2_lo[m], nn

    chosen = tuple(((i, i + 8),) for i in range(3))
    summed = pair_sums(taps(sb_hi, chosen), taps(sb_lo, chosen), forward2)
    summed = [x[32 * first_:32 * last] for first_, last, _ in GROUPS for x in summed]
    summed = jnp.concatenate(summed, axis=0) + b2_v[...]
    pre2[...] = summed
    act2, _ = gelu_parts(summed)

    high, low = halves(act2)
    cols = nn(oh[...], jnp.concatenate([high, low], axis=1)).astype(BF16)
    cols_hi, cols_lo = cols[:, :hid], cols[:, hid:]
    cols_both = jnp.concatenate([cols_hi, cols_lo], axis=0)
    terms = jnp.zeros((taken, hid), F32)
    for at, size in spans:
        span = slice(at, at + size)
        both = nt(cols_both, head_hi[span, :])
        decoded = both[:taken] + both[taken:] + nt(cols_hi, head_lo[span, :])
        high, low = halves(nn(flags_w[...], ok_rows[:, span]) * inv_row[0:1, span] * decoded)
        terms = back(high, low, at, size, terms)

    wanted_row = jnp.transpose(jnp.broadcast_to(wanted.astype(F32), (taken, 128)))[0:1, :].astype(jnp.int32)
    oht[...] = jnp.where(wanted_row == lax.broadcasted_iota(jnp.int32, (512, taken), 0), 1.0, 0.0).astype(BF16)
    named = [jnp.sum(jnp.where(pick[a:a + 1] == msg_k, cellsf[a:a + 1], 0.0), axis=1, keepdims=True)
             for a in range(n_lat)]
    named = jnp.broadcast_to(jnp.concatenate(named, axis=0), (rows, 128))
    wanted_row = jnp.transpose(named)[0:1, :].astype(jnp.int32) - 1
    oht_msg[...] = jnp.where(wanted_row == lax.broadcasted_iota(jnp.int32, (512, rows), 0), 1.0, 0.0).astype(BF16)
    high, low = halves(terms)
    hidden = nn(oht[...], jnp.concatenate([high, low], axis=1))
    hidden = hidden[:, :hid] + hidden[:, hid:]
    pre2[...] = gelu_slope(pre2[...])
    pre1[...] = gelu_slope(pre1[...])
    for copy in rim1:
        copy.wait_send()
    land_sent.wait_send()

    terms_sent.wait_recv()

    came = term_recv[...].reshape(rows, 128)
    came = jnp.concatenate([jnp.where(upper, came, 0.0), jnp.where(upper, 0.0, came)], axis=1)
    high, low = halves(came)
    came = jnp.concatenate([high, low], axis=1)

    moved = nn(oht_msg[...], came)
    grad2 = (hidden - moved[:, :hid] - moved[:, hid:]) * pre2[...]
    for first_, last, base in GROUPS:
        held = 32 * (last - first_)
        for parity in range(2):
            at = base + held * parity
            for h in range(hid // 128):
                g_ext[h, 2 + first_:2 + last, pl.ds(SIDE + parity, 32, stride=2), :] = (
                    grad2[at:at + held, 128 * h:128 * h + 128].reshape(last - first_, 32, 128))
    rim2 = packed_rim(sides, 0, g_send, g_recv)
    rim2 += packed_rim(corners, -1, g_send, g_recv) + packed_rim(corners, 1, g_send, g_recv)
    rim2 += rim(g_ext, g_send, g_recv, (edges,))
    terms_sent.wait_send()

    packed_arrived(sides, 0, g_send, g_recv)

    def backward(high_ref, low_ref, depth):
        def weights(m):
            at = (3, 1, 2, 0)[m]
            return tuple(jnp.concatenate([ref[at, i * depth:(i + 1) * depth] for i in range(3)], axis=1)
                         for ref in (high_ref, low_ref)) + (nt,)
        return weights

    def put2(chosen, groups, stacked=False):
        sums = pair_sums(taps(sg_hi, chosen), taps(sg_lo, chosen), backward(w2_hi, w2_lo, hid), stacked)
        for parity, grad1 in enumerate(sums):
            for source, target, length in groups:
                part = grad1[source * PAIRS:(source + length) * PAIRS].reshape(length, PAIRS, hid)
                p_ext[parity, target:target + length] = part * pre1[parity, target:target + length]

    def scaled_by(x, factor):
        return [y * factor for y in x]

    def plus(x, y, factor):
        return [u + v * factor for u, v in zip(x, y)]

    def near_pairs(first_, last):
        rows_ = slice(first_, last)
        return factors(p_ext[0, rows_, 0:32], p_ext[1, rows_, 0:32], p_ext[0, rows_, 1:33], p_ext[1, rows_, 1:33])

    def put_pairs(first_, last, at):
        for m, piece in enumerate(near_pairs(first_, last)):
            sp_hi[m, at:at + last - first_], sp_lo[m, at:at + last - first_] = halves(piece)

    def put3(chosen, rows_):
        products = []
        for m in range(4):
            wh, wl, dot = backward(w1_hi, w1_lo, k1)(m)
            lhs = taps(sp_hi, chosen)(m)
            count_ = lhs.shape[0]
            both_ = dot(jnp.concatenate([lhs, taps(sp_lo, chosen)(m)], axis=0), jnp.concatenate([wh, wl], axis=0))
            products.append(both_[:count_, :k1] + both_[:count_, k1:] + both_[count_:, :k1])
        m0, m1, m2, m3 = products
        for parity, part in enumerate((m0 + m1 + m2, m1 - m2 - m3)):
            part = part.reshape(part.shape[0] // 32, 32, k1)
            done = 0
            for first_, last in rows_:
                out[first_:last, pl.ds(parity, 32, stride=2), :] = part[done:done + last - first_]
                done += last - first_

    inner_rows(g_ext, sg_hi, sg_lo)
    put2((((1, 4),), ((4, 7),), ((0, 3),)), ((0, 2, 6),), True)
    put_pairs(2, 8, 2)
    put3((((4, 8),), ((3, 7),), ((2, 6),)), ((2, 6),))
    rim_arrived(g_ext, g_recv, g_send, (edges,))
    packed_arrived(corners, 1, g_send, g_recv)
    packed_arrived(corners, -1, g_send, g_recv)
    r0, r1 = pair_rows(g_ext, north), pair_rows(g_ext, 1 - north)
    r10, r11 = pair_rows(g_ext, 10 + south), pair_rows(g_ext, 11 - south)
    put_rows(sg_hi, sg_lo, 7, joined(r1, pair_rows(g_ext, 2)))
    put_rows(sg_hi, sg_lo, 8, joined(pair_rows(g_ext, 9), r10))
    put_rows(sg_hi, sg_lo, 9, joined(plus(pair_rows(g_ext, 2), r0, northf), plus(pair_rows(g_ext, 3), r1, northf)))
    put_rows(sg_hi, sg_lo, 10, joined(scaled_by(r10, 1.0 - southf), scaled_by(r11, 1.0 - southf)))
    put_rows(sg_hi, sg_lo, 11, joined(scaled_by(r0, 1.0 - northf), scaled_by(r1, 1.0 - northf)))
    put_rows(sg_hi, sg_lo, 12, joined(plus(pair_rows(g_ext, 8), r10, southf), plus(pair_rows(g_ext, 9), r11, southf)))
    put2((((9, 11),), ((7, 9),), ((11, 13),)), ((0, 0, 2), (2, 8, 2)), True)

    for m, (q0, q1, q2, q7, q8, q9) in enumerate(zip(*[near_pairs(at, at + 1) for at in (0, 1, 2, 7, 8, 9)])):
        for at, piece in ((1, q1), (8, q8), (10, q2 + northf * q0), (11, q9 * (1.0 - southf)),
                          (12, q0 * (1.0 - northf)), (13, q7 + southf * q9)):
            sp_hi[m, at:at + 1], sp_lo[m, at:at + 1] = halves(piece)
    put3((((10, 11), (3, 4), (8, 9), (11, 12)), ((1, 3), (7, 9)), ((12, 13), (1, 2), (6, 7), (13, 14))),
         ((0, 2), (6, 8)))
    for copy in rim2:
        copy.wait_send()


def shards(n_lon, n_lat, latent, conv1_weight, conv1_bias, conv2_weight, conv2_bias, head_weight, head_bias, land_sea,
           var_ok, obs_error, obs_band, obs_cell, obs_count, obs_value):
    lc, hid = conv1_weight.shape[2], conv1_weight.shape[3]
    slots, patch = obs_value.shape[1], obs_value.shape[2]
    variables = var_ok.shape[1]
    listed = n_lat * slots
    padded = -(-(listed + 128) // 128) * 128
    vmem = pltpu.VMEM
    rows = n_lat * MSG
    scratch = [
        vmem((lc // 128, 12, BUF, 128), F32),
        vmem((4, 13, 2 * PAIRS, lc), BF16), vmem((4, 13, 2 * PAIRS, lc), BF16),
        vmem((9 * lc, hid), F32), vmem((4, 3 * lc, hid), BF16), vmem((4, 3 * lc, hid), BF16),
        vmem((9 * hid, hid), F32), vmem((4, 3 * hid, hid), BF16), vmem((4, 3 * hid, hid), BF16),
        vmem((1, hid), F32), vmem((1, hid), F32),
        vmem((2, 10, PAIRS, hid), F32), vmem((2, 10, PAIRS, hid), F32),
        vmem((4, 10, 32, hid), BF16), vmem((4, 10, 32, hid), BF16),
        vmem((512, hid), F32),
        vmem((patch, hid), F32), vmem((patch, hid), BF16), vmem((patch, hid), BF16),
        vmem((patch,), F32), vmem(land_sea.shape, jnp.int32), vmem(var_ok.shape, jnp.int32),
        vmem((1, variables), F32),
        vmem((1, padded), jnp.int32), vmem((1, padded), jnp.int32), vmem((1, padded), jnp.int32),
        vmem((slots, patch), F32), vmem((slots, patch), BF16), vmem((slots, patch), BF16),
        vmem((2 * slots, patch), BF16),
        vmem((128, patch), BF16), vmem((8, patch), F32),
        vmem((512, 128), BF16), vmem((n_lat * CAP, 128), BF16),
        vmem((n_lat * CAP, 512), BF16), vmem((512, n_lat * CAP), BF16), vmem((512, rows), BF16),
        vmem((rows, 128), BF16),
        vmem((128, n_lat * LCAP), BF16), vmem((128, 128), F32),
        vmem((n_lat, LCAP, 128), F32), vmem((n_lat, LCAP, 128), F32),
        vmem((n_lat, MSG, 128), F32), vmem((n_lat, MSG, 128), F32),
        vmem((hid // 128, 12, BUF, 128), F32),
        vmem((2, hid // 128, 16, 128), F32), vmem((2, hid // 128, 16, 128), F32),
        vmem((4, hid // 128, 4, 128), F32), vmem((4, hid // 128, 4, 128), F32),
        vmem((4, 13, 2 * PAIRS, hid), BF16), vmem((4, 13, 2 * PAIRS, hid), BF16),
        vmem((2, 10, PAIRS, hid), F32),
        vmem((4, 14, 32, hid), BF16), vmem((4, 14, 32, hid), BF16),
        pltpu.SemaphoreType.DMA((14,)),
        pltpu.SemaphoreType.DMA((8,)), pltpu.SemaphoreType.DMA((9,)),
        pltpu.SemaphoreType.DMA((8,)), pltpu.SemaphoreType.DMA((9,)),
    ] + [pltpu.SemaphoreType.DMA((1,))] * 4
    return pl.pallas_call(
        functools.partial(kernel, n_lon, n_lat, slots, patch, variables),
        out_shape=jax.ShapeDtypeStruct(latent.shape, F32),
        in_specs=[pl.BlockSpec(memory_space=pl.ANY)] * 14,
        out_specs=pl.BlockSpec(memory_space=pltpu.VMEM),
        scratch_shapes=scratch,
        compiler_params=pltpu.CompilerParams(
            collective_id=0, has_side_effects=True, vmem_limit_bytes=48 * 1024 * 1024),
    )(*(pltpu.with_memory_space_constraint(x, pltpu.HBM) for x in (
        latent, conv1_weight.reshape(9 * lc, hid), conv1_bias.reshape(1, hid), conv2_weight.reshape(9 * hid, hid),
      conv2_bias.reshape(1, hid), head_weight.T, head_bias, land_sea, var_ok,
      obs_error.reshape(1, variables), obs_band.reshape(1, listed), obs_cell, obs_count, obs_value[0])))


def solution(mesh):
    in_specs = (
        P("lat", "lon", None),
        P(),
        P(),
        P(),
        P(),
        P(),
        P(),
        P("lat", "lon"),
        P(),
        P(),
        P("lon", None, None),
        P("lon", None),
        P("lon", None),
        P("lon", "lat", None),
    )
    out_specs = P("lat", "lon", None)
    body = functools.partial(shards, mesh.shape["lon"], mesh.shape["lat"])
    return jax.shard_map(body, mesh=mesh, in_specs=in_specs, out_specs=out_specs, check_vma=False)
```
